32 devices in a mesh: doc: 4 (over z), seq: 8 (over y, x, core).
Axes of the slice: x: 2, y: 2, z: 4, core: 2. Of those that a mesh axis runs over, the one named last changes fastest.
Arguments:
- dec_input: bfloat16 [4, 4, 1024, 768], P('doc', None, 'seq'), may hold values from -6 to 6
- memory: bfloat16 [4, 8192, 768], P('doc', 'seq'), may hold values from -6 to 6
- doc_lengths: int32 [4, 4], P('doc'), may hold values from 1 to 8192, as said below
- doc_count: int32 [4], P('doc'), may hold values from 1 to 4
- self_qkv: float32 [768, 2304], P('doc'), may hold values from -0.3125 to 0.3125
- self_out: float32 [768, 768], P('doc'), may hold values from -0.625 to 0.625
- cross_q: float32 [768, 768], P('doc'), may hold values from -0.4375 to 0.4375
- cross_kv: float32 [768, 1536], P('doc'), may hold values from -0.21875 to 0.21875
- cross_out: float32 [768, 768], P('doc'), may hold values from -2 to 2
- ffn_in: float32 [768, 3072], P('doc'), may hold values from -0.21875 to 0.21875
- ffn_in_bias: float32 [3072], P('doc'), may hold values from -3 to 3
- ffn_out: float32 [3072, 768], P('doc'), may hold values from -0.109375 to 0.109375
- norm_gains: float32 [3, 768], P(None, 'doc'), may hold values from 0.25 to 1.75
- biases: float32 [10, 768], P(None, 'doc'), may hold values from -1.75 to 1.75
- out_grad: bfloat16 [4, 4, 1024, 768], P('doc', None, 'seq'), may hold values from -6 to 6
Outputs:
- layer_out: bfloat16 [4, 4, 1024, 768], P('doc', None, 'seq')
- input_grad: float32 [4, 4, 1024, 768], P('doc', None, 'seq')
- memory_grad: float32 [4, 8192, 768], P('doc', 'seq')
- grad_self_qkv: float32 [768, 2304], P('doc')
- grad_self_out: float32 [768, 768], P('doc')
- grad_cross_q: float32 [768, 768], P('doc')
- grad_cross_kv: float32 [768, 1536], P('doc')
- grad_cross_out: float32 [768, 768], P('doc')
- grad_ffn_in: float32 [768, 3072], P('doc')
- grad_ffn_in_bias: float32 [3072], P('doc')
- grad_ffn_out: float32 [3072, 768], P('doc')
- grad_norm_gains: float32 [3, 768], P(None, 'doc')
- grad_biases: float32 [10, 768], P(None, 'doc')
The draws below stay inside these ranges and needn't reach their ends.
Inputs may be any that keep to these rules, and one draw needn't show every extreme that they name: `doc_lengths`: slots below doc_count hold the lengths of a group's documents, laid end to end from the start of its memory, together at most 8192 and more than 7680; memory after them is padding. Entries of later slots are no document's length. One group holds a single document of 8192 tokens; the others hold 4 documents of about 8192 // 4 tokens each.
All inputs are finite; a program needn't handle non-finite values.
Results may differ from the reference program's by a relative error of at most 0.03.
The reference program's roundings to bfloat16 on the way count: a program that leaves them out, or rounds other values in their place, can miss the bound.
Values may be sent and summed in bfloat16 or wider, within the bound.
No kernel may reach another device: no remote copies, remote signals or barrier semaphores. Data moves between devices by JAX's collectives and lax.ppermute only.
A program may use at most 512 MiB of HBM per device.

```python
import jax
import jax.numpy as jnp
from jax import lax

D = 768
HEADS = 12
HEAD_DIM = 64
FF = 3072
DEC = 1024
DOC_SLOTS = 4
MEM_DEV = 1024
GROUPS = 4
MEM_GROUP = 8192
N_SEQ = 8


def document_layout(key):
    keys = jax.random.split(key, 4)
    single_group = jax.random.randint(keys[0], (), 0, GROUPS)
    base_len = MEM_GROUP // DOC_SLOTS
    pads = jax.random.randint(keys[1], (GROUPS, DOC_SLOTS), 0, MEM_GROUP // (8 * DOC_SLOTS) + 1)
    tails = jax.random.randint(keys[2], (GROUPS,), 0, MEM_DEV // 2)
    spare = jax.random.randint(keys[3], (GROUPS, DOC_SLOTS), 1, base_len + 1)
    slot_ids = jnp.arange(DOC_SLOTS)[None, :]
    is_last = slot_ids == DOC_SLOTS - 1
    leading = base_len - pads
    lead_sum = jnp.sum(jnp.where(is_last, 0, leading), axis=1)
    regular = jnp.where(is_last, (MEM_GROUP - tails - lead_sum)[:, None], leading)
    single_row = jnp.where(slot_ids == 0, MEM_GROUP, spare)
    is_single = (jnp.arange(GROUPS) == single_group)[:, None]
    lengths = jnp.where(is_single, single_row, regular)
    counts = jnp.where(jnp.arange(GROUPS) == single_group, 1, DOC_SLOTS)
    return (lengths.astype(jnp.int32), counts.astype(jnp.int32))


def draw_doc_lengths(key, part):
    layout = document_layout(key)
    return layout[0]


def draw_doc_count(key, part):
    layout = document_layout(key)
    return layout[1]


def steps_of(own_key, extent, cuts, least, top_value):
    loudness, own = 1.0, jax.random.fold_in(own_key, 6)
    for position, parts in cuts:
        heights = jnp.exp(jax.random.uniform(jax.random.fold_in(own, position), (parts,), jnp.float32, least / len(cuts), top_value / len(cuts)))
        loudness = loudness * jnp.repeat(heights, extent[position] // parts).reshape([-1 if axis == position else 1 for axis in range(len(extent))])
    return loudness


def noise(key, dims, width, limit, cuts=(), held_as=jnp.bfloat16):
    values = width * jax.random.normal(key, dims, jnp.float32)
    if cuts:
        values = values * steps_of(key, dims, cuts, -0.22, 0.18)
    return jnp.clip(values, -limit, limit).astype(held_as)


def setup_inputs(seed: int = 0) -> dict:
    key_list = jax.random.split(jax.random.key(seed), 16)
    dec_input = noise(key_list[0], (GROUPS, DOC_SLOTS, DEC, D), 1.0, 6.0, ((0, 4), (2, 8)))
    memory = noise(key_list[1], (GROUPS, MEM_GROUP, D), 1.0, 6.0, ((0, 4), (1, 8)))
    doc_lengths = draw_doc_lengths(jax.random.fold_in(key_list[15], 71), 0)
    doc_count = draw_doc_count(jax.random.fold_in(key_list[15], 71), 0)
    self_qkv = noise(key_list[4], (D, 3 * D), (D // 2) ** -0.5, 0.3125, ((0, 4),), jnp.float32)
    self_out = noise(key_list[5], (D, D), (D // 8) ** -0.5, 0.625, ((0, 4),), jnp.float32)
    cross_q = noise(key_list[6], (D, D), (D // 4) ** -0.5, 0.4375, ((0, 4),), jnp.float32)
    cross_kv = noise(key_list[7], (D, 2 * D), D ** -0.5, 0.21875, ((0, 4),), jnp.float32)
    cross_out = noise(key_list[8], (D, D), 8 ** -0.5, 2.0, ((0, 4),), jnp.float32)
    ffn_in = noise(key_list[9], (D, FF), D ** -0.5, 0.21875, ((0, 4),), jnp.float32)
    ffn_in_bias = noise(key_list[10], (FF,), 0.5, 3.0, ((0, 4),), jnp.float32)
    ffn_out = noise(key_list[11], (FF, D), FF ** -0.5, 0.109375, ((0, 4),), jnp.float32)
    norm_gains = jnp.clip(1.0 + 0.15 * jax.random.normal(key_list[12], (3, D), jnp.float32), 0.25, 1.75)
    biases = noise(key_list[13], (10, D), 0.3, 1.75, ((1, 4),), jnp.float32)
    out_grad = noise(key_list[14], (GROUPS, DOC_SLOTS, DEC, D), 1.0, 6.0, ((0, 4), (2, 8)))
    return dict(dec_input=dec_input, memory=memory, doc_lengths=doc_lengths, doc_count=doc_count, self_qkv=self_qkv, self_out=self_out, cross_q=cross_q, cross_kv=cross_kv, cross_out=cross_out, ffn_in=ffn_in, ffn_in_bias=ffn_in_bias, ffn_out=ffn_out, norm_gains=norm_gains, biases=biases, out_grad=out_grad)


norm_eps = 1e-05
neg_fill = -1e+30

@jax.custom_vjp
def low(v):
    return lax.optimization_barrier(v.astype(jnp.bfloat16)).astype(jnp.float32)

@jax.custom_vjp
def low_back(v):
    return v

def low_keep(v):
    return (low(v), None)

def low_pass(kept, grad):
    return (grad,)

def back_keep(v):
    return (v, None)

def back_low(kept, grad):
    return (low(grad),)
low.defvjp(low_keep, low_pass)
low_back.defvjp(back_keep, back_low)

def layer_norm(resid_in, gain_row, shift_row):
    center = resid_in - lax.optimization_barrier(jnp.mean(resid_in, axis=-1, keepdims=True))
    variance = lax.optimization_barrier(jnp.mean(center * center, axis=-1, keepdims=True))
    return center * lax.rsqrt(variance + norm_eps) * gain_row + shift_row

def matmul(left_op, right_op):
    return jnp.dot(left_op, right_op, precision=lax.Precision.HIGHEST)

def memory_owner(lengths, live_count):
    slot_ids = jnp.arange(DOC_SLOTS)
    live_len = jnp.where(slot_ids < live_count, lengths, 0)
    ends = jnp.cumsum(live_len)
    positions = jnp.arange(MEM_GROUP)
    return lax.optimization_barrier(jnp.sum((positions[:, None] >= ends[None, :]).astype(jnp.int32), axis=1))

def self_attention(queries, keys, values):
    score_scale = HEAD_DIM ** (-0.5)
    causal = jnp.arange(DEC)[:, None] >= jnp.arange(DEC)[None, :]

    def one_doc(doc_item):
        q_doc, k_doc, v_doc = doc_item
        scores = low_back(jnp.einsum('qhd,khd->hqk', q_doc, k_doc, precision=lax.Precision.HIGHEST) * score_scale)
        scores = jnp.where(causal[None], scores, neg_fill)
        row_max = lax.optimization_barrier(jnp.max(scores, axis=-1, keepdims=True))
        prob_all = jnp.exp(scores - row_max)
        row_total = lax.optimization_barrier(jnp.sum(prob_all, axis=-1))
        mixed = jnp.einsum('hqk,khd->qhd', low(prob_all), v_doc, precision=lax.Precision.HIGHEST)
        return mixed / jnp.transpose(row_total)[:, :, None]
    return lax.map(jax.checkpoint(one_doc), (queries, keys, values))

def cross_attention(queries, keys, values, owner, live_count):
    score_scale = HEAD_DIM ** (-0.5)
    slot_ids = jnp.arange(DOC_SLOTS)
    key_blocks = keys.reshape(N_SEQ, MEM_DEV, HEADS, HEAD_DIM)
    value_blocks = values.reshape(N_SEQ, MEM_DEV, HEADS, HEAD_DIM)
    owner_blocks = owner.reshape(N_SEQ, MEM_DEV)

    def one_block(block_item):
        k_blk, v_blk, owner_blk = block_item
        key_valid = (owner_blk[None, :] == slot_ids[:, None]) & (slot_ids[:, None] < live_count)
        mask_full = key_valid[:, None, None, :]
        scores = low_back(jnp.einsum('sqhd,khd->shqk', queries, k_blk, precision=lax.Precision.HIGHEST) * score_scale)
        scores = jnp.where(mask_full, scores, neg_fill)
        part_max = lax.optimization_barrier(jnp.max(scores, axis=-1))
        part_weight = jnp.where(mask_full, jnp.exp(scores - part_max[..., None]), 0.0)
        part_sum = lax.optimization_barrier(jnp.sum(part_weight, axis=-1))
        part_out = jnp.einsum('shqk,khd->shqd', low(part_weight), v_blk, precision=lax.Precision.HIGHEST)
        return (part_max, part_sum, part_out)
    maxes, sums, outs = lax.map(jax.checkpoint(one_block), (key_blocks, value_blocks, owner_blocks))
    top = lax.optimization_barrier(jnp.max(maxes, axis=0))
    block_scale = jnp.exp(maxes - top)
    total = lax.optimization_barrier(jnp.sum(block_scale * sums, axis=0))
    numer = lax.optimization_barrier(jnp.sum(block_scale[..., None] * outs, axis=0))
    has_keys = (slot_ids < live_count)[:, None, None]
    total = jnp.where(has_keys, total, 1.0)
    mixed = numer / total[..., None]
    return jnp.transpose(mixed, (0, 2, 1, 3))

def group_forward(params, x_rows, mem_rows, owner, live_count):
    w_qkv, w_self_out, w_cross_q, w_cross_kv, w_cross_out, w_ffn_in, b_ffn_in, w_ffn_out, gains_low, biases_low = [low(p) for p in params]
    zero_row = jnp.zeros_like(biases_low[0])
    self_proj = matmul(x_rows, w_qkv) + jnp.concatenate([biases_low[0], zero_row, biases_low[1]])
    self_proj = low(low_back(self_proj)).reshape(DOC_SLOTS, DEC, 3, HEADS, HEAD_DIM)
    self_mix = self_attention(self_proj[:, :, 0], self_proj[:, :, 1], self_proj[:, :, 2])
    self_att = low(low_back(self_mix.reshape(DOC_SLOTS * DEC, D)))
    branch_self = low_back(matmul(self_att, w_self_out) + biases_low[2])
    norm_one = layer_norm(x_rows + branch_self, gains_low[0], biases_low[7])
    cross_query = low(low_back(matmul(low(norm_one), w_cross_q) + biases_low[3]))
    memory_kv = low(low_back(matmul(mem_rows, w_cross_kv) + jnp.concatenate([zero_row, biases_low[4]])))
    memory_kv = memory_kv.reshape(MEM_GROUP, 2, HEADS, HEAD_DIM)
    cross_mix = cross_attention(cross_query.reshape(DOC_SLOTS, DEC, HEADS, HEAD_DIM), memory_kv[:, 0], memory_kv[:, 1], owner, live_count)
    cross_att = low(low_back(cross_mix.reshape(DOC_SLOTS * DEC, D)))
    branch_cross = low_back(matmul(cross_att, w_cross_out) + biases_low[5])
    norm_two = layer_norm(norm_one + branch_cross, gains_low[1], biases_low[8])
    hidden = low_back(matmul(low(norm_two), w_ffn_in) + b_ffn_in)
    active = low(jax.nn.gelu(hidden, approximate=False))
    branch_ffn = low_back(matmul(active, w_ffn_out) + biases_low[6])
    return layer_norm(norm_two + branch_ffn, gains_low[2], biases_low[9])

def reference(dec_input, memory, doc_lengths, doc_count, self_qkv, self_out, cross_q, cross_kv, cross_out, ffn_in, ffn_in_bias, ffn_out, norm_gains, biases, out_grad):
    params = (self_qkv, self_out, cross_q, cross_kv, cross_out, ffn_in, ffn_in_bias, ffn_out, norm_gains, biases)

    def per_group(run_carry, group_item):
        x_group, mem_group, len_group, count_group, grad_group = group_item
        owner = memory_owner(len_group, count_group)
        x_rows = x_group.reshape(DOC_SLOTS * DEC, D).astype(jnp.float32)
        mem_rows = mem_group.astype(jnp.float32)

        def forward(param_set, x_in, mem_in):
            return group_forward(param_set, x_in, mem_in, owner, count_group)
        result, pull_back = jax.vjp(forward, params, x_rows, mem_rows)
        grad_params, grad_x, grad_mem = pull_back(grad_group.reshape(DOC_SLOTS * DEC, D).astype(jnp.float32))
        run_carry = jax.tree.map(jnp.add, run_carry, grad_params)
        return (run_carry, (result.astype(jnp.bfloat16).reshape(x_group.shape), grad_x.reshape(x_group.shape), grad_mem))
    start_sums = jax.tree.map(jnp.zeros_like, params)
    sums, stacked = lax.scan(per_group, start_sums, (dec_input, memory, doc_lengths, doc_count, out_grad))
    return (stacked[0], stacked[1], stacked[2], sums[0], sums[1], sums[2], sums[3], sums[4], sums[5], sums[6], sums[7], sums[8], sums[9])
```

```python
from functools import partial

import jax
import jax.numpy as jnp
from jax import lax
from jax.experimental import pallas as pl
from jax.experimental.pallas import tpu as pltpu
from jax.sharding import PartitionSpec as P

D = 768
HEADS = 12
HEAD_DIM = 64
HEAD_GROUPS = 4
GROUP_HEADS = HEADS // HEAD_GROUPS
GROUP_FEATS = GROUP_HEADS * HEAD_DIM

norm_eps = 1e-05
masked_score = -2e30
start_max = -1e30
score_scale = HEAD_DIM ** (-0.5)
key_tile = 256
row_tile = 256
vmem_bytes = 56 * 2**20

f32 = jnp.float32
half = jnp.bfloat16


def layer_norm(resid_in, gain_row, shift_row):
    center = resid_in - jnp.mean(resid_in, axis=-1, keepdims=True)
    variance = jnp.mean(center * center, axis=-1, keepdims=True)
    return center * lax.rsqrt(variance + norm_eps) * gain_row + shift_row


def contract(left_op, right_op, left_dim, right_dim):
    return lax.dot_general(
        left_op,
        right_op,
        (((left_dim,), (right_dim,)), ((), ())),
        preferred_element_type=f32,
    )


def dot_nn(left_op, right_op):
    return contract(left_op, right_op, 1, 0)


def dot_nt(left_op, right_op):
    return contract(left_op, right_op, 1, 1)


def dot_tn(left_op, right_op):
    return contract(left_op, right_op, 0, 0)


def dot_tt(left_op, right_op):
    return contract(left_op, right_op, 0, 1)


def col_sums(grad_low):
    return jnp.sum(grad_low.astype(f32), axis=0)


def head_rows(head):
    return slice(head * HEAD_DIM, (head + 1) * HEAD_DIM)


def self_forward_kernel(proj_ref, mix_ref, att_ref, lse_ref):
    length = proj_ref.shape[2]
    rows = min(row_tile, length)
    for head in range(GROUP_HEADS):
        feats = head_rows(head)
        for first in range(0, length, rows):
            upto = first + rows
            cols = slice(first, upto)
            q_low = proj_ref[0, feats, cols] * jnp.asarray(score_scale, half)
            k_low = proj_ref[0, GROUP_FEATS + head * HEAD_DIM : GROUP_FEATS + (head + 1) * HEAD_DIM, :upto]
            v_low = proj_ref[0, 2 * GROUP_FEATS + head * HEAD_DIM : 2 * GROUP_FEATS + (head + 1) * HEAD_DIM, :upto]
            scores = dot_tn(k_low, q_low)
            key_pos = lax.broadcasted_iota(jnp.int32, scores.shape, 0)
            row_pos = first + lax.broadcasted_iota(jnp.int32, scores.shape, 1)
            scores = jnp.where(key_pos <= row_pos, scores, masked_score)
            top = jnp.max(scores, axis=0, keepdims=True)
            weight = jnp.exp(scores - top)
            total = jnp.sum(weight, axis=0, keepdims=True)
            mix = dot_nn(v_low, weight.astype(half)) / total
            mix_ref[0, feats, cols] = mix
            att_ref[0, feats, cols] = mix.astype(half)
            lse_ref[0, head : head + 1, cols] = top + jnp.log(total)


def self_forward(proj):
    slots, feats, length = proj.shape
    return pl.pallas_call(
        self_forward_kernel,
        grid=(slots,),
        in_specs=[pl.BlockSpec((1, feats, length), lambda s: (s, 0, 0))],
        out_specs=[
            pl.BlockSpec((1, GROUP_FEATS, length), lambda s: (s, 0, 0)),
            pl.BlockSpec((1, GROUP_FEATS, length), lambda s: (s, 0, 0)),
            pl.BlockSpec((1, GROUP_HEADS, length), lambda s: (s, 0, 0)),
        ],
        out_shape=[
            jax.ShapeDtypeStruct((slots, GROUP_FEATS, length), f32),
            jax.ShapeDtypeStruct((slots, GROUP_FEATS, length), half),
            jax.ShapeDtypeStruct((slots, GROUP_HEADS, length), f32),
        ],
        compiler_params=pltpu.CompilerParams(vmem_limit_bytes=vmem_bytes),
        name="self_forward",
    )(proj)


def self_backward_kernel(proj_ref, grad_ref, mix_ref, lse_ref, dproj_ref, dk_ref, dv_ref):
    length = proj_ref.shape[2]
    rows = min(row_tile, length)
    dk_ref[...] = jnp.zeros_like(dk_ref)
    dv_ref[...] = jnp.zeros_like(dv_ref)
    for head in range(GROUP_HEADS):
        feats = head_rows(head)
        for first in range(0, length, rows):
            upto = first + rows
            cols = slice(first, upto)
            q_low = proj_ref[0, feats, cols] * jnp.asarray(score_scale, half)
            k_low = proj_ref[0, GROUP_FEATS + head * HEAD_DIM : GROUP_FEATS + (head + 1) * HEAD_DIM, :upto]
            v_low = proj_ref[0, 2 * GROUP_FEATS + head * HEAD_DIM : 2 * GROUP_FEATS + (head + 1) * HEAD_DIM, :upto]
            g_low = grad_ref[0, feats, cols]
            delta = jnp.sum(g_low.astype(f32) * mix_ref[0, feats, cols], axis=0, keepdims=True)
            scores = dot_tn(k_low, q_low)
            key_pos = lax.broadcasted_iota(jnp.int32, scores.shape, 0)
            row_pos = first + lax.broadcasted_iota(jnp.int32, scores.shape, 1)
            scores = jnp.where(key_pos <= row_pos, scores, masked_score)
            prob = jnp.exp(scores - lse_ref[0, head : head + 1, cols])
            grad_prob = dot_tn(v_low, g_low)
            grad_score = (prob * (grad_prob - delta)).astype(half)
            dv_ref[feats, :upto] += dot_nt(g_low, prob.astype(half))
            dk_ref[feats, :upto] += dot_nt(q_low, grad_score)
            dproj_ref[0, feats, cols] = (dot_nn(k_low, grad_score) * score_scale).astype(half)
    dproj_ref[0, GROUP_FEATS : 2 * GROUP_FEATS, :] = dk_ref[...].astype(half)
    dproj_ref[0, 2 * GROUP_FEATS :, :] = dv_ref[...].astype(half)


def self_backward(proj, grad_mix, mix, lse):
    slots, feats, length = proj.shape
    return pl.pallas_call(
        self_backward_kernel,
        grid=(slots,),
        in_specs=[
            pl.BlockSpec((1, feats, length), lambda s: (s, 0, 0)),
            pl.BlockSpec((1, GROUP_FEATS, length), lambda s: (s, 0, 0)),
            pl.BlockSpec((1, GROUP_FEATS, length), lambda s: (s, 0, 0)),
            pl.BlockSpec((1, GROUP_HEADS, length), lambda s: (s, 0, 0)),
        ],
        out_specs=pl.BlockSpec((1, feats, length), lambda s: (s, 0, 0)),
        out_shape=jax.ShapeDtypeStruct((slots, feats, length), half),
        scratch_shapes=[pltpu.VMEM((GROUP_FEATS, length), f32)] * 2,
        compiler_params=pltpu.CompilerParams(vmem_limit_bytes=vmem_bytes),
        name="self_backward",
    )(proj, grad_mix, mix, lse)


def cross_forward_kernel(low_ref, high_ref, q_ref, k_ref, v_ref, mix_ref, att_ref, lse_ref, acc_ref):
    slot = pl.program_id(0)
    low, high = low_ref[slot], high_ref[slot]
    rows = q_ref.shape[2]
    q_low = q_ref[0] * jnp.asarray(score_scale, half)
    first_tile = low // key_tile
    end_tile = jnp.where(high > low, (high + key_tile - 1) // key_tile, first_tile)
    acc_ref[...] = jnp.zeros_like(acc_ref)

    def step(tile, carry):
        tops, totals = carry
        start = pl.multiple_of(tile * key_tile, key_tile)
        key_pos = start + lax.broadcasted_iota(jnp.int32, (key_tile, rows), 0)
        counted = (key_pos >= low) & (key_pos < high)
        new_tops, new_totals = [], []
        for head in range(GROUP_HEADS):
            feats = head_rows(head)
            k_low = k_ref[feats, pl.ds(start, key_tile)]
            v_low = v_ref[feats, pl.ds(start, key_tile)]
            scores = jnp.where(counted, dot_tn(k_low, q_low[feats]), masked_score)
            top = jnp.maximum(tops[head], jnp.max(scores, axis=0, keepdims=True))
            weight = jnp.exp(scores - top)
            rescale = jnp.exp(tops[head] - top)
            new_totals.append(totals[head] * rescale + jnp.sum(weight, axis=0, keepdims=True))
            new_tops.append(top)
            acc_ref[feats, :] = acc_ref[feats, :] * rescale + dot_nn(v_low, weight.astype(half))
        return (tuple(new_tops), tuple(new_totals))

    init = (
        tuple(jnp.full((1, rows), start_max, f32) for _ in range(GROUP_HEADS)),
        tuple(jnp.zeros((1, rows), f32) for _ in range(GROUP_HEADS)),
    )
    tops, totals = lax.fori_loop(first_tile, end_tile, step, init)
    for head in range(GROUP_HEADS):
        feats = head_rows(head)
        live = totals[head] > 0
        total = jnp.where(live, totals[head], 1.0)
        mix = acc_ref[feats, :] / total
        mix_ref[0, feats, :] = mix
        att_ref[0, feats, :] = mix.astype(half)
        lse_ref[0, head : head + 1, :] = jnp.where(live, tops[head] + jnp.log(total), 0.0)


def cross_forward(low, high, queries, keys, values):
    slots, feats, rows = queries.shape
    tokens = keys.shape[1]
    row_block = pl.BlockSpec((1, feats, rows), lambda s, *_: (s, 0, 0))
    key_block = pl.BlockSpec((feats, tokens), lambda s, *_: (0, 0))
    return pl.pallas_call(
        cross_forward_kernel,
        grid_spec=pltpu.PrefetchScalarGridSpec(
            num_scalar_prefetch=2,
            grid=(slots,),
            in_specs=[row_block, key_block, key_block],
            out_specs=[
                row_block,
                row_block,
                pl.BlockSpec((1, GROUP_HEADS, rows), lambda s, *_: (s, 0, 0)),
            ],
            scratch_shapes=[pltpu.VMEM((feats, rows), f32)],
        ),
        out_shape=[
            jax.ShapeDtypeStruct((slots, feats, rows), f32),
            jax.ShapeDtypeStruct((slots, feats, rows), half),
            jax.ShapeDtypeStruct((slots, GROUP_HEADS, rows), f32),
        ],
        compiler_params=pltpu.CompilerParams(vmem_limit_bytes=vmem_bytes),
        name="cross_forward",
    )(low, high, queries, keys, values)


def cross_backward_kernel(
    low_ref, high_ref, q_ref, g_ref, mix_ref, lse_ref, k_ref, v_ref, dq_ref, dk_ref, dv_ref, acc_ref
):
    slot = pl.program_id(0)
    low, high = low_ref[slot], high_ref[slot]
    rows = q_ref.shape[2]
    q_low = q_ref[0] * jnp.asarray(score_scale, half)
    g_low = g_ref[0]

    @pl.when(slot == 0)
    def _():
        dk_ref[...] = jnp.zeros_like(dk_ref)
        dv_ref[...] = jnp.zeros_like(dv_ref)

    acc_ref[...] = jnp.zeros_like(acc_ref)
    product = g_low.astype(f32) * mix_ref[0]
    delta = [jnp.sum(product[head_rows(h)], axis=0, keepdims=True) for h in range(GROUP_HEADS)]
    lse = [lse_ref[0, h : h + 1, :] for h in range(GROUP_HEADS)]
    first_tile = low // key_tile
    end_tile = jnp.where(high > low, (high + key_tile - 1) // key_tile, first_tile)

    def step(tile, carry):
        start = pl.multiple_of(tile * key_tile, key_tile)
        key_pos = start + lax.broadcasted_iota(jnp.int32, (key_tile, rows), 0)
        counted = (key_pos >= low) & (key_pos < high)
        for head in range(GROUP_HEADS):
            feats = head_rows(head)
            where_keys = (feats, pl.ds(start, key_tile))
            k_low = k_ref[where_keys]
            v_low = v_ref[where_keys]
            scores = jnp.where(counted, dot_tn(k_low, q_low[feats]), masked_score)
            prob = jnp.exp(scores - lse[head])
            grad_prob = dot_tn(v_low, g_low[feats])
            grad_score = (prob * (grad_prob - delta[head])).astype(half)
            dv_ref[where_keys] += dot_nt(g_low[feats], prob.astype(half)).astype(half)
            dk_ref[where_keys] += dot_nt(q_low[feats], grad_score).astype(half)
            acc_ref[feats, :] += dot_nn(k_low, grad_score)
        return carry

    lax.fori_loop(first_tile, end_tile, step, 0)
    dq_ref[0] = (acc_ref[...] * score_scale).astype(half)


def cross_backward(low, high, queries, grad_mix, mix, lse, keys, values):
    slots, feats, rows = queries.shape
    tokens = keys.shape[1]
    row_block = pl.BlockSpec((1, feats, rows), lambda s, *_: (s, 0, 0))
    key_block = pl.BlockSpec((feats, tokens), lambda s, *_: (0, 0))
    return pl.pallas_call(
        cross_backward_kernel,
        grid_spec=pltpu.PrefetchScalarGridSpec(
            num_scalar_prefetch=2,
            grid=(slots,),
            in_specs=[
                row_block,
                row_block,
                row_block,
                pl.BlockSpec((1, GROUP_HEADS, rows), lambda s, *_: (s, 0, 0)),
                key_block,
                key_block,
            ],
            out_specs=[row_block, key_block, key_block],
            scratch_shapes=[pltpu.VMEM((feats, rows), f32)],
        ),
        out_shape=[
            jax.ShapeDtypeStruct((slots, feats, rows), half),
            jax.ShapeDtypeStruct((feats, tokens), half),
            jax.ShapeDtypeStruct((feats, tokens), half),
        ],
        compiler_params=pltpu.CompilerParams(vmem_limit_bytes=vmem_bytes),
        name="cross_backward",
    )(low, high, queries, grad_mix, mix, lse, keys, values)


def body(
    n_doc,
    n_seq,
    dec_input,
    memory,
    doc_lengths,
    doc_count,
    self_qkv,
    self_out,
    cross_q,
    cross_kv,
    cross_out,
    ffn_in,
    ffn_in_bias,
    ffn_out,
    norm_gains,
    biases,
    out_grad,
):
    seq_index = lax.axis_index("seq")
    slots_n, rows_dev = dec_input.shape[1:3]
    rows_total = slots_n * rows_dev
    mem_rows = memory.shape[1]
    spread = n_seq // HEAD_GROUPS
    head_group = seq_index // spread
    member = seq_index % spread
    member_slots = slots_n // spread
    dec_len = rows_dev * n_seq
    same_member = [[h * spread + m for h in range(HEAD_GROUPS)] for m in range(spread)]

    def gather_weight(weight):
        share = weight.shape[0] // n_seq
        piece = lax.dynamic_slice_in_dim(weight, seq_index * share, share, 0).astype(half)
        return lax.all_gather(piece, ("doc", "seq"), axis=0, tiled=True)

    def swap_heads(blocks):
        return lax.all_to_all(blocks, "seq", 0, 0, axis_index_groups=same_member, tiled=True)

    def rotate_heads(block, turn):
        return lax.ppermute(
            block,
            "seq",
            [
                (h * spread + m, (h + turn) % HEAD_GROUPS * spread + m)
                for h in range(HEAD_GROUPS)
                for m in range(spread)
            ],
        )

    def rotate_members(block, turn):
        return lax.ppermute(
            block,
            "seq",
            [
                (h * spread + m, h * spread + (m + turn) % spread)
                for h in range(HEAD_GROUPS)
                for m in range(spread)
            ],
        )

    def exchange(blocks, count, own, rotate):
        got = [lax.dynamic_index_in_dim(blocks, own, 0, keepdims=False)]
        for turn in range(1, count):
            block = lax.dynamic_index_in_dim(blocks, (own + turn) % count, 0, keepdims=False)
            got.append(rotate(block, turn))
        return jnp.stack(got)[(own - jnp.arange(count)) % count]

    qkv_piece = self_qkv.reshape(self_qkv.shape[0], 3, HEAD_GROUPS, GROUP_FEATS)
    qkv_piece = lax.dynamic_index_in_dim(qkv_piece, head_group, 2, keepdims=False)
    qkv_piece = qkv_piece.reshape(self_qkv.shape[0], 3 * GROUP_FEATS).astype(half)
    part = norm_gains.shape[1]
    small = jnp.concatenate([norm_gains, biases, ffn_in_bias.reshape(-1, part)], axis=0).astype(half)
    small_rows = small.shape[0]
    width = 3 * GROUP_FEATS
    pad_rows = -(-small_rows * part // (8 * width)) * 8
    small = jnp.pad(small.reshape(-1), (0, pad_rows * width - small_rows * part))
    first_gather = lax.all_gather(
        jnp.concatenate([qkv_piece, small.reshape(pad_rows, width)], axis=0), "doc", axis=0
    )
    w_qkv_part = first_gather[:, : self_qkv.shape[0]].reshape(D, width)
    small = first_gather[:, self_qkv.shape[0] :].reshape(n_doc, -1)[:, : small_rows * part]
    small = small.reshape(n_doc, small_rows, part).astype(f32)
    gains_f = small[:, :3].transpose(1, 0, 2).reshape(3, D)
    biases_f = small[:, 3:13].transpose(1, 0, 2).reshape(10, D)
    b_ffn_in = small[:, 13:].reshape(-1)

    x_low = dec_input[0].reshape(rows_total, D)
    x_all = lax.all_gather(dec_input[0], "seq", axis=1, tiled=True)
    x_part = lax.dynamic_slice_in_dim(x_all, member * member_slots, member_slots, 0)
    x_part = x_part.reshape(member_slots * dec_len, D)

    w_cross_kv = gather_weight(cross_kv)
    w_self_out = gather_weight(self_out)
    w_cross_q = gather_weight(cross_q)
    w_cross_out = gather_weight(cross_out)
    w_ffn_in = gather_weight(ffn_in)
    w_ffn_out = gather_weight(ffn_out)
    w_qkv = gather_weight(self_qkv)

    zero_part = jnp.zeros((GROUP_FEATS,), f32)
    b_query = lax.dynamic_slice_in_dim(biases_f[0], head_group * GROUP_FEATS, GROUP_FEATS)
    b_value = lax.dynamic_slice_in_dim(biases_f[1], head_group * GROUP_FEATS, GROUP_FEATS)
    proj = dot_tt(w_qkv_part, x_part) + jnp.concatenate([b_query, zero_part, b_value])[:, None]
    proj = proj.astype(half).reshape(width, member_slots, dec_len).transpose(1, 0, 2)
    self_mix, self_att_part, self_lse = self_forward(proj)

    def to_rows(part_grid, feats):
        blocks = part_grid.reshape(member_slots, feats, n_seq, rows_dev).transpose(2, 0, 1, 3)
        got = lax.all_to_all(blocks, "seq", 0, 0, tiled=True)
        return got.reshape(HEAD_GROUPS, spread, member_slots, feats, rows_dev)

    got = to_rows(self_att_part, GROUP_FEATS)
    self_att = got.transpose(0, 3, 1, 2, 4).reshape(D, rows_total)
    branch_self = dot_tn(self_att, w_self_out) + biases_f[2]
    norm_one, pull_one = jax.vjp(
        layer_norm, x_low.astype(f32) + branch_self, gains_f[0], biases_f[7]
    )
    norm_one_low = norm_one.astype(half)

    mem_low = memory[0]
    kv_bias = jnp.concatenate([jnp.zeros((D,), f32), biases_f[4]])
    mem_kv = (dot_tt(w_cross_kv, mem_low) + kv_bias[:, None]).astype(half)
    kv_blocks = mem_kv.reshape(2, HEAD_GROUPS, GROUP_FEATS, mem_rows).transpose(1, 0, 2, 3)
    kv_mine = exchange(kv_blocks, HEAD_GROUPS, head_group, rotate_heads)
    kv_members = [kv_mine] + [rotate_members(kv_mine, turn) for turn in range(1, spread)]
    kv_all = jnp.stack(kv_members)[(member - jnp.arange(spread)) % spread]
    kv_all = kv_all.transpose(2, 3, 1, 0, 4).reshape(2, GROUP_FEATS, n_seq * mem_rows)
    keys_all, values_all = kv_all[0], kv_all[1]

    lengths = doc_lengths[0]
    live_len = jnp.where(jnp.arange(slots_n) < doc_count[0], lengths, 0)
    key_high = jnp.minimum(jnp.cumsum(live_len), n_seq * mem_rows).astype(jnp.int32)
    key_low = jnp.concatenate([jnp.zeros((1,), jnp.int32), key_high[:-1]])

    def rows_to_heads(rows_grid):
        got = swap_heads(rows_grid.reshape(HEAD_GROUPS, GROUP_FEATS, slots_n, rows_dev))
        return got.transpose(2, 1, 0, 3).reshape(slots_n, GROUP_FEATS, HEAD_GROUPS * rows_dev)

    def heads_to_rows(heads_grid):
        blocks = heads_grid.reshape(slots_n, GROUP_FEATS, HEAD_GROUPS, rows_dev)
        return swap_heads(blocks.transpose(2, 1, 0, 3)).reshape(D, rows_total)

    cross_query = (dot_tt(w_cross_q, norm_one_low) + biases_f[3][:, None]).astype(half)
    query_part = rows_to_heads(cross_query)
    cross_mix, cross_att_part, cross_lse = cross_forward(
        key_low, key_high, query_part, keys_all, values_all
    )
    cross_att = heads_to_rows(cross_att_part)
    branch_cross = dot_tn(cross_att, w_cross_out) + biases_f[5]
    norm_two, pull_two = jax.vjp(layer_norm, norm_one + branch_cross, gains_f[1], biases_f[8])
    norm_two_low = norm_two.astype(half)
    hidden = dot_nn(norm_two_low, w_ffn_in) + b_ffn_in
    active, pull_gelu = jax.vjp(partial(jax.nn.gelu, approximate=False), hidden)
    active_low = active.astype(half)
    branch_ffn = dot_nn(active_low, w_ffn_out) + biases_f[6]
    result, pull_three = jax.vjp(layer_norm, norm_two + branch_ffn, gains_f[2], biases_f[9])
    layer_out = result.astype(half).reshape(dec_input.shape)

    def reduce_weight(grad):
        rows, cols = grad.shape
        share = rows // (n_doc * n_seq)
        pieces = grad.astype(half).reshape(n_doc, n_seq, share, cols).transpose(1, 0, 2, 3)
        over_seq = lax.psum_scatter(
            pieces.reshape(rows, cols), "seq", scatter_dimension=0, tiled=True
        )
        over_doc = lax.psum_scatter(over_seq, "doc", scatter_dimension=0, tiled=True)
        return lax.all_gather(over_doc, "seq", axis=0, tiled=True).astype(f32)

    grad_r3, grad_g2, grad_c9 = pull_three(out_grad[0].reshape(rows_total, D).astype(f32))
    grad_ffn_low = grad_r3.astype(half)
    grad_w_down = reduce_weight(dot_tn(active_low, grad_ffn_low))
    grad_b6 = col_sums(grad_ffn_low)
    grad_hidden = pull_gelu(dot_nt(grad_ffn_low, w_ffn_out))[0].astype(half)
    grad_w_in = reduce_weight(dot_tn(norm_two_low, grad_hidden))
    grad_b_in = col_sums(grad_hidden)
    grad_r2, grad_g1, grad_c8 = pull_two(grad_r3 + dot_nt(grad_hidden, w_ffn_in))
    grad_cross_low = grad_r2.astype(half)
    grad_w_cross_out = reduce_weight(dot_nn(cross_att, grad_cross_low))
    grad_b5 = col_sums(grad_cross_low)
    grad_mix = dot_nt(w_cross_out, grad_cross_low).astype(half)
    grad_query_part, grad_keys, grad_values = cross_backward(
        key_low,
        key_high,
        query_part,
        rows_to_heads(grad_mix),
        cross_mix,
        cross_lse,
        keys_all,
        values_all,
    )
    grad_query = heads_to_rows(grad_query_part)
    grad_w_cross_q = reduce_weight(dot_tt(norm_one_low, grad_query))
    grad_b3 = jnp.sum(grad_query.astype(f32), axis=1)
    grad_r1, grad_g0, grad_c7 = pull_one(grad_r2 + dot_tt(grad_query, w_cross_q))
    grad_self_low = grad_r1.astype(half)
    grad_w_self_out = reduce_weight(dot_nn(self_att, grad_self_low))
    grad_b2 = col_sums(grad_self_low)
    grad_self_mix = dot_nt(w_self_out, grad_self_low).astype(half)
    blocks = grad_self_mix.reshape(HEAD_GROUPS, GROUP_FEATS, spread, member_slots, rows_dev)
    blocks = blocks.transpose(0, 2, 3, 1, 4).reshape(n_seq, member_slots, GROUP_FEATS, rows_dev)
    got = lax.all_to_all(blocks, "seq", 0, 0, tiled=True)
    grad_self_part = got.transpose(1, 2, 0, 3).reshape(member_slots, GROUP_FEATS, dec_len)
    grad_proj_part = self_backward(proj, grad_self_part, self_mix, self_lse)

    grad_kv = jnp.stack([grad_keys, grad_values]).reshape(
        2, GROUP_FEATS, HEAD_GROUPS, spread, mem_rows
    )
    grad_kv = grad_kv.transpose(3, 2, 0, 1, 4)
    grad_kv = jnp.sum(exchange(grad_kv, spread, member, rotate_members).astype(f32), axis=0)
    grad_kv = exchange(grad_kv.astype(half), HEAD_GROUPS, head_group, rotate_heads)
    grad_mem_kv = grad_kv.transpose(1, 0, 2, 3).reshape(2 * D, mem_rows)
    grad_w_cross_kv = reduce_weight(dot_tt(mem_low, grad_mem_kv))
    grad_b4 = jnp.sum(grad_mem_kv[D:].astype(f32), axis=1)
    memory_grad = dot_tt(grad_mem_kv, w_cross_kv)[None]

    grad_part = dot_tt(
        x_part, grad_proj_part.transpose(1, 0, 2).reshape(width, member_slots * dec_len)
    ).astype(half)
    share = self_qkv.shape[0] // spread
    grad_part = grad_part.reshape(n_doc, spread, share, width).transpose(1, 0, 2, 3)
    grad_part = jnp.sum(exchange(grad_part, spread, member, rotate_members).astype(f32), axis=0)
    grad_part = lax.psum_scatter(
        grad_part.astype(half).reshape(n_doc * share, width), "doc", scatter_dimension=0, tiled=True
    )
    grad_w_qkv = lax.all_gather(grad_part, "seq", axis=0)
    grad_w_qkv = grad_w_qkv.reshape(HEAD_GROUPS, spread, share, 3, GROUP_FEATS)
    grad_w_qkv = grad_w_qkv.transpose(1, 2, 3, 0, 4).reshape(self_qkv.shape).astype(f32)
    got = to_rows(grad_proj_part, width).reshape(
        HEAD_GROUPS, slots_n, 3, GROUP_FEATS, rows_dev
    )
    grad_proj = got.transpose(2, 0, 3, 1, 4).reshape(3 * D, rows_total)
    row_sums = jnp.sum(grad_proj.astype(f32), axis=1)
    grad_b0 = row_sums[:D]
    grad_b1 = row_sums[2 * D :]
    input_grad = (grad_r1 + dot_tt(grad_proj, w_qkv)).reshape(dec_input.shape)

    small_grad = jnp.concatenate(
        [
            jnp.stack(
                [grad_g0, grad_g1, grad_g2]
                + [grad_b0, grad_b1, grad_b2, grad_b3, grad_b4, grad_b5, grad_b6]
                + [grad_c7, grad_c8, grad_c9]
            ),
            grad_b_in.reshape(n_doc, -1, part).transpose(1, 0, 2).reshape(-1, D),
        ]
    ).astype(half)
    small_grad = lax.psum(small_grad, ("doc", "seq"))
    small_grad = lax.dynamic_slice_in_dim(
        small_grad, lax.axis_index("doc") * part, part, 1
    ).astype(f32)
    return (
        layer_out,
        input_grad,
        memory_grad,
        grad_w_qkv,
        grad_w_self_out,
        grad_w_cross_q,
        grad_w_cross_kv,
        grad_w_cross_out,
        grad_w_in,
        small_grad[13:].reshape(-1),
        grad_w_down,
        small_grad[:3],
        small_grad[3:13],
    )


def solution(mesh):
    placed = (
        P("doc", None, "seq", None),
        P("doc", "seq", None),
        P("doc", None),
        P("doc"),
        P("doc", None),
        P("doc", None),
        P("doc", None),
        P("doc", None),
        P("doc", None),
        P("doc", None),
        P("doc"),
        P("doc", None),
        P(None, "doc"),
        P(None, "doc"),
        P("doc", None, "seq", None),
    )
    return jax.shard_map(
        partial(body, mesh.shape["doc"], mesh.shape["seq"]),
        mesh=mesh,
        in_specs=placed,
        out_specs=(
            P("doc", None, "seq", None),
            P("doc", None, "seq", None),
            P("doc", "seq", None),
            P("doc", None),
            P("doc", None),
            P("doc", None),
            P("doc", None),
            P("doc", None),
            P("doc", None),
            P("doc"),
            P("doc", None),
            P(None, "doc"),
            P(None, "doc"),
        ),
        check_vma=False,
    )
```

```python
from functools import partial

import jax
import jax.numpy as jnp
from jax import lax
from jax.experimental import pallas as pl
from jax.experimental.pallas import tpu as pltpu
from jax.sharding import PartitionSpec as P

D = 768
HEADS = 12
HEAD_DIM = 64
HEAD_GROUPS = 4
GROUP_HEADS = HEADS // HEAD_GROUPS
GROUP_FEATS = GROUP_HEADS * HEAD_DIM

norm_eps = 1e-05
masked_score = -2e30
start_max = -1e30
score_scale = HEAD_DIM ** (-0.5)
key_tile = 256
row_tile = 256
vmem_bytes = 56 * 2**20

f32 = jnp.float32
half = jnp.bfloat16


def layer_norm(resid_in, gain_row, shift_row):
    center = resid_in - jnp.mean(resid_in, axis=-1, keepdims=True)
    variance = jnp.mean(center * center, axis=-1, keepdims=True)
    return center * lax.rsqrt(variance + norm_eps) * gain_row + shift_row


def contract(left_op, right_op, left_dim, right_dim):
    return lax.dot_general(
        left_op,
        right_op,
        (((left_dim,), (right_dim,)), ((), ())),
        preferred_element_type=f32,
    )


def dot_nn(left_op, right_op):
    return contract(left_op, right_op, 1, 0)


def dot_nt(left_op, right_op):
    return contract(left_op, right_op, 1, 1)


def dot_tn(left_op, right_op):
    return contract(left_op, right_op, 0, 0)


def dot_tt(left_op, right_op):
    return contract(left_op, right_op, 0, 1)


def col_sums(grad_low):
    return jnp.sum(grad_low.astype(f32), axis=0)


def normalize(resid):
    center = resid - jnp.mean(resid, axis=-1, keepdims=True)
    scale = lax.rsqrt(jnp.mean(center * center, axis=-1, keepdims=True) + norm_eps)
    return center * scale, scale


def norm_backward(incoming, gain_row, unit, scale):
    grad = incoming * gain_row
    mean_one = jnp.mean(grad, axis=-1, keepdims=True)
    mean_two = jnp.mean(grad * unit, axis=-1, keepdims=True)
    return (grad - mean_one - unit * mean_two) * scale


def row_sum(grad):
    return jnp.sum(grad, axis=0, keepdims=True)


def store_rows(packed_ref, n_doc, grad, cols):
    n_seq, rows = packed_ref.shape[:2]
    share = rows // n_doc
    for s in range(n_seq):
        mine = [grad[(z * n_seq + s) * share : (z * n_seq + s + 1) * share] for z in range(n_doc)]
        packed_ref[s, :, cols] = jnp.concatenate(mine, axis=0).astype(half)


def head_feats(head, block=0):
    start = block * GROUP_FEATS + head * HEAD_DIM
    return slice(start, start + HEAD_DIM)


def load_rows(place_ref, piece_refs, x_ref, sems):
    spread = place_ref.shape[0] // HEAD_GROUPS
    slots = x_ref.shape[0]
    rows_dev = x_ref.shape[1] // place_ref.shape[0]
    member = place_ref[0] % spread
    copies = []
    for i in range(place_ref.shape[0]):
        turn_m, turn_h = i // HEAD_GROUPS, i % HEAD_GROUPS
        if turn_m:
            piece = piece_refs[HEAD_GROUPS + turn_m - 1].at[turn_h]
        else:
            piece = piece_refs[turn_h].at[pl.ds(member * slots, slots)]
        first = pl.multiple_of(place_ref[i] * rows_dev, rows_dev)
        copies.append(
            pltpu.make_async_copy(piece, x_ref.at[:, pl.ds(first, rows_dev)], sems.at[i])
        )
    for copy in copies:
        copy.start()
    for copy in copies:
        copy.wait()


def self_forward_kernel(place_ref, w_ref, bias_ref, *rest):
    pieces, (proj_ref, mix_ref, att_ref, lse_ref, x_ref, sems) = rest[:-6], rest[-6:]
    slot = pl.program_id(0)

    @pl.when(slot == 0)
    def _():
        load_rows(place_ref, pieces, x_ref, sems)

    length = proj_ref.shape[1]
    rows_dev = att_ref.shape[3]
    rows = min(row_tile, length)
    for first in range(0, length, rows):
        part = dot_nn(x_ref[slot, first : first + rows, :], w_ref[...]) + bias_ref[0:1, :]
        proj_ref[:, first : first + rows] = part.astype(half).T
    for head in range(GROUP_HEADS):
        feats = head_feats(head)
        for first in range(0, length, rows):
            upto = first + rows
            cols = slice(first, upto)
            q_low = proj_ref[feats, cols] * jnp.asarray(score_scale, half)
            k_low = proj_ref[head_feats(head, 1), :upto]
            v_low = proj_ref[head_feats(head, 2), :upto]
            scores = dot_tn(k_low, q_low)
            key_pos = lax.broadcasted_iota(jnp.int32, scores.shape, 0)
            row_pos = first + lax.broadcasted_iota(jnp.int32, scores.shape, 1)
            scores = jnp.where(key_pos <= row_pos, scores, masked_score)
            top = jnp.max(scores, axis=0, keepdims=True)
            weight = jnp.exp(scores - top)
            total = jnp.sum(weight, axis=0, keepdims=True)
            mix = dot_nn(v_low, weight.astype(half)) / total
            mix_ref[0, feats, cols] = mix
            mix_low = mix.astype(half)
            for place in range(rows // rows_dev):
                att_ref[first // rows_dev + place, 0, feats, :] = mix_low[
                    :, place * rows_dev : (place + 1) * rows_dev
                ]
            lse_ref[0, head : head + 1, cols] = top + jnp.log(total)


def self_forward(places, w_part, bias, pieces, n_seq, *after):
    slots = pieces[0].shape[0] * HEAD_GROUPS // n_seq
    length = pieces[0].shape[1] * n_seq
    feats, rows_dev = w_part.shape[1], length // n_seq
    return pl.pallas_call(
        self_forward_kernel,
        grid_spec=pltpu.PrefetchScalarGridSpec(
            num_scalar_prefetch=1,
            grid=(slots,),
            in_specs=[
                pl.BlockSpec(w_part.shape, lambda s, *_: (0, 0)),
                pl.BlockSpec(bias.shape, lambda s, *_: (0, 0)),
            ]
            + [pl.BlockSpec(memory_space=pl.ANY)] * (len(pieces) + len(after)),
            out_specs=[
                pl.BlockSpec((feats, length), lambda s, *_: (0, s)),
                pl.BlockSpec((1, GROUP_FEATS, length), lambda s, *_: (s, 0, 0)),
                pl.BlockSpec((n_seq, 1, GROUP_FEATS, rows_dev), lambda s, *_: (0, s, 0, 0)),
                pl.BlockSpec((1, GROUP_HEADS, length), lambda s, *_: (s, 0, 0)),
            ],
            scratch_shapes=[
                pltpu.VMEM((slots, length, D), half),
                pltpu.SemaphoreType.DMA((n_seq,)),
            ],
        ),
        out_shape=[
            jax.ShapeDtypeStruct((feats, slots * length), half),
            jax.ShapeDtypeStruct((slots, GROUP_FEATS, length), f32),
            jax.ShapeDtypeStruct((n_seq, slots, GROUP_FEATS, rows_dev), half),
            jax.ShapeDtypeStruct((slots, GROUP_HEADS, length), f32),
        ],
        compiler_params=pltpu.CompilerParams(vmem_limit_bytes=vmem_bytes),
        name="self_forward",
    )(places, w_part, bias, *pieces, *after)


def self_backward_kernel(n_doc, place_ref, proj_ref, grad_ref, mix_ref, lse_ref, *rest):
    ins, (send_ref, w_grad_ref, sums_ref, dproj_ref, dk_ref, dv_ref, w_acc, x_ref, sems) = (
        rest[:-9],
        rest[-9:],
    )
    pieces = ins[: HEAD_GROUPS + place_ref.shape[0] // HEAD_GROUPS - 1]
    slot = pl.program_id(0)

    @pl.when(slot == 0)
    def _():
        load_rows(place_ref, pieces, x_ref, sems)
        w_acc[...] = jnp.zeros_like(w_acc)
        sums_ref[...] = jnp.zeros_like(sums_ref)

    length = proj_ref.shape[1]
    n_seq, rows_dev = grad_ref.shape[0], grad_ref.shape[3]
    rows = min(row_tile, length)
    dk_ref[...] = jnp.zeros_like(dk_ref)
    dv_ref[...] = jnp.zeros_like(dv_ref)
    for head in range(GROUP_HEADS):
        feats = head_feats(head)
        for first in range(0, length, rows):
            upto = first + rows
            cols = slice(first, upto)
            places = range(first // rows_dev, upto // rows_dev)
            q_low = proj_ref[feats, cols] * jnp.asarray(score_scale, half)
            k_low = proj_ref[head_feats(head, 1), :upto]
            v_low = proj_ref[head_feats(head, 2), :upto]
            g_low = jnp.concatenate([grad_ref[place, 0, feats, :] for place in places], axis=1)
            delta = jnp.sum(g_low.astype(f32) * mix_ref[0, feats, cols], axis=0, keepdims=True)
            scores = dot_tn(k_low, q_low)
            key_pos = lax.broadcasted_iota(jnp.int32, scores.shape, 0)
            row_pos = first + lax.broadcasted_iota(jnp.int32, scores.shape, 1)
            scores = jnp.where(key_pos <= row_pos, scores, masked_score)
            prob = jnp.exp(scores - lse_ref[0, head : head + 1, cols])
            grad_prob = dot_tn(v_low, g_low)
            grad_score = (prob * (grad_prob - delta)).astype(half)
            dv_ref[feats, :upto] += dot_nt(g_low, prob.astype(half))
            dk_ref[feats, :upto] += dot_nt(q_low, grad_score)
            dproj_ref[feats, cols] = (dot_nn(k_low, grad_score) * score_scale).astype(half)
    dproj_ref[GROUP_FEATS : 2 * GROUP_FEATS, :] = dk_ref[...].astype(half)
    dproj_ref[2 * GROUP_FEATS :, :] = dv_ref[...].astype(half)
    for place in range(n_seq):
        send_ref[place, 0] = dproj_ref[:, place * rows_dev : (place + 1) * rows_dev]
    for first in range(0, length, rows):
        turned = dproj_ref[:, first : first + rows].T
        sums_ref[0:1, :] += row_sum(turned.astype(f32))
        w_acc[...] += dot_tn(x_ref[slot, first : first + rows, :], turned)

    @pl.when(slot == pl.num_programs(0) - 1)
    def _():
        spread, stored, width = w_grad_ref.shape
        share = stored // n_doc
        feats = dproj_ref.shape[0]
        quarters = width // feats
        for m in range(spread):
            for q in range(quarters):
                mine = []
                for z in range(n_doc):
                    first = ((z * spread + m) * quarters + q) * share
                    mine.append(w_acc[first : first + share, :])
                w_grad_ref[m, :, q * feats : (q + 1) * feats] = jnp.concatenate(
                    mine, axis=0
                ).astype(half)


def self_backward(n_doc, places, proj, grad_mix, mix, lse, pieces, *after):
    n_seq, slots, _, rows_dev = grad_mix.shape
    feats, length = proj.shape[0], n_seq * rows_dev
    spread = n_seq // HEAD_GROUPS
    stored = D // n_seq
    return pl.pallas_call(
        partial(self_backward_kernel, n_doc),
        grid_spec=pltpu.PrefetchScalarGridSpec(
            num_scalar_prefetch=1,
            grid=(slots,),
            in_specs=[
                pl.BlockSpec((feats, length), lambda s, *_: (0, s)),
                pl.BlockSpec((n_seq, 1, GROUP_FEATS, rows_dev), lambda s, *_: (0, s, 0, 0)),
                pl.BlockSpec((1, GROUP_FEATS, length), lambda s, *_: (s, 0, 0)),
                pl.BlockSpec((1, GROUP_HEADS, length), lambda s, *_: (s, 0, 0)),
            ]
            + [pl.BlockSpec(memory_space=pl.ANY)] * (len(pieces) + len(after)),
            out_specs=[
                pl.BlockSpec((n_seq, 1, feats, rows_dev), lambda s, *_: (0, s, 0, 0)),
                pl.BlockSpec((spread, stored, HEAD_GROUPS * feats), lambda s, *_: (0, 0, 0)),
                pl.BlockSpec((8, feats), lambda s, *_: (0, 0)),
            ],
            scratch_shapes=[
                pltpu.VMEM((feats, length), half),
                pltpu.VMEM((GROUP_FEATS, length), f32),
                pltpu.VMEM((GROUP_FEATS, length), f32),
                pltpu.VMEM((D, feats), f32),
                pltpu.VMEM((slots, length, D), half),
                pltpu.SemaphoreType.DMA((n_seq,)),
            ],
        ),
        out_shape=[
            jax.ShapeDtypeStruct((n_seq, slots, feats, rows_dev), half),
            jax.ShapeDtypeStruct((spread, stored, HEAD_GROUPS * feats), half),
            jax.ShapeDtypeStruct((8, feats), f32),
        ],
        compiler_params=pltpu.CompilerParams(vmem_limit_bytes=vmem_bytes),
        name="self_backward",
    )(places, proj, grad_mix, mix, lse, *pieces, *after)


def enter_kernel(att_ref, x_ref, vec_ref, w_ref, norm_ref, unit_ref, scale_ref, send_ref, att_all):
    gather_att(att_ref, att_all)
    slots, rows_dev = send_ref.shape[1], send_ref.shape[3]
    rows = min(middle_rows, x_ref.shape[0])
    for first in range(0, x_ref.shape[0], rows):
        where = slice(first, first + rows)
        branch = dot_tn(att_all[:, where], w_ref[:, :D]) + vec_ref[0:1, :]
        unit, scale = normalize(x_ref[where, :].astype(f32) + branch)
        norm = unit * vec_ref[1:2, :] + vec_ref[2:3, :]
        norm_ref[where, :] = norm
        unit_ref[where, :] = unit
        scale_ref[where, :] = jnp.broadcast_to(scale, (rows, scale_ref.shape[1]))
        query = dot_nn(norm.astype(half), w_ref[:, D:]) + vec_ref[3:4, :]
        query = query.astype(half).T
        for group in range(HEAD_GROUPS):
            for place in range(rows // rows_dev):
                send_ref[group, first // rows_dev + place] = query[
                    group * GROUP_FEATS : (group + 1) * GROUP_FEATS,
                    place * rows_dev : (place + 1) * rows_dev,
                ]


def gather_att(att_ref, att_all):
    n_seq, member_slots, _, rows_dev = att_ref.shape
    spread = n_seq // HEAD_GROUPS
    for source in range(n_seq):
        group, m = source // spread, source % spread
        for inner in range(member_slots):
            slot = m * member_slots + inner
            att_all[
                group * GROUP_FEATS : (group + 1) * GROUP_FEATS,
                slot * rows_dev : (slot + 1) * rows_dev,
            ] = att_ref[source, inner]


def enter(att, x_low, vectors, w_pair, slots):
    rows_total, rows_dev = x_low.shape[0], att.shape[3]
    vmem = pl.BlockSpec(memory_space=pltpu.VMEM)
    return pl.pallas_call(
        enter_kernel,
        in_specs=[vmem] * 4,
        out_specs=[vmem] * 4,
        out_shape=[
            jax.ShapeDtypeStruct((rows_total, D), f32),
            jax.ShapeDtypeStruct((rows_total, D), f32),
            jax.ShapeDtypeStruct((rows_total, 128), f32),
            jax.ShapeDtypeStruct((HEAD_GROUPS, slots, GROUP_FEATS, rows_dev), half),
        ],
        scratch_shapes=[pltpu.VMEM((D, rows_total), half)],
        compiler_params=pltpu.CompilerParams(vmem_limit_bytes=vmem_bytes),
        name="enter",
    )(att, x_low, vectors, w_pair)


def leave_kernel(
    n_doc,
    query_ref,
    att_ref,
    resid_ref,
    norm_ref,
    unit_ref,
    scale_ref,
    vec_ref,
    w_ref,
    *rest,
):
    out_ref, send_ref, packed_ref, sums_ref, att_all, query_all, query_rows, low_rows = rest[-8:]
    slots, rows_dev = query_ref.shape[1], query_ref.shape[3]
    member_slots = att_ref.shape[1]
    spread = slots // member_slots
    rows_total = resid_ref.shape[0]
    rows = min(middle_rows, rows_total)
    gather_att(att_ref, att_all)
    for group in range(HEAD_GROUPS):
        for slot in range(slots):
            query_all[
                group * GROUP_FEATS : (group + 1) * GROUP_FEATS,
                slot * rows_dev : (slot + 1) * rows_dev,
            ] = query_ref[group, slot]
    sums_ref[...] = jnp.zeros_like(sums_ref)
    for first in range(0, rows_total, rows):
        where = slice(first, first + rows)
        query = query_all[:, where].T
        query_rows[where, :] = query
        sums_ref[3:4, :] += row_sum(query.astype(f32))
        incoming = resid_ref[where, :] + dot_nt(query, w_ref[:, D:])
        unit = unit_ref[where, :]
        sums_ref[0:1, :] += row_sum(incoming * unit)
        sums_ref[1:2, :] += row_sum(incoming)
        grad = norm_backward(incoming, vec_ref[1:2, :], unit, scale_ref[where, 0:1])
        out_ref[where, :] = grad
        grad_low = grad.astype(half)
        low_rows[where, :] = grad_low
        sums_ref[2:3, :] += row_sum(grad_low.astype(f32))
    grad_att = dot_nt(w_ref[:, :D], low_rows[...]).astype(half)
    for target in range(HEAD_GROUPS * spread):
        group, m = target // spread, target % spread
        for inner in range(member_slots):
            slot = m * member_slots + inner
            send_ref[target, inner] = grad_att[
                group * GROUP_FEATS : (group + 1) * GROUP_FEATS,
                slot * rows_dev : (slot + 1) * rows_dev,
            ]
    store_rows(packed_ref, n_doc, dot_nn(att_all[...], low_rows[...]), slice(0, D))
    grad = dot_tn(norm_ref[...].astype(half), query_rows[...])
    store_rows(packed_ref, n_doc, grad, slice(D, 2 * D))


def leave(n_doc, grad_query, att, resid, norm_one, unit, scale, vectors, w_pair, *after):
    rows_total, n_seq = resid.shape[0], att.shape[0]
    vmem = pl.BlockSpec(memory_space=pltpu.VMEM)
    return pl.pallas_call(
        partial(leave_kernel, n_doc),
        in_specs=[vmem] * 8 + [pl.BlockSpec(memory_space=pl.ANY)] * len(after),
        out_specs=[vmem] * 4,
        out_shape=[
            jax.ShapeDtypeStruct((rows_total, D), f32),
            jax.ShapeDtypeStruct(att.shape, half),
            jax.ShapeDtypeStruct((n_seq, D // n_seq, 2 * D), half),
            jax.ShapeDtypeStruct((8, D), f32),
        ],
        scratch_shapes=[
            pltpu.VMEM((D, rows_total), half),
            pltpu.VMEM((D, rows_total), half),
            pltpu.VMEM((rows_total, D), half),
            pltpu.VMEM((rows_total, D), half),
        ],
        compiler_params=pltpu.CompilerParams(vmem_limit_bytes=vmem_bytes),
        name="leave",
    )(grad_query, att, resid, norm_one, unit, scale, vectors, w_pair, *after)


def memory_kernel(n_doc, place_ref, mem_ref, rows_a_ref, rows_b_ref, rows_c_ref, *rest):
    pieces, (packed_ref, all_ref) = rest[: place_ref.shape[0]], rest[-2:]
    for turn, piece in enumerate(pieces):
        for kind in range(2):
            first = pl.multiple_of(kind * D + place_ref[turn] * GROUP_FEATS, GROUP_FEATS)
            all_ref[pl.ds(first, GROUP_FEATS), :] = piece[kind]
    turned = all_ref[...].T
    for kind in range(2):
        cols = slice(kind * D, (kind + 1) * D)
        store_rows(packed_ref, n_doc, dot_tn(mem_ref[...], turned[:, cols]), cols)
    value_sum = row_sum(turned[:, D:].astype(f32))
    small = [rows_a_ref[...], rows_b_ref[...], rows_c_ref[...], value_sum]
    used = sum(rows.shape[0] for rows in small)
    small.append(jnp.zeros((small_cols - used, D), f32))
    store_rows(
        packed_ref, n_doc, jnp.concatenate(small, axis=0).T, slice(2 * D, 2 * D + small_cols)
    )


small_cols = 128


def memory_backward(n_doc, n_seq, places, mem_low, rows_a, rows_b, rows_c, pieces, *after):
    tokens = mem_low.shape[0]
    vmem = pl.BlockSpec(memory_space=pltpu.VMEM)
    return pl.pallas_call(
        partial(memory_kernel, n_doc),
        grid_spec=pltpu.PrefetchScalarGridSpec(
            num_scalar_prefetch=1,
            grid=(1,),
            in_specs=[vmem] * (4 + len(pieces))
            + [pl.BlockSpec(memory_space=pl.ANY)] * len(after),
            out_specs=[vmem] * 2,
        ),
        out_shape=[
            jax.ShapeDtypeStruct((n_seq, D // n_seq, 2 * D + small_cols), half),
            jax.ShapeDtypeStruct((2 * D, tokens), half),
        ],
        compiler_params=pltpu.CompilerParams(vmem_limit_bytes=vmem_bytes),
        name="memory_backward",
    )(places, mem_low, rows_a, rows_b, rows_c, *pieces, *after)


def finish_kernel(
    n_seq,
    stack_n,
    in_ref,
    qkv_ref,
    out_ref,
    q_ref,
    kv_ref,
    small_ref,
    bias_ref,
    down_ref,
    ffn_ref,
    cross_ref,
):
    rows = in_ref.shape[0]
    share = rows // n_seq
    spread = n_seq // HEAD_GROUPS
    out_ref[...] = in_ref[:, :D].astype(f32)
    q_ref[...] = in_ref[:, D : 2 * D].astype(f32)
    kv_ref[...] = in_ref[:, 2 * D : 4 * D].astype(f32)
    small_ref[...] = in_ref[:, 4 * D : 4 * D + small_cols].astype(f32).T
    first_col = 4 * D + small_cols
    feats = 3 * GROUP_FEATS
    ff = ffn_ref.shape[1]
    down_col = first_col + HEAD_GROUPS * feats + small_cols
    ffn_col = down_col + stack_n * D
    ffn_ref[...] = in_ref[:, ffn_col : ffn_col + ff].astype(f32)
    cross_ref[...] = in_ref[:, ffn_col + ff :].astype(f32)
    for q in range(stack_n):
        mine = in_ref[:, down_col + q * D : down_col + (q + 1) * D].astype(f32)
        for s in range(n_seq):
            first = (s * stack_n + q) * share
            down_ref[first : first + share, :] = mine[s * share : (s + 1) * share]
    bias = jnp.zeros(bias_ref.shape, f32)
    wide = in_ref[:, first_col:down_col].astype(f32)
    for s in range(n_seq):
        group, m = s // spread, s % spread
        mine = wide[s * share : (s + 1) * share]
        for q in range(HEAD_GROUPS):
            first = (m * HEAD_GROUPS + q) * share
            for part in range(3):
                start = q * feats + part * GROUP_FEATS
                qkv_ref[
                    first : first + share,
                    part * D + group * GROUP_FEATS : part * D + (group + 1) * GROUP_FEATS,
                ] = mine[:, start : start + GROUP_FEATS]
        bias = bias + mine[:, HEAD_GROUPS * feats :]
    bias_ref[...] = bias


def finish(n_seq, stack_n, packed):
    rows = packed.shape[0]
    vmem = pl.BlockSpec(memory_space=pltpu.VMEM)
    return pl.pallas_call(
        partial(finish_kernel, n_seq, stack_n),
        in_specs=[vmem],
        out_specs=[vmem] * 9,
        out_shape=[
            jax.ShapeDtypeStruct((rows, 3 * D), f32),
            jax.ShapeDtypeStruct((rows, D), f32),
            jax.ShapeDtypeStruct((rows, D), f32),
            jax.ShapeDtypeStruct((rows, 2 * D), f32),
            jax.ShapeDtypeStruct((small_cols, rows), f32),
            jax.ShapeDtypeStruct((rows // n_seq, small_cols), f32),
            jax.ShapeDtypeStruct((rows * stack_n, D), f32),
            jax.ShapeDtypeStruct((rows, stack_n * D), f32),
            jax.ShapeDtypeStruct((rows, D), f32),
        ],
        compiler_params=pltpu.CompilerParams(vmem_limit_bytes=vmem_bytes),
        name="finish",
    )(packed)


def load_pieces(place_ref, piece_refs, kv_ref, sems):
    tokens = piece_refs[0].shape[2]
    copies = [
        pltpu.make_async_copy(
            piece,
            kv_ref.at[:, :, pl.ds(pl.multiple_of(place_ref[i] * tokens, tokens), tokens)],
            sems.at[i],
        )
        for i, piece in enumerate(piece_refs)
    ]
    for copy in copies:
        copy.start()
    for copy in copies:
        copy.wait()


def tiles_of(low, high):
    first = low // key_tile
    return first, jnp.where(high > low, (high + key_tile - 1) // key_tile, first)


def cross_forward_kernel(low_ref, high_ref, place_ref, q_ref, *rest):
    pieces, (mix_ref, att_ref, lse_ref, acc_ref, kv_ref, sems) = rest[:-6], rest[-6:]
    slot = pl.program_id(0)

    @pl.when(slot == 0)
    def _():
        load_pieces(place_ref, pieces, kv_ref, sems)

    low, high = low_ref[slot], high_ref[slot]
    rows_dev = q_ref.shape[3]
    q_low = jnp.concatenate([q_ref[i, 0] for i in range(HEAD_GROUPS)], axis=1)
    q_low = q_low * jnp.asarray(score_scale, half)
    rows = q_low.shape[1]
    acc_ref[...] = jnp.zeros_like(acc_ref)

    def step(tile, carry):
        tops, totals = carry
        start = pl.multiple_of(tile * key_tile, key_tile)
        key_pos = start + lax.broadcasted_iota(jnp.int32, (key_tile, rows), 0)
        counted = (key_pos >= low) & (key_pos < high)
        new_tops, new_totals = [], []
        for head in range(GROUP_HEADS):
            feats = head_feats(head)
            k_low = kv_ref[0, feats, pl.ds(start, key_tile)]
            v_low = kv_ref[1, feats, pl.ds(start, key_tile)]
            scores = jnp.where(counted, dot_tn(k_low, q_low[feats]), masked_score)
            top = jnp.maximum(tops[head], jnp.max(scores, axis=0, keepdims=True))
            weight = jnp.exp(scores - top)
            rescale = jnp.exp(tops[head] - top)
            new_totals.append(totals[head] * rescale + jnp.sum(weight, axis=0, keepdims=True))
            new_tops.append(top)
            acc_ref[feats, :] = acc_ref[feats, :] * rescale + dot_nn(v_low, weight.astype(half))
        return (tuple(new_tops), tuple(new_totals))

    init = (
        tuple(jnp.full((1, rows), start_max, f32) for _ in range(GROUP_HEADS)),
        tuple(jnp.zeros((1, rows), f32) for _ in range(GROUP_HEADS)),
    )
    tops, totals = lax.fori_loop(*tiles_of(low, high), step, init)
    for head in range(GROUP_HEADS):
        feats = head_feats(head)
        live = totals[head] > 0
        total = jnp.where(live, totals[head], 1.0)
        mix = acc_ref[feats, :] / total
        mix_ref[0, feats, :] = mix
        mix_low = mix.astype(half)
        for i in range(HEAD_GROUPS):
            att_ref[i, 0, feats, :] = mix_low[:, i * rows_dev : (i + 1) * rows_dev]
        lse_ref[0, head : head + 1, :] = jnp.where(live, tops[head] + jnp.log(total), 0.0)


def cross_forward(low, high, places, queries, pieces):
    groups, slots, feats, rows_dev = queries.shape
    rows = groups * rows_dev
    tokens = pieces[0].shape[2] * len(pieces)
    row_block = pl.BlockSpec((groups, 1, feats, rows_dev), lambda s, *_: (0, s, 0, 0))
    return pl.pallas_call(
        cross_forward_kernel,
        grid_spec=pltpu.PrefetchScalarGridSpec(
            num_scalar_prefetch=3,
            grid=(slots,),
            in_specs=[row_block] + [pl.BlockSpec(memory_space=pl.ANY)] * len(pieces),
            out_specs=[
                pl.BlockSpec((1, feats, rows), lambda s, *_: (s, 0, 0)),
                row_block,
                pl.BlockSpec((1, GROUP_HEADS, rows), lambda s, *_: (s, 0, 0)),
            ],
            scratch_shapes=[
                pltpu.VMEM((feats, rows), f32),
                pltpu.VMEM((2, feats, tokens), half),
                pltpu.SemaphoreType.DMA((len(pieces),)),
            ],
        ),
        out_shape=[
            jax.ShapeDtypeStruct((slots, feats, rows), f32),
            jax.ShapeDtypeStruct(queries.shape, half),
            jax.ShapeDtypeStruct((slots, GROUP_HEADS, rows), f32),
        ],
        compiler_params=pltpu.CompilerParams(vmem_limit_bytes=vmem_bytes),
        name="cross_forward",
    )(low, high, places, queries, *pieces)


def cross_backward_kernel(
    low_ref, high_ref, place_ref, q_ref, g_ref, mix_ref, lse_ref, *rest
):
    count = place_ref.shape[0]
    spread = count // HEAD_GROUPS
    pieces = rest[:count]
    dq_ref, *dkv_outs = rest[-5 - spread : -4]
    dkv_ref, acc_ref, kv_ref, sems = rest[-4:]
    member = place_ref[0] % spread
    slot = pl.program_id(0)

    @pl.when(slot == 0)
    def _():
        dkv_ref[...] = jnp.zeros_like(dkv_ref)
        load_pieces(place_ref, pieces, kv_ref, sems)

    low, high = low_ref[slot], high_ref[slot]
    rows_dev = q_ref.shape[3]
    tiles_dev = dkv_ref.shape[4] // key_tile
    q_low = jnp.concatenate([q_ref[i, 0] for i in range(HEAD_GROUPS)], axis=1)
    q_low = q_low * jnp.asarray(score_scale, half)
    g_low = jnp.concatenate([g_ref[i, 0] for i in range(HEAD_GROUPS)], axis=1)
    rows = q_low.shape[1]
    acc_ref[...] = jnp.zeros_like(acc_ref)
    product = g_low.astype(f32) * mix_ref[0]
    delta = [jnp.sum(product[head_feats(h)], axis=0, keepdims=True) for h in range(GROUP_HEADS)]
    lse = [lse_ref[0, h : h + 1, :] for h in range(GROUP_HEADS)]

    def step(tile, carry):
        start = pl.multiple_of(tile * key_tile, key_tile)
        owner = tile // tiles_dev
        turn, group = (owner - member + spread) % spread, owner // spread
        inside = pl.multiple_of(tile % tiles_dev * key_tile, key_tile)
        key_pos = start + lax.broadcasted_iota(jnp.int32, (key_tile, rows), 0)
        counted = (key_pos >= low) & (key_pos < high)
        for head in range(GROUP_HEADS):
            feats = head_feats(head)
            k_low = kv_ref[0, feats, pl.ds(start, key_tile)]
            v_low = kv_ref[1, feats, pl.ds(start, key_tile)]
            scores = jnp.where(counted, dot_tn(k_low, q_low[feats]), masked_score)
            prob = jnp.exp(scores - lse[head])
            grad_prob = dot_tn(v_low, g_low[feats])
            grad_score = (prob * (grad_prob - delta[head])).astype(half)
            dkv_ref[turn, group, 1, feats, pl.ds(inside, key_tile)] += dot_nt(
                g_low[feats], prob.astype(half)
            ).astype(half)
            dkv_ref[turn, group, 0, feats, pl.ds(inside, key_tile)] += dot_nt(
                q_low[feats], grad_score
            ).astype(half)
            acc_ref[feats, :] += dot_nn(k_low, grad_score)
        return carry

    lax.fori_loop(*tiles_of(low, high), step, 0)
    dq_low = (acc_ref[...] * score_scale).astype(half)
    for i in range(HEAD_GROUPS):
        dq_ref[i, 0] = dq_low[:, i * rows_dev : (i + 1) * rows_dev]

    @pl.when(slot == pl.num_programs(0) - 1)
    def _():
        copies = [
            pltpu.make_async_copy(dkv_ref.at[turn], out, sems.at[turn])
            for turn, out in enumerate(dkv_outs)
        ]
        for copy in copies:
            copy.start()
        for copy in copies:
            copy.wait()


def cross_backward(low, high, places, queries, grad_mix, mix, lse, pieces, *after):
    groups, slots, feats, rows_dev = queries.shape
    rows = groups * rows_dev
    tokens = pieces[0].shape[2]
    row_block = pl.BlockSpec((groups, 1, feats, rows_dev), lambda s, *_: (0, s, 0, 0))
    grad_shape = (len(pieces) // groups, groups, 2, feats, tokens)
    return pl.pallas_call(
        cross_backward_kernel,
        grid_spec=pltpu.PrefetchScalarGridSpec(
            num_scalar_prefetch=3,
            grid=(slots,),
            in_specs=[
                row_block,
                row_block,
                pl.BlockSpec((1, feats, rows), lambda s, *_: (s, 0, 0)),
                pl.BlockSpec((1, GROUP_HEADS, rows), lambda s, *_: (s, 0, 0)),
            ]
            + [pl.BlockSpec(memory_space=pl.ANY)] * (len(pieces) + len(after)),
            out_specs=[row_block] + [pl.BlockSpec(memory_space=pl.ANY)] * grad_shape[0],
            scratch_shapes=[
                pltpu.VMEM(grad_shape, half),
                pltpu.VMEM((feats, rows), f32),
                pltpu.VMEM((2, feats, tokens * len(pieces)), half),
                pltpu.SemaphoreType.DMA((len(pieces),)),
            ],
        ),
        out_shape=[
            jax.ShapeDtypeStruct(queries.shape, half),
        ]
        + [jax.ShapeDtypeStruct(grad_shape[1:], half)] * grad_shape[0],
        compiler_params=pltpu.CompilerParams(vmem_limit_bytes=vmem_bytes),
        name="cross_backward",
    )(low, high, places, queries, grad_mix, mix, lse, *pieces, *after)


middle_rows = 256


def middle_kernel(
    n_doc,
    n_seq,
    att_ref,
    norm_ref,
    out_grad_ref,
    vec_ref,
    bias_ref,
    *rest,
):
    weights = rest[:-17]
    out_ref, resid_ref, send_ref, packed_ref, sums_ref, bias_grad_ref = rest[-17:-11]
    att_all, w_cross, w_in, w_out, norm_low, active = rest[-11:-5]
    slope, low_three, hidden_grad, low_two, sems = rest[-5:]
    slots, rows_dev = att_ref.shape[1], att_ref.shape[3]
    rows_total = slots * rows_dev
    rows = min(middle_rows, rows_total)
    ff = w_out.shape[0]
    chunk = ff // n_doc
    copies = []

    def copy_block(block, block_col, target, row, col):
        rows = pl.ds(block * block_rows, block_rows)
        copies.append(
            pltpu.make_async_copy(
                w_ref.at[rows, pl.ds(block_col * D, D)],
                target.at[pl.ds(row, block_rows), pl.ds(col, D)],
                sems.at[len(copies)],
            )
        )

    blocks = n_doc * n_seq
    block_rows = ff // blocks
    if len(weights) == 1:
        (w_ref,) = weights
        for band in range(blocks // 4):
            row = band * block_rows
            copy_block(4 * band, 1, w_cross, row, 0)
            for at, (block_col, block) in enumerate([(2, 0), (1, 1), (2, 1), (1, 2)]):
                copy_block(4 * band + block, block_col, w_in, row, at * D)
        for block in range(blocks):
            copy_block(block, 0, w_out, block * block_rows, 0)
    else:
        for i, (weight, target) in enumerate(zip(weights, (w_cross, w_in, w_out))):
            copies.append(pltpu.make_async_copy(weight, target, sems.at[i]))
    for copy in copies:
        copy.start()
    for group in range(HEAD_GROUPS):
        for slot in range(slots):
            att_all[
                group * GROUP_FEATS : (group + 1) * GROUP_FEATS,
                slot * rows_dev : (slot + 1) * rows_dev,
            ] = att_ref[group, slot]
    sums_ref[...] = jnp.zeros_like(sums_ref)
    bias_grad_ref[...] = jnp.zeros_like(bias_grad_ref)
    for copy in copies:
        copy.wait()

    def row_block(block, carry):
        where = pl.ds(pl.multiple_of(block * rows, rows), rows)
        gain_two, shift_two = vec_ref[0:1, :], vec_ref[1:2, :]
        gain_three, shift_three = vec_ref[2:3, :], vec_ref[3:4, :]
        branch = dot_tn(att_all[:, where], w_cross[...]) + vec_ref[4:5, :]
        unit_two, scale_two = normalize(norm_ref[where, :] + branch)
        norm_two = unit_two * gain_two + shift_two
        norm_two_low = norm_two.astype(half)
        norm_low[where, :] = norm_two_low
        branch = vec_ref[5:6, :]
        for z in range(n_doc):
            cols = slice(z * chunk, (z + 1) * chunk)
            hidden = dot_nn(norm_two_low, w_in[:, cols]) + bias_ref[:, cols]
            below = 0.5 + 0.5 * lax.erf(hidden * (0.5**0.5))
            density = jnp.exp(-0.5 * hidden * hidden) * 0.3989422804014327
            slope[:, cols] = below + hidden * density
            active_low = (hidden * below).astype(half)
            active[where, cols] = active_low
            branch = branch + dot_nn(active_low, w_out[cols, :])
        unit_three, scale_three = normalize(norm_two + branch)
        out_ref[where, :] = (unit_three * gain_three + shift_three).astype(half)
        incoming = out_grad_ref[where, :].astype(f32)
        sums_ref[2:3, :] += row_sum(incoming * unit_three)
        sums_ref[3:4, :] += row_sum(incoming)
        grad_three = norm_backward(incoming, gain_three, unit_three, scale_three)
        grad_low = grad_three.astype(half)
        low_three[where, :] = grad_low
        sums_ref[5:6, :] += row_sum(grad_low.astype(f32))
        incoming = grad_three
        for z in range(n_doc):
            cols = slice(z * chunk, (z + 1) * chunk)
            hidden_low = (dot_nt(grad_low, w_out[cols, :]) * slope[:, cols]).astype(half)
            hidden_grad[where, cols] = hidden_low
            bias_grad_ref[:, cols] += row_sum(hidden_low.astype(f32))
            incoming = incoming + dot_nt(hidden_low, w_in[:, cols])
        sums_ref[0:1, :] += row_sum(incoming * unit_two)
        sums_ref[1:2, :] += row_sum(incoming)
        grad_two = norm_backward(incoming, gain_two, unit_two, scale_two)
        resid_ref[where, :] = grad_two
        grad_low = grad_two.astype(half)
        low_two[where, :] = grad_low
        sums_ref[4:5, :] += row_sum(grad_low.astype(f32))
        return carry

    lax.fori_loop(0, rows_total // rows, row_block, 0)

    grad_att = dot_nt(w_cross[...], low_two[...]).astype(half)
    for group in range(HEAD_GROUPS):
        for slot in range(slots):
            send_ref[group, slot] = grad_att[
                group * GROUP_FEATS : (group + 1) * GROUP_FEATS,
                slot * rows_dev : (slot + 1) * rows_dev,
            ]

    share = D // (n_doc * n_seq)
    stack_n = chunk // (share * n_seq)

    store_rows(packed_ref, n_doc, dot_nn(att_all[...], low_two[...]), slice(2 * ff, 2 * ff + D))
    for z in range(n_doc):
        cols = slice(z * chunk, (z + 1) * chunk)
        grad = dot_tn(norm_low[...], hidden_grad[:, cols])
        store_rows(packed_ref, n_doc, grad, slice(ff + z * chunk, ff + (z + 1) * chunk))
    for pair in range(n_doc // 2):
        grads = []
        for z in (2 * pair, 2 * pair + 1):
            cols = slice(z * chunk, (z + 1) * chunk)
            grads.append(dot_tn(active[:, cols], low_three[...]))
        for s in range(n_seq):
            for q in range(stack_n):
                first = (s * stack_n + q) * share
                mine = [grad[first : first + share] for grad in grads]
                packed_ref[
                    s, pair * 2 * share : (pair + 1) * 2 * share, q * D : (q + 1) * D
                ] = jnp.concatenate(mine, axis=0).astype(half)


def middle(n_doc, n_seq, att, norm_one, out_grad, vectors, bias, weights):
    groups, slots, feats, rows_dev = att.shape
    rows_total = slots * rows_dev
    ff = weights[-1].shape[0]
    share = D // (n_doc * n_seq)
    vmem = pl.BlockSpec(memory_space=pltpu.VMEM)
    hbm = pl.BlockSpec(memory_space=pl.ANY)
    return pl.pallas_call(
        partial(middle_kernel, n_doc, n_seq),
        in_specs=[vmem] * 5 + [hbm] * len(weights),
        out_specs=[vmem] * 6,
        out_shape=[
            jax.ShapeDtypeStruct((rows_total, D), half),
            jax.ShapeDtypeStruct((rows_total, D), f32),
            jax.ShapeDtypeStruct(att.shape, half),
            jax.ShapeDtypeStruct((n_seq, n_doc * share, 2 * ff + D), half),
            jax.ShapeDtypeStruct((8, D), f32),
            jax.ShapeDtypeStruct((1, ff), f32),
        ],
        scratch_shapes=[
            pltpu.VMEM((D, rows_total), half),
            pltpu.VMEM((D, D), half),
            pltpu.VMEM((D, ff), half),
            pltpu.VMEM((ff, D), half),
            pltpu.VMEM((rows_total, D), half),
            pltpu.VMEM((rows_total, ff), half),
            pltpu.VMEM((min(middle_rows, rows_total), ff), f32),
            pltpu.VMEM((rows_total, D), half),
            pltpu.VMEM((rows_total, ff), half),
            pltpu.VMEM((rows_total, D), half),
            pltpu.SemaphoreType.DMA((n_doc * n_seq * 9 // 4,)),
        ],
        compiler_params=pltpu.CompilerParams(vmem_limit_bytes=vmem_bytes),
        name="middle",
    )(att, norm_one, out_grad, vectors, bias, *weights)


def body(
    n_doc,
    n_seq,
    dec_input,
    memory,
    doc_lengths,
    doc_count,
    self_qkv,
    self_out,
    cross_q,
    cross_kv,
    cross_out,
    ffn_in,
    ffn_in_bias,
    ffn_out,
    norm_gains,
    biases,
    out_grad,
):
    seq_index = lax.axis_index("seq")
    doc_index = lax.axis_index("doc")
    slots_n, rows_dev = dec_input.shape[1:3]
    rows_total = slots_n * rows_dev
    mem_rows = memory.shape[1]
    spread = n_seq // HEAD_GROUPS
    head_group = seq_index // spread
    member = seq_index % spread
    member_slots = slots_n // spread
    dec_len = rows_dev * n_seq
    same_member = [[h * spread + m for h in range(HEAD_GROUPS)] for m in range(spread)]

    def swap_heads(blocks):
        return lax.all_to_all(blocks, "seq", 0, 0, axis_index_groups=same_member, tiled=True)

    def rotate_both(block, turn_h, turn_m):
        if turn_h == turn_m == 0:
            return block
        return lax.ppermute(
            block,
            "seq",
            [
                (
                    h * spread + m,
                    (h + turn_h) % HEAD_GROUPS * spread + (m + turn_m) % spread,
                )
                for h in range(HEAD_GROUPS)
                for m in range(spread)
            ],
        )

    def rotate_heads(block, turn):
        return rotate_both(block, turn, 0)

    def rotate_members(block, turn):
        return rotate_both(block, 0, turn)

    def rotate_doc(block, turn):
        return lax.ppermute(block, "doc", [(d, (d + turn) % n_doc) for d in range(n_doc)])

    def in_order(pieces, own, axis):
        count = len(pieces)
        shape = pieces[0].shape
        whole = jnp.zeros(shape[:axis] + (count,) + shape[axis:], pieces[0].dtype)
        for turn, piece in enumerate(pieces):
            whole = lax.dynamic_update_index_in_dim(whole, piece, (own - turn) % count, axis)
        return whole

    def send_turns(blocks, axis, count, own, rotate):
        got = []
        for turn in range(count):
            block = lax.dynamic_index_in_dim(blocks, (own + turn) % count, axis, keepdims=False)
            got.append(rotate(block, turn) if turn else block)
        return got

    part = self_qkv.shape[0]
    width = 3 * GROUP_FEATS
    qkv_piece = jnp.concatenate(
        [
            lax.dynamic_slice_in_dim(
                self_qkv, block * D + head_group * GROUP_FEATS, GROUP_FEATS, 1
            )
            for block in range(3)
        ],
        axis=1,
    )
    small = jnp.concatenate([norm_gains, biases, ffn_in_bias.reshape(-1, part)], axis=0)
    small_rows = small.shape[0]
    first_width = width
    pad_rows = -(-small_rows * part // first_width)
    first_rows = -(-(part + pad_rows) // (8 * spread)) * 8 * spread
    pad_rows = first_rows - part
    small = jnp.pad(small.reshape(-1), (0, pad_rows * first_width - small_rows * part))
    first_piece = jnp.concatenate(
        [qkv_piece, small.reshape(pad_rows, width)], axis=0
    )
    first_piece = lax.dynamic_slice_in_dim(
        first_piece.astype(half), member * (first_rows // spread), first_rows // spread, 0
    )

    def join_members(mine):
        pieces = [mine] + [rotate_members(mine, turn) for turn in range(1, spread)]
        return in_order(pieces, member, 1).reshape(n_doc, -1, mine.shape[2])

    first_piece = jnp.broadcast_to(first_piece[None], (n_doc,) + first_piece.shape)
    first_gather = join_members(lax.all_to_all(first_piece, "doc", 0, 0, tiled=True))
    w_qkv_part = first_gather[:, :part].reshape(D, width)
    small = first_gather[:, part:].reshape(n_doc, -1)[:, : small_rows * part]
    small = small.reshape(n_doc, small_rows, part).astype(f32)
    gains_f = small[:, :3].transpose(1, 0, 2).reshape(3, D)
    biases_f = small[:, 3:13].transpose(1, 0, 2).reshape(10, D)
    b_ffn_in = small[:, 13:].reshape(1, -1)

    share = part // n_seq
    ff = ffn_in.shape[1]
    stack_n = ffn_out.shape[0] // part
    member_rows = part // spread

    def gather_halves(*weights):
        piece = [
            lax.dynamic_slice_in_dim(weight, member * member_rows, member_rows, 0).astype(half)
            for weight in weights
        ]
        return lax.all_gather(jnp.concatenate(piece, axis=1), "doc", axis=0)

    w_cross_kv = join_members(gather_halves(cross_kv)).reshape(D, 2 * D)
    pair_halves = gather_halves(self_out, cross_q)

    block_rows, block_cols = divmod(seq_index, 4)

    def column_block(weight, first):
        return lax.dynamic_slice(
            weight, (block_rows * member_rows, first), (member_rows, D)
        ).astype(half)

    def first_cols(*starts):
        return jnp.stack(starts)[block_cols]

    left = jnp.where(
        block_cols == 0,
        column_block(cross_out, 0),
        jnp.where(
            block_cols == 3,
            column_block(self_qkv, D),
            column_block(ffn_in, first_cols(0, D, 3 * D, 0)),
        ),
    )
    right = jnp.where(
        block_cols < 2,
        column_block(ffn_in, first_cols(0, 2 * D, 0, 0)),
        column_block(self_qkv, first_cols(0, 0, 0, 2 * D)),
    )
    down = lax.dynamic_slice_in_dim(ffn_out, seq_index * member_rows, member_rows, 0).astype(half)
    w_blocks = lax.all_gather(
        jnp.concatenate([down, left, right], axis=1), ("doc", "seq"), axis=0, tiled=True
    )
    by_block = w_blocks.reshape(n_doc, spread, 4, member_rows, 3 * D)

    def columns(*blocks):
        found = [by_block[:, :, c, :, third * D : (third + 1) * D] for c, third in blocks]
        return jnp.concatenate(found, axis=3).reshape(D, -1)

    late_weights = [w_blocks]
    if member_rows % 16:
        late_weights = [
            columns((0, 1)),
            columns((0, 2), (1, 1), (1, 2), (2, 1)),
            w_blocks[:, :D],
        ]

    mem_low = memory[0]
    kv_bias = jnp.concatenate([jnp.zeros((D,), f32), biases_f[4]])
    mem_kv = (dot_tt(w_cross_kv, mem_low) + kv_bias[:, None]).astype(half)
    mem_kv = mem_kv.reshape(2, HEAD_GROUPS, GROUP_FEATS, mem_rows)
    pieces = send_turns(mem_kv, 1, HEAD_GROUPS, head_group, rotate_heads)
    pieces = pieces + [
        rotate_members(piece, turn) for turn in range(1, spread) for piece in pieces
    ]

    x_low = dec_input[0].reshape(rows_total, D)
    places = jnp.stack(
        [
            (head_group - turn_h) % HEAD_GROUPS * spread + (member - turn_m) % spread
            for turn_m in range(spread)
            for turn_h in range(HEAD_GROUPS)
        ]
    ).astype(jnp.int32)
    x_pieces = [rotate_heads(dec_input[0], turn) if turn else dec_input[0] for turn in range(HEAD_GROUPS)]
    for turn in range(1, spread):
        first_slot = (member + turn) % spread * member_slots
        blocks = [
            lax.dynamic_slice_in_dim(piece, first_slot, member_slots, 0)
            for piece in x_pieces[:HEAD_GROUPS]
        ]
        x_pieces.append(rotate_members(jnp.stack(blocks), turn))
    group_places = ((head_group - jnp.arange(HEAD_GROUPS)) % HEAD_GROUPS).astype(jnp.int32)
    zero_part = jnp.zeros((GROUP_FEATS,), f32)
    b_query = lax.dynamic_slice_in_dim(biases_f[0], head_group * GROUP_FEATS, GROUP_FEATS)
    b_value = lax.dynamic_slice_in_dim(biases_f[1], head_group * GROUP_FEATS, GROUP_FEATS)
    b_proj = jnp.concatenate([b_query, zero_part, b_value])[None]
    proj, self_mix, self_att_send, self_lse = self_forward(
        places, w_qkv_part, b_proj, x_pieces, n_seq, pieces[0]
    )

    def from_heads(blocks):
        feats = blocks.shape[2]
        got = blocks.reshape(HEAD_GROUPS, slots_n, feats // GROUP_FEATS, GROUP_FEATS, rows_dev)
        return got.transpose(2, 0, 3, 1, 4).reshape(HEAD_GROUPS * feats, rows_total)

    self_att = lax.all_to_all(self_att_send, "seq", 0, 0, tiled=True)
    pair_halves = lax.optimization_barrier((pair_halves, self_att_send))[0]
    w_pair = join_members(pair_halves).reshape(D, 2 * D)
    first_vectors = jnp.stack([biases_f[2], gains_f[0], biases_f[7], biases_f[3]])
    first_vectors = jnp.pad(first_vectors, ((0, 4), (0, 0)))
    norm_one, unit_one, scale_one, query_send = enter(
        self_att, x_low, first_vectors, w_pair, slots_n
    )

    lengths = doc_lengths[0]
    live_len = jnp.where(jnp.arange(slots_n) < doc_count[0], lengths, 0)
    key_high = jnp.minimum(jnp.cumsum(live_len), n_seq * mem_rows).astype(jnp.int32)
    key_low = jnp.concatenate([jnp.zeros((1,), jnp.int32), key_high[:-1]])
    query_part = swap_heads(query_send)
    cross_mix, cross_att_send, cross_lse = cross_forward(
        key_low, key_high, places, query_part, pieces
    )
    vectors = jnp.stack(
        [gains_f[1], biases_f[8], gains_f[2], biases_f[9], biases_f[5], biases_f[6]]
    )
    layer_out, grad_r2, grad_mix_send, late_packed, late_rows, grad_b_in = middle(
        n_doc,
        n_seq,
        swap_heads(cross_att_send),
        norm_one,
        out_grad[0].reshape(rows_total, D),
        jnp.pad(vectors, ((0, 2), (0, 0))),
        b_ffn_in,
        late_weights,
    )
    layer_out = layer_out.reshape(dec_input.shape)
    grad_g1, grad_c8, grad_g2, grad_c9, grad_b5, grad_b6 = late_rows[:6]

    def sum_over_seq(packed):
        packed = packed.reshape(D, packed.shape[2])
        return lax.psum_scatter(packed, "seq", scatter_dimension=0, tiled=True)

    def own_rows(packed):
        blocks = packed.reshape(n_doc, share, -1)
        pieces = send_turns(blocks, 0, n_doc, doc_index, rotate_doc)
        return sum(piece.astype(f32) for piece in pieces).astype(half)

    late_blocks = sum_over_seq(late_packed)
    grad_query_send, *grad_kv = cross_backward(
        key_low,
        key_high,
        places,
        query_part,
        swap_heads(grad_mix_send),
        cross_mix,
        cross_lse,
        pieces,
        late_packed,
    )
    grad_kv = [grad_kv[0]] + [
        rotate_members(grad_kv[turn], turn) for turn in range(1, spread)
    ]
    grad_kv_own = []
    for turn in range(HEAD_GROUPS):
        group = (head_group + turn) % HEAD_GROUPS
        total = sum(
            lax.dynamic_index_in_dim(piece, group, 0, keepdims=False).astype(f32)
            for piece in grad_kv
        ).astype(half)
        grad_kv_own.append(rotate_heads(total, turn) if turn else total)
    grad_r1, grad_att_send, pair_packed, first_rows_grad = leave(
        n_doc,
        swap_heads(grad_query_send),
        self_att,
        grad_r2,
        norm_one,
        unit_one,
        scale_one,
        first_vectors,
        w_pair,
        grad_kv_own[0],
    )
    pair_over_seq = sum_over_seq(pair_packed)
    grad_self_part = lax.all_to_all(grad_att_send, "seq", 0, 0, tiled=True)
    late_own = own_rows(lax.optimization_barrier((late_blocks, grad_r1))[0])
    mem_packed, grad_mem_kv = memory_backward(
        n_doc,
        n_seq,
        group_places,
        mem_low,
        first_rows_grad,
        late_rows,
        grad_b_in.reshape(n_doc, -1, part).transpose(1, 0, 2).reshape(-1, D),
        grad_kv_own,
        grad_self_part,
        late_blocks,
    )
    grad_proj_send, grad_part, part_sums = self_backward(
        n_doc,
        places,
        proj,
        grad_self_part,
        self_mix,
        self_lse,
        x_pieces,
        mem_packed,
        late_own,
    )
    grad_proj_got = lax.all_to_all(grad_proj_send, "seq", 0, 0, tiled=True)

    bias_rows = jnp.zeros((2, D), f32)
    bias_rows = lax.dynamic_update_slice(
        bias_rows,
        jnp.stack([part_sums[0, :GROUP_FEATS], part_sums[0, 2 * GROUP_FEATS :]]),
        (0, head_group * GROUP_FEATS),
    )
    lanes = -(-part // small_cols) * small_cols
    bias_rows = jnp.pad(bias_rows.reshape(2, n_doc, part), ((0, 0), (0, 0), (0, lanes - part)))
    bias_rows = bias_rows.transpose(1, 0, 2).reshape(n_doc, -1, small_cols)
    bias_used = bias_rows.shape[1]
    bias_rows = jnp.pad(bias_rows, ((0, 0), (0, share - bias_used), (0, 0)))
    bias_rows = bias_rows.reshape(1, n_doc * share, small_cols).astype(half)
    bias_rows = jnp.pad(bias_rows, ((0, spread - 1), (0, 0), (0, 0)))
    grad_part = jnp.concatenate([grad_part, bias_rows], axis=2)
    grad_part = send_turns(grad_part, 0, spread, member, rotate_members)
    grad_part = sum(piece.astype(f32) for piece in grad_part).astype(half)

    pair_own = own_rows(pair_over_seq)
    grads = jnp.concatenate([sum_over_seq(mem_packed), grad_part], axis=1)
    grads, grad_proj_got = lax.optimization_barrier((grads, grad_proj_got))
    (
        grad_w_qkv,
        grad_w_self_out,
        grad_w_cross_q,
        grad_w_cross_kv,
        small_grad,
        bias_sums,
        grad_w_down,
        grad_w_in,
        grad_w_cross_out,
    ) = finish(
        n_seq,
        stack_n,
        lax.all_gather(
            jnp.concatenate([pair_own, own_rows(grads), late_own], axis=1), "seq", axis=0, tiled=True
        ),
    )
    grad_proj = from_heads(grad_proj_got)
    memory_grad = dot_tt(grad_mem_kv, w_cross_kv)[None]
    w_qkv = columns((2, 2), (3, 1), (3, 2))
    input_grad = (grad_r1 + dot_tt(grad_proj, w_qkv)).reshape(dec_input.shape)
    grad_g0, grad_c7, grad_b2, grad_b3 = small_grad[:4]
    grad_g1, grad_c8, grad_g2, grad_c9, grad_b5, grad_b6 = small_grad[8:14]
    grad_b0, grad_b1 = bias_sums[:bias_used].reshape(2, lanes)[:, :part]
    grad_b4 = small_grad[16 + stack_n]
    return (
        layer_out,
        input_grad,
        memory_grad,
        grad_w_qkv,
        grad_w_self_out,
        grad_w_cross_q,
        grad_w_cross_kv,
        grad_w_cross_out,
        grad_w_in,
        small_grad[16 : 16 + stack_n].reshape(-1),
        grad_w_down,
        jnp.stack([grad_g0, grad_g1, grad_g2]),
        jnp.stack(
            [grad_b0, grad_b1, grad_b2, grad_b3, grad_b4, grad_b5, grad_b6]
            + [grad_c7, grad_c8, grad_c9]
        ),
    )


def solution(mesh):
    placed = (
        P("doc", None, "seq", None),
        P("doc", "seq", None),
        P("doc", None),
        P("doc"),
        P("doc", None),
        P("doc", None),
        P("doc", None),
        P("doc", None),
        P("doc", None),
        P("doc", None),
        P("doc"),
        P("doc", None),
        P(None, "doc"),
        P(None, "doc"),
        P("doc", None, "seq", None),
    )
    return jax.shard_map(
        partial(body, mesh.shape["doc"], mesh.shape["seq"]),
        mesh=mesh,
        in_specs=placed,
        out_specs=(
            P("doc", None, "seq", None),
            P("doc", None, "seq", None),
            P("doc", "seq", None),
            P("doc", None),
            P("doc", None),
            P("doc", None),
            P("doc", None),
            P("doc", None),
            P("doc", None),
            P("doc"),
            P("doc", None),
            P(None, "doc"),
            P(None, "doc"),
        ),
        check_vma=False,
    )
```

```python
from functools import partial

import jax
import jax.numpy as jnp
from jax import lax
from jax.experimental import pallas as pl
from jax.experimental.pallas import tpu as pltpu
from jax.sharding import PartitionSpec as P

D = 768
HEADS = 12
HEAD_DIM = 64
HEAD_GROUPS = 4
GROUP_HEADS = HEADS // HEAD_GROUPS
GROUP_FEATS = GROUP_HEADS * HEAD_DIM

norm_eps = 1e-05
masked_score = -2e30
start_max = -1e30
score_scale = HEAD_DIM ** (-0.5)
key_tile = 256
row_tile = 256
vmem_bytes = 56 * 2**20

f32 = jnp.float32
half = jnp.bfloat16


def cost_of(micros):
    return pl.CostEstimate(flops=micros * 10**9, bytes_accessed=micros * 10**6, transcendentals=0)


def layer_norm(resid_in, gain_row, shift_row):
    center = resid_in - jnp.mean(resid_in, axis=-1, keepdims=True)
    variance = jnp.mean(center * center, axis=-1, keepdims=True)
    return center * lax.rsqrt(variance + norm_eps) * gain_row + shift_row


def contract(left_op, right_op, left_dim, right_dim):
    return lax.dot_general(
        left_op,
        right_op,
        (((left_dim,), (right_dim,)), ((), ())),
        preferred_element_type=f32,
    )


def dot_nn(left_op, right_op):
    return contract(left_op, right_op, 1, 0)


def dot_nt(left_op, right_op):
    return contract(left_op, right_op, 1, 1)


def dot_tn(left_op, right_op):
    return contract(left_op, right_op, 0, 0)


def dot_tt(left_op, right_op):
    return contract(left_op, right_op, 0, 1)


def col_sums(grad_low):
    return jnp.sum(grad_low.astype(f32), axis=0)


def normalize(resid):
    center = resid - jnp.mean(resid, axis=-1, keepdims=True)
    scale = lax.rsqrt(jnp.mean(center * center, axis=-1, keepdims=True) + norm_eps)
    return center * scale, scale


def norm_backward(incoming, gain_row, unit, scale):
    grad = incoming * gain_row
    mean_one = jnp.mean(grad, axis=-1, keepdims=True)
    mean_two = jnp.mean(grad * unit, axis=-1, keepdims=True)
    return (grad - mean_one - unit * mean_two) * scale


def row_sum(grad):
    return jnp.sum(grad, axis=0, keepdims=True)


def store_rows(packed_ref, n_doc, grad, cols):
    n_seq, rows = packed_ref.shape[:2]
    share = rows // n_doc
    for s in range(n_seq):
        mine = [grad[(z * n_seq + s) * share : (z * n_seq + s + 1) * share] for z in range(n_doc)]
        packed_ref[s, :, cols] = jnp.concatenate(mine, axis=0).astype(half)


def head_feats(head, block=0):
    start = block * GROUP_FEATS + head * HEAD_DIM
    return slice(start, start + HEAD_DIM)


def load_rows(place_ref, piece_refs, x_ref, sems):
    spread = place_ref.shape[0] // HEAD_GROUPS
    slots = x_ref.shape[0]
    rows_dev = x_ref.shape[1] // place_ref.shape[0]
    member = place_ref[0] % spread
    copies = []
    for i in range(place_ref.shape[0]):
        turn_m, turn_h = i // HEAD_GROUPS, i % HEAD_GROUPS
        if turn_m:
            piece = piece_refs[HEAD_GROUPS + turn_m - 1].at[turn_h]
        else:
            piece = piece_refs[turn_h].at[pl.ds(member * slots, slots)]
        first = pl.multiple_of(place_ref[i] * rows_dev, rows_dev)
        copies.append(
            pltpu.make_async_copy(piece, x_ref.at[:, pl.ds(first, rows_dev)], sems.at[i])
        )
    for copy in copies:
        copy.start()
    for copy in copies:
        copy.wait()


def self_forward_kernel(place_ref, w_ref, bias_ref, *rest):
    pieces, (proj_ref, mix_ref, att_ref, lse_ref, x_ref, sems) = rest[:-6], rest[-6:]
    slot = pl.program_id(0)

    @pl.when(slot == 0)
    def _():
        load_rows(place_ref, pieces, x_ref, sems)

    length = proj_ref.shape[1]
    rows_dev = att_ref.shape[3]
    rows = min(row_tile, length)
    for first in range(0, length, rows):
        part = dot_nn(x_ref[slot, first : first + rows, :], w_ref[...]) + bias_ref[0:1, :]
        proj_ref[:, first : first + rows] = part.astype(half).T
    for head in range(GROUP_HEADS):
        feats = head_feats(head)
        for first in range(0, length, rows):
            upto = first + rows
            cols = slice(first, upto)
            q_low = proj_ref[feats, cols] * jnp.asarray(score_scale, half)
            k_low = proj_ref[head_feats(head, 1), :upto]
            v_low = proj_ref[head_feats(head, 2), :upto]
            scores = dot_tn(k_low, q_low)
            key_pos = lax.broadcasted_iota(jnp.int32, scores.shape, 0)
            row_pos = first + lax.broadcasted_iota(jnp.int32, scores.shape, 1)
            scores = jnp.where(key_pos <= row_pos, scores, masked_score)
            top = jnp.max(scores, axis=0, keepdims=True)
            weight = jnp.exp(scores - top)
            total = jnp.sum(weight, axis=0, keepdims=True)
            mix = dot_nn(v_low, weight.astype(half)) / total
            mix_ref[0, feats, cols] = mix
            mix_low = mix.astype(half)
            for place in range(rows // rows_dev):
                att_ref[first // rows_dev + place, 0, feats, :] = mix_low[
                    :, place * rows_dev : (place + 1) * rows_dev
                ]
            lse_ref[0, head : head + 1, cols] = top + jnp.log(total)


def self_forward(places, w_part, bias, pieces, n_seq, *after):
    slots = pieces[0].shape[0] * HEAD_GROUPS // n_seq
    length = pieces[0].shape[1] * n_seq
    feats, rows_dev = w_part.shape[1], length // n_seq
    return pl.pallas_call(
        self_forward_kernel,
        grid_spec=pltpu.PrefetchScalarGridSpec(
            num_scalar_prefetch=1,
            grid=(slots,),
            in_specs=[
                pl.BlockSpec(w_part.shape, lambda s, *_: (0, 0)),
                pl.BlockSpec(bias.shape, lambda s, *_: (0, 0)),
            ]
            + [pl.BlockSpec(memory_space=pl.ANY)] * (len(pieces) + len(after)),
            out_specs=[
                pl.BlockSpec((feats, length), lambda s, *_: (0, s)),
                pl.BlockSpec((1, GROUP_FEATS, length), lambda s, *_: (s, 0, 0)),
                pl.BlockSpec((n_seq, 1, GROUP_FEATS, rows_dev), lambda s, *_: (0, s, 0, 0)),
                pl.BlockSpec((1, GROUP_HEADS, length), lambda s, *_: (s, 0, 0)),
            ],
            scratch_shapes=[
                pltpu.VMEM((slots, length, D), half),
                pltpu.SemaphoreType.DMA((n_seq,)),
            ],
        ),
        out_shape=[
            jax.ShapeDtypeStruct((feats, slots * length), half),
            jax.ShapeDtypeStruct((slots, GROUP_FEATS, length), f32),
            jax.ShapeDtypeStruct((n_seq, slots, GROUP_FEATS, rows_dev), half),
            jax.ShapeDtypeStruct((slots, GROUP_HEADS, length), f32),
        ],
        compiler_params=pltpu.CompilerParams(vmem_limit_bytes=vmem_bytes),
        cost_estimate=cost_of(18),
        name="self_forward",
    )(places, w_part, bias, *pieces, *after)


def self_backward_kernel(n_doc, place_ref, proj_ref, grad_ref, mix_ref, lse_ref, *rest):
    ins, (send_ref, w_grad_ref, sums_ref, dproj_ref, dk_ref, dv_ref, w_acc, x_ref, sems) = (
        rest[:-9],
        rest[-9:],
    )
    pieces = ins[: HEAD_GROUPS + place_ref.shape[0] // HEAD_GROUPS - 1]
    slot = pl.program_id(0)

    @pl.when(slot == 0)
    def _():
        load_rows(place_ref, pieces, x_ref, sems)
        w_acc[...] = jnp.zeros_like(w_acc)
        sums_ref[...] = jnp.zeros_like(sums_ref)

    length = proj_ref.shape[1]
    n_seq, rows_dev = grad_ref.shape[0], grad_ref.shape[3]
    rows = min(row_tile, length)
    dk_ref[...] = jnp.zeros_like(dk_ref)
    dv_ref[...] = jnp.zeros_like(dv_ref)
    for head in range(GROUP_HEADS):
        feats = head_feats(head)
        for first in range(0, length, rows):
            upto = first + rows
            cols = slice(first, upto)
            places = range(first // rows_dev, upto // rows_dev)
            q_low = proj_ref[feats, cols] * jnp.asarray(score_scale, half)
            k_low = proj_ref[head_feats(head, 1), :upto]
            v_low = proj_ref[head_feats(head, 2), :upto]
            g_low = jnp.concatenate([grad_ref[place, 0, feats, :] for place in places], axis=1)
            delta = jnp.sum(g_low.astype(f32) * mix_ref[0, feats, cols], axis=0, keepdims=True)
            scores = dot_tn(k_low, q_low)
            key_pos = lax.broadcasted_iota(jnp.int32, scores.shape, 0)
            row_pos = first + lax.broadcasted_iota(jnp.int32, scores.shape, 1)
            scores = jnp.where(key_pos <= row_pos, scores, masked_score)
            prob = jnp.exp(scores - lse_ref[0, head : head + 1, cols])
            grad_prob = dot_tn(v_low, g_low)
            grad_score = (prob * (grad_prob - delta)).astype(half)
            dv_ref[feats, :upto] += dot_nt(g_low, prob.astype(half))
            dk_ref[feats, :upto] += dot_nt(q_low, grad_score)
            dproj_ref[feats, cols] = (dot_nn(k_low, grad_score) * score_scale).astype(half)
    dproj_ref[GROUP_FEATS : 2 * GROUP_FEATS, :] = dk_ref[...].astype(half)
    dproj_ref[2 * GROUP_FEATS :, :] = dv_ref[...].astype(half)
    for place in range(n_seq):
        send_ref[place, 0] = dproj_ref[:, place * rows_dev : (place + 1) * rows_dev]
    for first in range(0, length, rows):
        turned = dproj_ref[:, first : first + rows].T
        sums_ref[0:1, :] += row_sum(turned.astype(f32))
        w_acc[...] += dot_tn(x_ref[slot, first : first + rows, :], turned)

    @pl.when(slot == pl.num_programs(0) - 1)
    def _():
        spread, stored, width = w_grad_ref.shape
        share = stored // n_doc
        feats = dproj_ref.shape[0]
        quarters = width // feats
        for m in range(spread):
            for q in range(quarters):
                mine = []
                for z in range(n_doc):
                    first = ((z * spread + m) * quarters + q) * share
                    mine.append(w_acc[first : first + share, :])
                w_grad_ref[m, :, q * feats : (q + 1) * feats] = jnp.concatenate(
                    mine, axis=0
                ).astype(half)


def self_backward(n_doc, places, proj, grad_mix, mix, lse, pieces, *after):
    n_seq, slots, _, rows_dev = grad_mix.shape
    feats, length = proj.shape[0], n_seq * rows_dev
    spread = n_seq // HEAD_GROUPS
    stored = D // n_seq
    return pl.pallas_call(
        partial(self_backward_kernel, n_doc),
        grid_spec=pltpu.PrefetchScalarGridSpec(
            num_scalar_prefetch=1,
            grid=(slots,),
            in_specs=[
                pl.BlockSpec((feats, length), lambda s, *_: (0, s)),
                pl.BlockSpec((n_seq, 1, GROUP_FEATS, rows_dev), lambda s, *_: (0, s, 0, 0)),
                pl.BlockSpec((1, GROUP_FEATS, length), lambda s, *_: (s, 0, 0)),
                pl.BlockSpec((1, GROUP_HEADS, length), lambda s, *_: (s, 0, 0)),
            ]
            + [pl.BlockSpec(memory_space=pl.ANY)] * (len(pieces) + len(after)),
            out_specs=[
                pl.BlockSpec((n_seq, 1, feats, rows_dev), lambda s, *_: (0, s, 0, 0)),
                pl.BlockSpec((spread, stored, HEAD_GROUPS * feats), lambda s, *_: (0, 0, 0)),
                pl.BlockSpec((8, feats), lambda s, *_: (0, 0)),
            ],
            scratch_shapes=[
                pltpu.VMEM((feats, length), half),
                pltpu.VMEM((GROUP_FEATS, length), f32),
                pltpu.VMEM((GROUP_FEATS, length), f32),
                pltpu.VMEM((D, feats), f32),
                pltpu.VMEM((slots, length, D), half),
                pltpu.SemaphoreType.DMA((n_seq,)),
            ],
        ),
        out_shape=[
            jax.ShapeDtypeStruct((n_seq, slots, feats, rows_dev), half),
            jax.ShapeDtypeStruct((spread, stored, HEAD_GROUPS * feats), half),
            jax.ShapeDtypeStruct((8, feats), f32),
        ],
        compiler_params=pltpu.CompilerParams(vmem_limit_bytes=vmem_bytes),
        cost_estimate=cost_of(20),
        name="self_backward",
    )(places, proj, grad_mix, mix, lse, *pieces, *after)


def enter_kernel(att_ref, x_ref, vec_ref, w_ref, norm_ref, unit_ref, scale_ref, send_ref, att_all):
    gather_att(att_ref, att_all)
    slots, rows_dev = send_ref.shape[1], send_ref.shape[3]
    rows = min(middle_rows, x_ref.shape[0])
    for first in range(0, x_ref.shape[0], rows):
        where = slice(first, first + rows)
        branch = dot_tn(att_all[:, where], w_ref[:, :D]) + vec_ref[0:1, :]
        unit, scale = normalize(x_ref[where, :].astype(f32) + branch)
        norm = unit * vec_ref[1:2, :] + vec_ref[2:3, :]
        norm_ref[where, :] = norm
        unit_ref[where, :] = unit
        scale_ref[where, :] = jnp.broadcast_to(scale, (rows, scale_ref.shape[1]))
        query = dot_nn(norm.astype(half), w_ref[:, D:]) + vec_ref[3:4, :]
        query = query.astype(half).T
        for group in range(HEAD_GROUPS):
            for place in range(rows // rows_dev):
                send_ref[group, first // rows_dev + place] = query[
                    group * GROUP_FEATS : (group + 1) * GROUP_FEATS,
                    place * rows_dev : (place + 1) * rows_dev,
                ]


def gather_att(att_ref, att_all):
    n_seq, member_slots, _, rows_dev = att_ref.shape
    spread = n_seq // HEAD_GROUPS
    for source in range(n_seq):
        group, m = source // spread, source % spread
        for inner in range(member_slots):
            slot = m * member_slots + inner
            att_all[
                group * GROUP_FEATS : (group + 1) * GROUP_FEATS,
                slot * rows_dev : (slot + 1) * rows_dev,
            ] = att_ref[source, inner]


def enter(att, x_low, vectors, w_pair, slots):
    rows_total, rows_dev = x_low.shape[0], att.shape[3]
    vmem = pl.BlockSpec(memory_space=pltpu.VMEM)
    return pl.pallas_call(
        enter_kernel,
        in_specs=[vmem] * 4,
        out_specs=[vmem] * 4,
        out_shape=[
            jax.ShapeDtypeStruct((rows_total, D), f32),
            jax.ShapeDtypeStruct((rows_total, D), f32),
            jax.ShapeDtypeStruct((rows_total, 128), f32),
            jax.ShapeDtypeStruct((HEAD_GROUPS, slots, GROUP_FEATS, rows_dev), half),
        ],
        scratch_shapes=[pltpu.VMEM((D, rows_total), half)],
        compiler_params=pltpu.CompilerParams(vmem_limit_bytes=vmem_bytes),
        cost_estimate=cost_of(6),
        name="enter",
    )(att, x_low, vectors, w_pair)


def leave_kernel(
    n_doc,
    query_ref,
    att_ref,
    resid_ref,
    norm_ref,
    unit_ref,
    scale_ref,
    vec_ref,
    w_ref,
    mem_ref,
    rows_a_ref,
    rows_b_ref,
    rows_c_ref,
    out_ref,
    send_ref,
    packed_ref,
    att_all,
    query_all,
    query_rows,
    low_rows,
    sums_ref,
):
    slots, rows_dev = query_ref.shape[1], query_ref.shape[3]
    member_slots = att_ref.shape[1]
    spread = slots // member_slots
    rows_total = resid_ref.shape[0]
    rows = min(middle_rows, rows_total)
    gather_att(att_ref, att_all)
    for group in range(HEAD_GROUPS):
        for slot in range(slots):
            query_all[
                group * GROUP_FEATS : (group + 1) * GROUP_FEATS,
                slot * rows_dev : (slot + 1) * rows_dev,
            ] = query_ref[group, slot]
    sums_ref[...] = jnp.zeros_like(sums_ref)
    for first in range(0, rows_total, rows):
        where = slice(first, first + rows)
        query = query_all[:, where].T
        query_rows[where, :] = query
        sums_ref[3:4, :] += row_sum(query.astype(f32))
        incoming = resid_ref[where, :] + dot_nt(query, w_ref[:, D:])
        unit = unit_ref[where, :]
        sums_ref[0:1, :] += row_sum(incoming * unit)
        sums_ref[1:2, :] += row_sum(incoming)
        grad = norm_backward(incoming, vec_ref[1:2, :], unit, scale_ref[where, 0:1])
        out_ref[where, :] = grad
        grad_low = grad.astype(half)
        low_rows[where, :] = grad_low
        sums_ref[2:3, :] += row_sum(grad_low.astype(f32))
    grad_att = dot_nt(w_ref[:, :D], low_rows[...]).astype(half)
    for target in range(HEAD_GROUPS * spread):
        group, m = target // spread, target % spread
        for inner in range(member_slots):
            slot = m * member_slots + inner
            send_ref[target, inner] = grad_att[
                group * GROUP_FEATS : (group + 1) * GROUP_FEATS,
                slot * rows_dev : (slot + 1) * rows_dev,
            ]
    store_rows(packed_ref, n_doc, dot_nn(att_all[...], low_rows[...]), slice(0, D))
    grad = dot_tn(norm_ref[...].astype(half), query_rows[...])
    store_rows(packed_ref, n_doc, grad, slice(D, 2 * D))
    packed_ref[:, :, 2 * D : 4 * D] = mem_ref[...]
    small = [sums_ref[...], rows_a_ref[...], rows_b_ref[...], rows_c_ref[0:1, :]]
    used = sum(rows.shape[0] for rows in small)
    small.append(jnp.zeros((small_cols - used, D), f32))
    store_rows(
        packed_ref, n_doc, jnp.concatenate(small, axis=0).T, slice(4 * D, 4 * D + small_cols)
    )


def leave(n_doc, grad_query, att, resid, norm_one, unit, scale, vectors, w_pair, *others):
    rows_total, n_seq = resid.shape[0], att.shape[0]
    vmem = pl.BlockSpec(memory_space=pltpu.VMEM)
    return pl.pallas_call(
        partial(leave_kernel, n_doc),
        in_specs=[vmem] * (8 + len(others)),
        out_specs=[vmem] * 3,
        out_shape=[
            jax.ShapeDtypeStruct((rows_total, D), f32),
            jax.ShapeDtypeStruct(att.shape, half),
            jax.ShapeDtypeStruct((n_seq, D // n_seq, 4 * D + small_cols), half),
        ],
        scratch_shapes=[
            pltpu.VMEM((D, rows_total), half),
            pltpu.VMEM((D, rows_total), half),
            pltpu.VMEM((rows_total, D), half),
            pltpu.VMEM((rows_total, D), half),
            pltpu.VMEM((8, D), f32),
        ],
        compiler_params=pltpu.CompilerParams(vmem_limit_bytes=vmem_bytes),
        cost_estimate=cost_of(8),
        name="leave",
    )(grad_query, att, resid, norm_one, unit, scale, vectors, w_pair, *others)


def memory_kernel(n_doc, place_ref, mem_ref, *rest):
    pieces, (packed_ref, all_ref, sums_ref) = rest[: place_ref.shape[0]], rest[-3:]
    for turn, piece in enumerate(pieces):
        for kind in range(2):
            first = pl.multiple_of(kind * D + place_ref[turn] * GROUP_FEATS, GROUP_FEATS)
            all_ref[pl.ds(first, GROUP_FEATS), :] = piece[kind]
    turned = all_ref[...].T
    for kind in range(2):
        cols = slice(kind * D, (kind + 1) * D)
        store_rows(packed_ref, n_doc, dot_tn(mem_ref[...], turned[:, cols]), cols)
    sums_ref[...] = jnp.broadcast_to(row_sum(turned[:, D:].astype(f32)), sums_ref.shape)


small_cols = 128


def memory_backward(n_doc, n_seq, places, mem_low, pieces):
    tokens = mem_low.shape[0]
    vmem = pl.BlockSpec(memory_space=pltpu.VMEM)
    return pl.pallas_call(
        partial(memory_kernel, n_doc),
        grid_spec=pltpu.PrefetchScalarGridSpec(
            num_scalar_prefetch=1,
            grid=(1,),
            in_specs=[vmem] * (1 + len(pieces)),
            out_specs=[vmem] * 3,
        ),
        out_shape=[
            jax.ShapeDtypeStruct((n_seq, D // n_seq, 2 * D), half),
            jax.ShapeDtypeStruct((2 * D, tokens), half),
            jax.ShapeDtypeStruct((8, D), f32),
        ],
        compiler_params=pltpu.CompilerParams(vmem_limit_bytes=vmem_bytes),
        cost_estimate=cost_of(7),
        name="memory_backward",
    )(places, mem_low, *pieces)


def finish_kernel(
    n_seq,
    stack_n,
    lanes,
    in_ref,
    qkv_ref,
    out_ref,
    q_ref,
    kv_ref,
    down_ref,
    ffn_ref,
    cross_ref,
    gains_ref,
    biases_ref,
    hidden_ref,
):
    rows = in_ref.shape[0]
    share = rows // n_seq
    spread = n_seq // HEAD_GROUPS
    out_ref[...] = in_ref[:, :D].astype(f32)
    q_ref[...] = in_ref[:, D : 2 * D].astype(f32)
    kv_ref[...] = in_ref[:, 2 * D : 4 * D].astype(f32)
    small = in_ref[:, 4 * D : 4 * D + small_cols].astype(f32).T
    first_col = 4 * D + small_cols
    feats = 3 * GROUP_FEATS
    ff = ffn_ref.shape[1]
    down_col = first_col + HEAD_GROUPS * feats + small_cols
    ffn_col = down_col + stack_n * D
    ffn_ref[...] = in_ref[:, ffn_col : ffn_col + ff].astype(f32)
    cross_ref[...] = in_ref[:, ffn_col + ff :].astype(f32)
    for q in range(stack_n):
        mine = in_ref[:, down_col + q * D : down_col + (q + 1) * D].astype(f32)
        for s in range(n_seq):
            first = (s * stack_n + q) * share
            down_ref[first : first + share, :] = mine[s * share : (s + 1) * share]
    bias = jnp.zeros((share, small_cols), f32)
    wide = in_ref[:, first_col:down_col].astype(f32)
    for s in range(n_seq):
        group, m = s // spread, s % spread
        mine = wide[s * share : (s + 1) * share]
        for q in range(HEAD_GROUPS):
            first = (m * HEAD_GROUPS + q) * share
            for part in range(3):
                start = q * feats + part * GROUP_FEATS
                qkv_ref[
                    first : first + share,
                    part * D + group * GROUP_FEATS : part * D + (group + 1) * GROUP_FEATS,
                ] = mine[:, start : start + GROUP_FEATS]
        bias = bias + mine[:, HEAD_GROUPS * feats :]
    for row, source in enumerate((0, 8, 10)):
        gains_ref[row : row + 1, :] = small[source : source + 1]
    for row, source in ((2, 2), (3, 3), (4, 16 + stack_n), (5, 12), (6, 13), (7, 1), (8, 9), (9, 11)):
        biases_ref[row : row + 1, :] = small[source : source + 1]
    hidden_ref[...] = small[16 : 16 + stack_n]
    per_row = lanes // small_cols
    for row in range(2):
        found = [bias[row * per_row + i : row * per_row + i + 1] for i in range(per_row)]
        biases_ref[row : row + 1, :] = jnp.concatenate(found, axis=1)[:, :rows]


def finish(n_seq, stack_n, lanes, packed):
    rows = packed.shape[0]
    vmem = pl.BlockSpec(memory_space=pltpu.VMEM)
    return pl.pallas_call(
        partial(finish_kernel, n_seq, stack_n, lanes),
        in_specs=[vmem],
        out_specs=[vmem] * 10,
        out_shape=[
            jax.ShapeDtypeStruct((rows, 3 * D), f32),
            jax.ShapeDtypeStruct((rows, D), f32),
            jax.ShapeDtypeStruct((rows, D), f32),
            jax.ShapeDtypeStruct((rows, 2 * D), f32),
            jax.ShapeDtypeStruct((rows * stack_n, D), f32),
            jax.ShapeDtypeStruct((rows, stack_n * D), f32),
            jax.ShapeDtypeStruct((rows, D), f32),
            jax.ShapeDtypeStruct((3, rows), f32),
            jax.ShapeDtypeStruct((10, rows), f32),
            jax.ShapeDtypeStruct((stack_n, rows), f32),
        ],
        compiler_params=pltpu.CompilerParams(vmem_limit_bytes=vmem_bytes),
        cost_estimate=cost_of(6),
        name="finish",
    )(packed)


def load_pieces(place_ref, piece_refs, kv_ref, sems):
    tokens = piece_refs[0].shape[2]
    copies = [
        pltpu.make_async_copy(
            piece,
            kv_ref.at[:, :, pl.ds(pl.multiple_of(place_ref[i] * tokens, tokens), tokens)],
            sems.at[i],
        )
        for i, piece in enumerate(piece_refs)
    ]
    for copy in copies:
        copy.start()
    for copy in copies:
        copy.wait()


def tiles_of(low, high):
    first = low // key_tile
    return first, jnp.where(high > low, (high + key_tile - 1) // key_tile, first)


def cross_forward_kernel(low_ref, high_ref, place_ref, q_ref, *rest):
    pieces, (mix_ref, att_ref, lse_ref, acc_ref, kv_ref, sems) = rest[:-6], rest[-6:]
    slot = pl.program_id(0)

    @pl.when(slot == 0)
    def _():
        load_pieces(place_ref, pieces, kv_ref, sems)

    low, high = low_ref[slot], high_ref[slot]
    rows_dev = q_ref.shape[3]
    q_low = jnp.concatenate([q_ref[i, 0] for i in range(HEAD_GROUPS)], axis=1)
    q_low = q_low * jnp.asarray(score_scale, half)
    rows = q_low.shape[1]
    acc_ref[...] = jnp.zeros_like(acc_ref)

    def step(tile, carry):
        tops, totals = carry
        start = pl.multiple_of(tile * key_tile, key_tile)
        key_pos = start + lax.broadcasted_iota(jnp.int32, (key_tile, rows), 0)
        counted = (key_pos >= low) & (key_pos < high)
        new_tops, new_totals = [], []
        for head in range(GROUP_HEADS):
            feats = head_feats(head)
            k_low = kv_ref[0, feats, pl.ds(start, key_tile)]
            v_low = kv_ref[1, feats, pl.ds(start, key_tile)]
            scores = jnp.where(counted, dot_tn(k_low, q_low[feats]), masked_score)
            top = jnp.maximum(tops[head], jnp.max(scores, axis=0, keepdims=True))
            weight = jnp.exp(scores - top)
            rescale = jnp.exp(tops[head] - top)
            new_totals.append(totals[head] * rescale + jnp.sum(weight, axis=0, keepdims=True))
            new_tops.append(top)
            acc_ref[feats, :] = acc_ref[feats, :] * rescale + dot_nn(v_low, weight.astype(half))
        return (tuple(new_tops), tuple(new_totals))

    init = (
        tuple(jnp.full((1, rows), start_max, f32) for _ in range(GROUP_HEADS)),
        tuple(jnp.zeros((1, rows), f32) for _ in range(GROUP_HEADS)),
    )
    tops, totals = lax.fori_loop(*tiles_of(low, high), step, init)
    for head in range(GROUP_HEADS):
        feats = head_feats(head)
        live = totals[head] > 0
        total = jnp.where(live, totals[head], 1.0)
        mix = acc_ref[feats, :] / total
        mix_ref[0, feats, :] = mix
        mix_low = mix.astype(half)
        for i in range(HEAD_GROUPS):
            att_ref[i, 0, feats, :] = mix_low[:, i * rows_dev : (i + 1) * rows_dev]
        lse_ref[0, head : head + 1, :] = jnp.where(live, tops[head] + jnp.log(total), 0.0)


def cross_forward(low, high, places, queries, pieces):
    groups, slots, feats, rows_dev = queries.shape
    rows = groups * rows_dev
    tokens = pieces[0].shape[2] * len(pieces)
    row_block = pl.BlockSpec((groups, 1, feats, rows_dev), lambda s, *_: (0, s, 0, 0))
    return pl.pallas_call(
        cross_forward_kernel,
        grid_spec=pltpu.PrefetchScalarGridSpec(
            num_scalar_prefetch=3,
            grid=(slots,),
            in_specs=[row_block] + [pl.BlockSpec(memory_space=pl.ANY)] * len(pieces),
            out_specs=[
                pl.BlockSpec((1, feats, rows), lambda s, *_: (s, 0, 0)),
                row_block,
                pl.BlockSpec((1, GROUP_HEADS, rows), lambda s, *_: (s, 0, 0)),
            ],
            scratch_shapes=[
                pltpu.VMEM((feats, rows), f32),
                pltpu.VMEM((2, feats, tokens), half),
                pltpu.SemaphoreType.DMA((len(pieces),)),
            ],
        ),
        out_shape=[
            jax.ShapeDtypeStruct((slots, feats, rows), f32),
            jax.ShapeDtypeStruct(queries.shape, half),
            jax.ShapeDtypeStruct((slots, GROUP_HEADS, rows), f32),
        ],
        compiler_params=pltpu.CompilerParams(vmem_limit_bytes=vmem_bytes),
        cost_estimate=cost_of(45),
        name="cross_forward",
    )(low, high, places, queries, *pieces)


def cross_backward_kernel(
    low_ref, high_ref, place_ref, q_ref, g_ref, mix_ref, lse_ref, *rest
):
    count = place_ref.shape[0]
    spread = count // HEAD_GROUPS
    pieces = rest[:count]
    dq_ref, *dkv_outs = rest[-5 - spread : -4]
    dkv_ref, acc_ref, kv_ref, sems = rest[-4:]
    member = place_ref[0] % spread
    slot = pl.program_id(0)

    @pl.when(slot == 0)
    def _():
        dkv_ref[...] = jnp.zeros_like(dkv_ref)
        load_pieces(place_ref, pieces, kv_ref, sems)

    low, high = low_ref[slot], high_ref[slot]
    rows_dev = q_ref.shape[3]
    tiles_dev = dkv_ref.shape[4] // key_tile
    q_low = jnp.concatenate([q_ref[i, 0] for i in range(HEAD_GROUPS)], axis=1)
    q_low = q_low * jnp.asarray(score_scale, half)
    g_low = jnp.concatenate([g_ref[i, 0] for i in range(HEAD_GROUPS)], axis=1)
    rows = q_low.shape[1]
    acc_ref[...] = jnp.zeros_like(acc_ref)
    product = g_low.astype(f32) * mix_ref[0]
    delta = [jnp.sum(product[head_feats(h)], axis=0, keepdims=True) for h in range(GROUP_HEADS)]
    lse = [lse_ref[0, h : h + 1, :] for h in range(GROUP_HEADS)]

    def step(tile, carry):
        start = pl.multiple_of(tile * key_tile, key_tile)
        owner = tile // tiles_dev
        turn, group = (owner - member + spread) % spread, owner // spread
        inside = pl.multiple_of(tile % tiles_dev * key_tile, key_tile)
        key_pos = start + lax.broadcasted_iota(jnp.int32, (key_tile, rows), 0)
        counted = (key_pos >= low) & (key_pos < high)
        for head in range(GROUP_HEADS):
            feats = head_feats(head)
            k_low = kv_ref[0, feats, pl.ds(start, key_tile)]
            v_low = kv_ref[1, feats, pl.ds(start, key_tile)]
            scores = jnp.where(counted, dot_tn(k_low, q_low[feats]), masked_score)
            prob = jnp.exp(scores - lse[head])
            grad_prob = dot_tn(v_low, g_low[feats])
            grad_score = (prob * (grad_prob - delta[head])).astype(half)
            dkv_ref[turn, group, 1, feats, pl.ds(inside, key_tile)] += dot_nt(
                g_low[feats], prob.astype(half)
            ).astype(half)
            dkv_ref[turn, group, 0, feats, pl.ds(inside, key_tile)] += dot_nt(
                q_low[feats], grad_score
            ).astype(half)
            acc_ref[feats, :] += dot_nn(k_low, grad_score)
        return carry

    lax.fori_loop(*tiles_of(low, high), step, 0)
    dq_low = (acc_ref[...] * score_scale).astype(half)
    for i in range(HEAD_GROUPS):
        dq_ref[i, 0] = dq_low[:, i * rows_dev : (i + 1) * rows_dev]

    @pl.when(slot == pl.num_programs(0) - 1)
    def _():
        copies = [
            pltpu.make_async_copy(dkv_ref.at[turn], out, sems.at[turn])
            for turn, out in enumerate(dkv_outs)
        ]
        for copy in copies:
            copy.start()
        for copy in copies:
            copy.wait()


def cross_backward(low, high, places, queries, grad_mix, mix, lse, pieces, *after):
    groups, slots, feats, rows_dev = queries.shape
    rows = groups * rows_dev
    tokens = pieces[0].shape[2]
    row_block = pl.BlockSpec((groups, 1, feats, rows_dev), lambda s, *_: (0, s, 0, 0))
    grad_shape = (len(pieces) // groups, groups, 2, feats, tokens)
    return pl.pallas_call(
        cross_backward_kernel,
        grid_spec=pltpu.PrefetchScalarGridSpec(
            num_scalar_prefetch=3,
            grid=(slots,),
            in_specs=[
                row_block,
                row_block,
                pl.BlockSpec((1, feats, rows), lambda s, *_: (s, 0, 0)),
                pl.BlockSpec((1, GROUP_HEADS, rows), lambda s, *_: (s, 0, 0)),
            ]
            + [pl.BlockSpec(memory_space=pl.ANY)] * (len(pieces) + len(after)),
            out_specs=[row_block] + [pl.BlockSpec(memory_space=pl.ANY)] * grad_shape[0],
            scratch_shapes=[
                pltpu.VMEM(grad_shape, half),
                pltpu.VMEM((feats, rows), f32),
                pltpu.VMEM((2, feats, tokens * len(pieces)), half),
                pltpu.SemaphoreType.DMA((len(pieces),)),
            ],
        ),
        out_shape=[
            jax.ShapeDtypeStruct(queries.shape, half),
        ]
        + [jax.ShapeDtypeStruct(grad_shape[1:], half)] * grad_shape[0],
        compiler_params=pltpu.CompilerParams(vmem_limit_bytes=vmem_bytes),
        cost_estimate=cost_of(53),
        name="cross_backward",
    )(low, high, places, queries, grad_mix, mix, lse, *pieces, *after)


middle_rows = 256


def middle_kernel(
    n_doc,
    n_seq,
    att_ref,
    norm_ref,
    out_grad_ref,
    vec_ref,
    bias_ref,
    *rest,
):
    weights = rest[:-17]
    out_ref, resid_ref, send_ref, packed_ref, sums_ref, bias_grad_ref = rest[-17:-11]
    att_all, w_cross, w_in, w_out, norm_low, active = rest[-11:-5]
    slope, low_three, hidden_grad, low_two, sems = rest[-5:]
    slots, rows_dev = att_ref.shape[1], att_ref.shape[3]
    rows_total = slots * rows_dev
    rows = min(middle_rows, rows_total)
    ff = w_out.shape[0]
    chunk = ff // n_doc
    copies = []

    def copy_block(block, block_col, target, row, col):
        rows = pl.ds(block * block_rows, block_rows)
        copies.append(
            pltpu.make_async_copy(
                w_ref.at[rows, pl.ds(block_col * D, D)],
                target.at[pl.ds(row, block_rows), pl.ds(col, D)],
                sems.at[len(copies)],
            )
        )

    blocks = n_doc * n_seq
    block_rows = ff // blocks
    if len(weights) == 1:
        (w_ref,) = weights
        for band in range(blocks // 4):
            row = band * block_rows
            copy_block(4 * band, 1, w_cross, row, 0)
            for at, (block_col, block) in enumerate([(2, 0), (1, 1), (2, 1), (1, 2)]):
                copy_block(4 * band + block, block_col, w_in, row, at * D)
        for block in range(blocks):
            copy_block(block, 0, w_out, block * block_rows, 0)
    else:
        for i, (weight, target) in enumerate(zip(weights, (w_cross, w_in, w_out))):
            copies.append(pltpu.make_async_copy(weight, target, sems.at[i]))
    for copy in copies:
        copy.start()
    for group in range(HEAD_GROUPS):
        for slot in range(slots):
            att_all[
                group * GROUP_FEATS : (group + 1) * GROUP_FEATS,
                slot * rows_dev : (slot + 1) * rows_dev,
            ] = att_ref[group, slot]
    sums_ref[...] = jnp.zeros_like(sums_ref)
    bias_grad_ref[...] = jnp.zeros_like(bias_grad_ref)
    for copy in copies:
        copy.wait()

    def row_block(block, carry):
        where = pl.ds(pl.multiple_of(block * rows, rows), rows)
        gain_two, shift_two = vec_ref[0:1, :], vec_ref[1:2, :]
        gain_three, shift_three = vec_ref[2:3, :], vec_ref[3:4, :]
        branch = dot_tn(att_all[:, where], w_cross[...]) + vec_ref[4:5, :]
        unit_two, scale_two = normalize(norm_ref[where, :] + branch)
        norm_two = unit_two * gain_two + shift_two
        norm_two_low = norm_two.astype(half)
        norm_low[where, :] = norm_two_low
        branch = vec_ref[5:6, :]
        for z in range(n_doc):
            cols = slice(z * chunk, (z + 1) * chunk)
            hidden = dot_nn(norm_two_low, w_in[:, cols]) + bias_ref[:, cols]
            below = 0.5 + 0.5 * lax.erf(hidden * (0.5**0.5))
            density = jnp.exp(-0.5 * hidden * hidden) * 0.3989422804014327
            slope[:, cols] = below + hidden * density
            active_low = (hidden * below).astype(half)
            active[where, cols] = active_low
            branch = branch + dot_nn(active_low, w_out[cols, :])
        unit_three, scale_three = normalize(norm_two + branch)
        out_ref[where, :] = (unit_three * gain_three + shift_three).astype(half)
        incoming = out_grad_ref[where, :].astype(f32)
        sums_ref[2:3, :] += row_sum(incoming * unit_three)
        sums_ref[3:4, :] += row_sum(incoming)
        grad_three = norm_backward(incoming, gain_three, unit_three, scale_three)
        grad_low = grad_three.astype(half)
        low_three[where, :] = grad_low
        sums_ref[5:6, :] += row_sum(grad_low.astype(f32))
        incoming = grad_three
        for z in range(n_doc):
            cols = slice(z * chunk, (z + 1) * chunk)
            hidden_low = (dot_nt(grad_low, w_out[cols, :]) * slope[:, cols]).astype(half)
            hidden_grad[where, cols] = hidden_low
            bias_grad_ref[:, cols] += row_sum(hidden_low.astype(f32))
            incoming = incoming + dot_nt(hidden_low, w_in[:, cols])
        sums_ref[0:1, :] += row_sum(incoming * unit_two)
        sums_ref[1:2, :] += row_sum(incoming)
        grad_two = norm_backward(incoming, gain_two, unit_two, scale_two)
        resid_ref[where, :] = grad_two
        grad_low = grad_two.astype(half)
        low_two[where, :] = grad_low
        sums_ref[4:5, :] += row_sum(grad_low.astype(f32))
        return carry

    lax.fori_loop(0, rows_total // rows, row_block, 0)

    grad_att = dot_nt(w_cross[...], low_two[...]).astype(half)
    for group in range(HEAD_GROUPS):
        for slot in range(slots):
            send_ref[group, slot] = grad_att[
                group * GROUP_FEATS : (group + 1) * GROUP_FEATS,
                slot * rows_dev : (slot + 1) * rows_dev,
            ]

    share = D // (n_doc * n_seq)
    stack_n = chunk // (share * n_seq)

    store_rows(packed_ref, n_doc, dot_nn(att_all[...], low_two[...]), slice(2 * ff, 2 * ff + D))
    for z in range(n_doc):
        cols = slice(z * chunk, (z + 1) * chunk)
        grad = dot_tn(norm_low[...], hidden_grad[:, cols])
        store_rows(packed_ref, n_doc, grad, slice(ff + z * chunk, ff + (z + 1) * chunk))
    for pair in range(n_doc // 2):
        grads = []
        for z in (2 * pair, 2 * pair + 1):
            cols = slice(z * chunk, (z + 1) * chunk)
            grads.append(dot_tn(active[:, cols], low_three[...]))
        for s in range(n_seq):
            for q in range(stack_n):
                first = (s * stack_n + q) * share
                mine = [grad[first : first + share] for grad in grads]
                packed_ref[
                    s, pair * 2 * share : (pair + 1) * 2 * share, q * D : (q + 1) * D
                ] = jnp.concatenate(mine, axis=0).astype(half)


def middle(n_doc, n_seq, att, norm_one, out_grad, vectors, bias, weights):
    groups, slots, feats, rows_dev = att.shape
    rows_total = slots * rows_dev
    ff = weights[-1].shape[0]
    share = D // (n_doc * n_seq)
    vmem = pl.BlockSpec(memory_space=pltpu.VMEM)
    hbm = pl.BlockSpec(memory_space=pl.ANY)
    return pl.pallas_call(
        partial(middle_kernel, n_doc, n_seq),
        in_specs=[vmem] * 5 + [hbm] * len(weights),
        out_specs=[vmem] * 6,
        out_shape=[
            jax.ShapeDtypeStruct((rows_total, D), half),
            jax.ShapeDtypeStruct((rows_total, D), f32),
            jax.ShapeDtypeStruct(att.shape, half),
            jax.ShapeDtypeStruct((n_seq, n_doc * share, 2 * ff + D), half),
            jax.ShapeDtypeStruct((8, D), f32),
            jax.ShapeDtypeStruct((1, ff), f32),
        ],
        scratch_shapes=[
            pltpu.VMEM((D, rows_total), half),
            pltpu.VMEM((D, D), half),
            pltpu.VMEM((D, ff), half),
            pltpu.VMEM((ff, D), half),
            pltpu.VMEM((rows_total, D), half),
            pltpu.VMEM((rows_total, ff), half),
            pltpu.VMEM((min(middle_rows, rows_total), ff), f32),
            pltpu.VMEM((rows_total, D), half),
            pltpu.VMEM((rows_total, ff), half),
            pltpu.VMEM((rows_total, D), half),
            pltpu.SemaphoreType.DMA((n_doc * n_seq * 9 // 4,)),
        ],
        compiler_params=pltpu.CompilerParams(vmem_limit_bytes=vmem_bytes),
        cost_estimate=cost_of(31),
        name="middle",
    )(att, norm_one, out_grad, vectors, bias, *weights)


def body(
    n_doc,
    n_seq,
    dec_input,
    memory,
    doc_lengths,
    doc_count,
    self_qkv,
    self_out,
    cross_q,
    cross_kv,
    cross_out,
    ffn_in,
    ffn_in_bias,
    ffn_out,
    norm_gains,
    biases,
    out_grad,
):
    seq_index = lax.axis_index("seq")
    doc_index = lax.axis_index("doc")
    slots_n, rows_dev = dec_input.shape[1:3]
    rows_total = slots_n * rows_dev
    mem_rows = memory.shape[1]
    spread = n_seq // HEAD_GROUPS
    head_group = seq_index // spread
    member = seq_index % spread
    member_slots = slots_n // spread
    dec_len = rows_dev * n_seq
    same_member = [[h * spread + m for h in range(HEAD_GROUPS)] for m in range(spread)]

    def swap_heads(blocks):
        return lax.all_to_all(blocks, "seq", 0, 0, axis_index_groups=same_member, tiled=True)

    def rotate_both(block, turn_h, turn_m):
        if turn_h == turn_m == 0:
            return block
        return lax.ppermute(
            block,
            "seq",
            [
                (
                    h * spread + m,
                    (h + turn_h) % HEAD_GROUPS * spread + (m + turn_m) % spread,
                )
                for h in range(HEAD_GROUPS)
                for m in range(spread)
            ],
        )

    def rotate_heads(block, turn):
        return rotate_both(block, turn, 0)

    def rotate_members(block, turn):
        return rotate_both(block, 0, turn)

    def rotate_doc(block, turn):
        return lax.ppermute(block, "doc", [(d, (d + turn) % n_doc) for d in range(n_doc)])

    def in_order(pieces, own, axis):
        count = len(pieces)
        shape = pieces[0].shape
        whole = jnp.zeros(shape[:axis] + (count,) + shape[axis:], pieces[0].dtype)
        for turn, piece in enumerate(pieces):
            whole = lax.dynamic_update_index_in_dim(whole, piece, (own - turn) % count, axis)
        return whole

    def send_turns(blocks, axis, count, own, rotate):
        got = []
        for turn in range(count):
            block = lax.dynamic_index_in_dim(blocks, (own + turn) % count, axis, keepdims=False)
            got.append(rotate(block, turn) if turn else block)
        return got

    part = self_qkv.shape[0]
    width = 3 * GROUP_FEATS
    qkv_piece = jnp.concatenate(
        [
            lax.dynamic_slice_in_dim(
                self_qkv, block * D + head_group * GROUP_FEATS, GROUP_FEATS, 1
            )
            for block in range(3)
        ],
        axis=1,
    )
    small = jnp.concatenate([norm_gains, biases, ffn_in_bias.reshape(-1, part)], axis=0)
    small_rows = small.shape[0]
    first_width = width
    pad_rows = -(-small_rows * part // first_width)
    first_rows = -(-(part + pad_rows) // (8 * spread)) * 8 * spread
    pad_rows = first_rows - part
    small = jnp.pad(small.reshape(-1), (0, pad_rows * first_width - small_rows * part))
    first_piece = jnp.concatenate(
        [qkv_piece, small.reshape(pad_rows, width)], axis=0
    )
    first_piece = lax.dynamic_slice_in_dim(
        first_piece.astype(half), member * (first_rows // spread), first_rows // spread, 0
    )

    def join_members(mine):
        pieces = [mine] + [rotate_members(mine, turn) for turn in range(1, spread)]
        return in_order(pieces, member, 1).reshape(n_doc, -1, mine.shape[2])

    first_piece = jnp.broadcast_to(first_piece[None], (n_doc,) + first_piece.shape)
    first_gather = join_members(lax.all_to_all(first_piece, "doc", 0, 0, tiled=True))
    w_qkv_part = first_gather[:, :part].reshape(D, width)
    small = first_gather[:, part:].reshape(n_doc, -1)[:, : small_rows * part]
    small = small.reshape(n_doc, small_rows, part).astype(f32)
    gains_f = small[:, :3].transpose(1, 0, 2).reshape(3, D)
    biases_f = small[:, 3:13].transpose(1, 0, 2).reshape(10, D)
    b_ffn_in = small[:, 13:].reshape(1, -1)

    share = part // n_seq
    ff = ffn_in.shape[1]
    stack_n = ffn_out.shape[0] // part
    member_rows = part // spread

    def gather_halves(*weights):
        piece = [
            lax.dynamic_slice_in_dim(weight, member * member_rows, member_rows, 0).astype(half)
            for weight in weights
        ]
        return lax.all_gather(jnp.concatenate(piece, axis=1), "doc", axis=0)

    w_cross_kv = join_members(gather_halves(cross_kv)).reshape(D, 2 * D)
    pair_halves = gather_halves(self_out, cross_q)

    block_rows, block_cols = divmod(seq_index, 4)

    def column_block(weight, first):
        return lax.dynamic_slice(
            weight, (block_rows * member_rows, first), (member_rows, D)
        ).astype(half)

    def first_cols(*starts):
        return sum(jnp.where(block_cols == i, start, 0) for i, start in enumerate(starts) if start)

    left = jnp.where(
        block_cols == 0,
        column_block(cross_out, 0),
        jnp.where(
            block_cols == 3,
            column_block(self_qkv, D),
            column_block(ffn_in, first_cols(0, D, 3 * D, 0)),
        ),
    )
    right = jnp.where(
        block_cols < 2,
        column_block(ffn_in, first_cols(0, 2 * D, 0, 0)),
        column_block(self_qkv, first_cols(0, 0, 0, 2 * D)),
    )
    down = lax.dynamic_slice_in_dim(ffn_out, seq_index * member_rows, member_rows, 0).astype(half)
    w_blocks = lax.all_gather(
        jnp.concatenate([down, left, right], axis=1), ("doc", "seq"), axis=0, tiled=True
    )
    by_block = w_blocks.reshape(n_doc, spread, 4, member_rows, 3 * D)

    def columns(*blocks):
        found = [by_block[:, :, c, :, third * D : (third + 1) * D] for c, third in blocks]
        return jnp.concatenate(found, axis=3).reshape(D, -1)

    late_weights = [w_blocks]
    if member_rows % 16:
        late_weights = [
            columns((0, 1)),
            columns((0, 2), (1, 1), (1, 2), (2, 1)),
            w_blocks[:, :D],
        ]

    mem_low = memory[0]
    kv_bias = jnp.concatenate([jnp.zeros((D,), f32), biases_f[4]])
    mem_kv = (dot_tt(w_cross_kv, mem_low) + kv_bias[:, None]).astype(half)
    mem_kv = mem_kv.reshape(2, HEAD_GROUPS, GROUP_FEATS, mem_rows)
    pieces = send_turns(mem_kv, 1, HEAD_GROUPS, head_group, rotate_heads)
    pieces = pieces + [
        rotate_members(piece, turn) for turn in range(1, spread) for piece in pieces
    ]

    x_low = dec_input[0].reshape(rows_total, D)
    places = jnp.stack(
        [
            (head_group - turn_h) % HEAD_GROUPS * spread + (member - turn_m) % spread
            for turn_m in range(spread)
            for turn_h in range(HEAD_GROUPS)
        ]
    ).astype(jnp.int32)
    x_pieces = [rotate_heads(dec_input[0], turn) if turn else dec_input[0] for turn in range(HEAD_GROUPS)]
    for turn in range(1, spread):
        first_slot = (member + turn) % spread * member_slots
        blocks = [
            lax.dynamic_slice_in_dim(piece, first_slot, member_slots, 0)
            for piece in x_pieces[:HEAD_GROUPS]
        ]
        x_pieces.append(rotate_members(jnp.stack(blocks), turn))
    group_places = ((head_group - jnp.arange(HEAD_GROUPS)) % HEAD_GROUPS).astype(jnp.int32)
    zero_part = jnp.zeros((GROUP_FEATS,), f32)
    b_query = lax.dynamic_slice_in_dim(biases_f[0], head_group * GROUP_FEATS, GROUP_FEATS)
    b_value = lax.dynamic_slice_in_dim(biases_f[1], head_group * GROUP_FEATS, GROUP_FEATS)
    b_proj = jnp.concatenate([b_query, zero_part, b_value])[None]
    proj, self_mix, self_att_send, self_lse = self_forward(
        places, w_qkv_part, b_proj, x_pieces, n_seq, pieces[0]
    )

    def from_heads(blocks):
        feats = blocks.shape[2]
        got = blocks.reshape(HEAD_GROUPS, slots_n, feats // GROUP_FEATS, GROUP_FEATS, rows_dev)
        return got.transpose(2, 0, 3, 1, 4).reshape(HEAD_GROUPS * feats, rows_total)

    self_att_send, *pieces[1:HEAD_GROUPS] = lax.optimization_barrier(
        (self_att_send, *pieces[1:HEAD_GROUPS])
    )
    self_att = lax.all_to_all(self_att_send, "seq", 0, 0, tiled=True)
    pair_halves = lax.optimization_barrier((pair_halves, self_att_send))[0]
    w_pair = join_members(pair_halves).reshape(D, 2 * D)
    first_vectors = jnp.stack([biases_f[2], gains_f[0], biases_f[7], biases_f[3]])
    first_vectors = jnp.pad(first_vectors, ((0, 4), (0, 0)))
    norm_one, unit_one, scale_one, query_send = enter(
        self_att, x_low, first_vectors, w_pair, slots_n
    )

    lengths = doc_lengths[0]
    live_len = jnp.where(jnp.arange(slots_n) < doc_count[0], lengths, 0)
    key_high = jnp.minimum(jnp.cumsum(live_len), n_seq * mem_rows).astype(jnp.int32)
    key_low = jnp.concatenate([jnp.zeros((1,), jnp.int32), key_high[:-1]])
    query_part = swap_heads(query_send)
    cross_mix, cross_att_send, cross_lse = cross_forward(
        key_low, key_high, places, query_part, pieces
    )
    vectors = jnp.stack(
        [gains_f[1], biases_f[8], gains_f[2], biases_f[9], biases_f[5], biases_f[6]]
    )
    layer_out, grad_r2, grad_mix_send, late_packed, late_rows, grad_b_in = middle(
        n_doc,
        n_seq,
        swap_heads(cross_att_send),
        norm_one,
        out_grad[0].reshape(rows_total, D),
        jnp.pad(vectors, ((0, 2), (0, 0))),
        b_ffn_in,
        late_weights,
    )
    layer_out = layer_out.reshape(dec_input.shape)
    grad_g1, grad_c8, grad_g2, grad_c9, grad_b5, grad_b6 = late_rows[:6]

    def sum_over_seq(packed):
        packed = packed.reshape(D, packed.shape[2])
        return lax.psum_scatter(packed, "seq", scatter_dimension=0, tiled=True)

    def own_rows(packed):
        blocks = packed.reshape(n_doc, share, -1)
        pieces = send_turns(blocks, 0, n_doc, doc_index, rotate_doc)
        return sum(piece.astype(f32) for piece in pieces).astype(half)

    late_blocks = sum_over_seq(late_packed)
    grad_query_send, *grad_kv = cross_backward(
        key_low,
        key_high,
        places,
        query_part,
        swap_heads(grad_mix_send),
        cross_mix,
        cross_lse,
        pieces,
        late_packed,
    )
    grad_kv = [grad_kv[0]] + [
        rotate_members(grad_kv[turn], turn) for turn in range(1, spread)
    ]
    grad_kv_own = []
    for turn in range(HEAD_GROUPS):
        group = (head_group + turn) % HEAD_GROUPS
        total = sum(
            lax.dynamic_index_in_dim(piece, group, 0, keepdims=False).astype(f32)
            for piece in grad_kv
        ).astype(half)
        grad_kv_own.append(rotate_heads(total, turn) if turn else total)
    late_own = own_rows(lax.optimization_barrier((late_blocks, grad_kv_own[0]))[0])
    grad_query_send, late_own, *grad_kv_own = lax.optimization_barrier(
        (grad_query_send, late_own, *grad_kv_own)
    )
    mem_packed, grad_mem_kv, value_rows = memory_backward(
        n_doc, n_seq, group_places, mem_low, grad_kv_own
    )
    grad_r1, grad_att_send, packed = leave(
        n_doc,
        swap_heads(grad_query_send),
        self_att,
        grad_r2,
        norm_one,
        unit_one,
        scale_one,
        first_vectors,
        w_pair,
        mem_packed,
        late_rows,
        grad_b_in.reshape(n_doc, -1, part).transpose(1, 0, 2).reshape(-1, D),
        value_rows,
    )
    over_seq = sum_over_seq(packed)
    grad_self_part = lax.all_to_all(grad_att_send, "seq", 0, 0, tiled=True)
    grad_proj_send, grad_part, part_sums = self_backward(
        n_doc,
        places,
        proj,
        grad_self_part,
        self_mix,
        self_lse,
        x_pieces,
        packed,
    )
    grad_proj_send = lax.optimization_barrier((grad_proj_send, over_seq))[0]
    grad_proj_got = lax.all_to_all(grad_proj_send, "seq", 0, 0, tiled=True)

    bias_rows = jnp.zeros((2, D), f32)
    bias_rows = lax.dynamic_update_slice(
        bias_rows,
        jnp.stack([part_sums[0, :GROUP_FEATS], part_sums[0, 2 * GROUP_FEATS :]]),
        (0, head_group * GROUP_FEATS),
    )
    lanes = -(-part // small_cols) * small_cols
    bias_rows = jnp.pad(bias_rows.reshape(2, n_doc, part), ((0, 0), (0, 0), (0, lanes - part)))
    bias_rows = bias_rows.transpose(1, 0, 2).reshape(n_doc, -1, small_cols)
    bias_used = bias_rows.shape[1]
    bias_rows = jnp.pad(bias_rows, ((0, 0), (0, share - bias_used), (0, 0)))
    bias_rows = bias_rows.reshape(1, n_doc * share, small_cols).astype(half)
    bias_rows = jnp.pad(bias_rows, ((0, spread - 1), (0, 0), (0, 0)))
    grad_part = jnp.concatenate([grad_part, bias_rows], axis=2)
    grad_part = send_turns(grad_part, 0, spread, member, rotate_members)
    grad_part = sum(piece.astype(f32) for piece in grad_part).astype(half)

    grads = jnp.concatenate([over_seq, grad_part], axis=1)
    owned = jnp.concatenate([own_rows(grads), late_own], axis=1)
    param_grads = finish(n_seq, stack_n, lanes, lax.all_gather(owned, "seq", axis=0, tiled=True))
    (
        grad_w_qkv,
        grad_w_self_out,
        grad_w_cross_q,
        grad_w_cross_kv,
        grad_w_down,
        grad_w_in,
        grad_w_cross_out,
        grad_gains,
        grad_biases,
        grad_b_hidden,
    ) = param_grads
    grad_proj = from_heads(grad_proj_got)
    memory_grad = dot_tt(grad_mem_kv, w_cross_kv)[None]
    w_qkv = columns((2, 2), (3, 1), (3, 2))
    input_grad = (grad_r1 + dot_tt(grad_proj, w_qkv)).reshape(dec_input.shape)
    return (
        layer_out,
        input_grad,
        memory_grad,
        grad_w_qkv,
        grad_w_self_out,
        grad_w_cross_q,
        grad_w_cross_kv,
        grad_w_cross_out,
        grad_w_in,
        grad_b_hidden.reshape(-1),
        grad_w_down,
        grad_gains,
        grad_biases,
    )


def solution(mesh):
    placed = (
        P("doc", None, "seq", None),
        P("doc", "seq", None),
        P("doc", None),
        P("doc"),
        P("doc", None),
        P("doc", None),
        P("doc", None),
        P("doc", None),
        P("doc", None),
        P("doc", None),
        P("doc"),
        P("doc", None),
        P(None, "doc"),
        P(None, "doc"),
        P("doc", None, "seq", None),
    )
    return jax.shard_map(
        partial(body, mesh.shape["doc"], mesh.shape["seq"]),
        mesh=mesh,
        in_specs=placed,
        out_specs=(
            P("doc", None, "seq", None),
            P("doc", None, "seq", None),
            P("doc", "seq", None),
            P("doc", None),
            P("doc", None),
            P("doc", None),
            P("doc", None),
            P("doc", None),
            P("doc", None),
            P("doc"),
            P("doc", None),
            P(None, "doc"),
            P(None, "doc"),
        ),
        check_vma=False,
    )
```

```python
from functools import partial

import jax
import jax.numpy as jnp
from jax import lax
from jax.experimental import pallas as pl
from jax.experimental.pallas import tpu as pltpu
from jax.sharding import PartitionSpec as P

D = 768
HEADS = 12
HEAD_DIM = 64
HEAD_GROUPS = 4
GROUP_HEADS = HEADS // HEAD_GROUPS
GROUP_FEATS = GROUP_HEADS * HEAD_DIM

norm_eps = 1e-05
masked_score = -2e30
start_max = -1e30
score_scale = HEAD_DIM ** (-0.5)
forward_tile = 512
key_tile = 256
row_tile = 256
vmem_bytes = 56 * 2**20

f32 = jnp.float32
half = jnp.bfloat16


def cost_of(micros):
    return pl.CostEstimate(flops=micros * 10**9, bytes_accessed=micros * 10**6, transcendentals=0)


def layer_norm(resid_in, gain_row, shift_row):
    center = resid_in - jnp.mean(resid_in, axis=-1, keepdims=True)
    variance = jnp.mean(center * center, axis=-1, keepdims=True)
    return center * lax.rsqrt(variance + norm_eps) * gain_row + shift_row


def contract(left_op, right_op, left_dim, right_dim):
    return lax.dot_general(
        left_op,
        right_op,
        (((left_dim,), (right_dim,)), ((), ())),
        preferred_element_type=f32,
    )


def dot_nn(left_op, right_op):
    return contract(left_op, right_op, 1, 0)


def dot_nt(left_op, right_op):
    return contract(left_op, right_op, 1, 1)


def dot_tn(left_op, right_op):
    return contract(left_op, right_op, 0, 0)


def dot_tt(left_op, right_op):
    return contract(left_op, right_op, 0, 1)


def col_sums(grad_low):
    return jnp.sum(grad_low.astype(f32), axis=0)


def normalize(resid):
    center = resid - jnp.mean(resid, axis=-1, keepdims=True)
    scale = lax.rsqrt(jnp.mean(center * center, axis=-1, keepdims=True) + norm_eps)
    return center * scale, scale


def norm_backward(incoming, gain_row, unit, scale):
    grad = incoming * gain_row
    mean_one = jnp.mean(grad, axis=-1, keepdims=True)
    mean_two = jnp.mean(grad * unit, axis=-1, keepdims=True)
    return (grad - mean_one - unit * mean_two) * scale


def row_sum(grad):
    return jnp.sum(grad, axis=0, keepdims=True)


def store_rows(packed_ref, n_doc, grad, cols):
    n_seq, rows = packed_ref.shape[:2]
    share = rows // n_doc
    for s in range(n_seq):
        mine = [grad[(z * n_seq + s) * share : (z * n_seq + s + 1) * share] for z in range(n_doc)]
        packed_ref[s, :, cols] = jnp.concatenate(mine, axis=0).astype(half)


def head_feats(head, block=0):
    start = block * GROUP_FEATS + head * HEAD_DIM
    return slice(start, start + HEAD_DIM)


def load_rows(place_ref, piece_refs, x_ref, sems):
    spread = place_ref.shape[0] // HEAD_GROUPS
    slots = x_ref.shape[0]
    rows_dev = x_ref.shape[1] // place_ref.shape[0]
    member = place_ref[0] % spread
    copies = []
    for i in range(place_ref.shape[0]):
        turn_m, turn_h = i // HEAD_GROUPS, i % HEAD_GROUPS
        if turn_m:
            piece = piece_refs[HEAD_GROUPS + turn_m - 1].at[turn_h]
        else:
            piece = piece_refs[turn_h].at[pl.ds(member * slots, slots)]
        first = pl.multiple_of(place_ref[i] * rows_dev, rows_dev)
        copies.append(
            pltpu.make_async_copy(piece, x_ref.at[:, pl.ds(first, rows_dev)], sems.at[i])
        )
    for copy in copies:
        copy.start()
    for copy in copies:
        copy.wait()


def self_forward_kernel(place_ref, w_ref, bias_ref, *rest):
    pieces, (proj_ref, mix_ref, att_ref, lse_ref, x_ref, sems) = rest[:-6], rest[-6:]
    slot = pl.program_id(0)

    @pl.when(slot == 0)
    def _():
        load_rows(place_ref, pieces, x_ref, sems)

    length = proj_ref.shape[1]
    rows_dev = att_ref.shape[3]
    rows = min(row_tile, length)
    for first in range(0, length, rows):
        part = dot_nn(x_ref[slot, first : first + rows, :], w_ref[...]) + bias_ref[0:1, :]
        proj_ref[:, first : first + rows] = part.astype(half).T
    def score(head, first):
        upto = first + rows
        q_low = proj_ref[head_feats(head), first:upto] * jnp.asarray(score_scale, half)
        scores = dot_tn(proj_ref[head_feats(head, 1), :upto], q_low)
        key_pos = lax.broadcasted_iota(jnp.int32, scores.shape, 0)
        row_pos = first + lax.broadcasted_iota(jnp.int32, scores.shape, 1)
        return jnp.where(key_pos <= row_pos, scores, masked_score)

    def store(head, first, weight_low, top, total):
        feats, cols = head_feats(head), slice(first, first + rows)
        mix = dot_nn(proj_ref[head_feats(head, 2), : first + rows], weight_low) / total
        mix_ref[0, feats, cols] = mix
        mix_low = mix.astype(half)
        for place in range(rows // rows_dev):
            att_ref[first // rows_dev + place, 0, feats, :] = mix_low[
                :, place * rows_dev : (place + 1) * rows_dev
            ]
        lse_ref[0, head : head + 1, cols] = top + jnp.log(total)

    parts = [(head, first) for first in range(0, length, rows) for head in range(GROUP_HEADS)]
    ahead, waiting = score(*parts[0]), None
    for i, part in enumerate(parts):
        scores = ahead
        if i + 1 < len(parts):
            ahead = score(*parts[i + 1])
        top = jnp.max(scores, axis=0, keepdims=True)
        weight = jnp.exp(scores - top)
        total = jnp.sum(weight, axis=0, keepdims=True)
        if waiting is not None:
            store(*waiting)
        waiting = (*part, weight.astype(half), top, total)
    store(*waiting)


def self_forward(places, w_part, bias, pieces, n_seq, *after):
    slots = pieces[0].shape[0] * HEAD_GROUPS // n_seq
    length = pieces[0].shape[1] * n_seq
    feats, rows_dev = w_part.shape[1], length // n_seq
    return pl.pallas_call(
        self_forward_kernel,
        grid_spec=pltpu.PrefetchScalarGridSpec(
            num_scalar_prefetch=1,
            grid=(slots,),
            in_specs=[
                pl.BlockSpec(w_part.shape, lambda s, *_: (0, 0)),
                pl.BlockSpec(bias.shape, lambda s, *_: (0, 0)),
            ]
            + [pl.BlockSpec(memory_space=pl.ANY)] * (len(pieces) + len(after)),
            out_specs=[
                pl.BlockSpec((feats, length), lambda s, *_: (0, s)),
                pl.BlockSpec((1, GROUP_FEATS, length), lambda s, *_: (s, 0, 0)),
                pl.BlockSpec((n_seq, 1, GROUP_FEATS, rows_dev), lambda s, *_: (0, s, 0, 0)),
                pl.BlockSpec((1, GROUP_HEADS, length), lambda s, *_: (s, 0, 0)),
            ],
            scratch_shapes=[
                pltpu.VMEM((slots, length, D), half),
                pltpu.SemaphoreType.DMA((n_seq,)),
            ],
        ),
        out_shape=[
            jax.ShapeDtypeStruct((feats, slots * length), half),
            jax.ShapeDtypeStruct((slots, GROUP_FEATS, length), f32),
            jax.ShapeDtypeStruct((n_seq, slots, GROUP_FEATS, rows_dev), half),
            jax.ShapeDtypeStruct((slots, GROUP_HEADS, length), f32),
        ],
        compiler_params=pltpu.CompilerParams(vmem_limit_bytes=vmem_bytes),
        cost_estimate=cost_of(18),
        name="self_forward",
    )(places, w_part, bias, *pieces, *after)


def self_backward_kernel(n_doc, place_ref, proj_ref, grad_ref, mix_ref, lse_ref, *rest):
    ins, (send_ref, w_grad_ref, sums_ref, dproj_ref, dk_ref, dv_ref, w_acc, x_ref, sems) = (
        rest[:-9],
        rest[-9:],
    )
    pieces = ins[: HEAD_GROUPS + place_ref.shape[0] // HEAD_GROUPS - 1]
    slot = pl.program_id(0)

    @pl.when(slot == 0)
    def _():
        load_rows(place_ref, pieces, x_ref, sems)
        w_acc[...] = jnp.zeros_like(w_acc)
        sums_ref[...] = jnp.zeros_like(sums_ref)

    length = proj_ref.shape[1]
    n_seq, rows_dev = grad_ref.shape[0], grad_ref.shape[3]
    rows = min(row_tile, length)
    dk_ref[...] = jnp.zeros_like(dk_ref)
    dv_ref[...] = jnp.zeros_like(dv_ref)
    def products(head, first):
        upto = first + rows
        feats, cols = head_feats(head), slice(first, upto)
        places = range(first // rows_dev, upto // rows_dev)
        q_low = proj_ref[feats, cols] * jnp.asarray(score_scale, half)
        g_low = jnp.concatenate([grad_ref[place, 0, feats, :] for place in places], axis=1)
        delta = jnp.sum(g_low.astype(f32) * mix_ref[0, feats, cols], axis=0, keepdims=True)
        scores = dot_tn(proj_ref[head_feats(head, 1), :upto], q_low)
        key_pos = lax.broadcasted_iota(jnp.int32, scores.shape, 0)
        row_pos = first + lax.broadcasted_iota(jnp.int32, scores.shape, 1)
        scores = jnp.where(key_pos <= row_pos, scores, masked_score)
        return scores, dot_tn(proj_ref[head_feats(head, 2), :upto], g_low), q_low, g_low, delta

    def add(head, first, q_low, g_low, prob_low, grad_score):
        feats, upto = head_feats(head), first + rows
        dv_ref[feats, :upto] += dot_nt(g_low, prob_low)
        dk_ref[feats, :upto] += dot_nt(q_low, grad_score)
        grad_query = dot_nn(proj_ref[head_feats(head, 1), :upto], grad_score) * score_scale
        dproj_ref[feats, first:upto] = grad_query.astype(half)

    parts = [(head, first) for first in range(0, length, rows) for head in range(GROUP_HEADS)]
    ahead, waiting = products(*parts[0]), None
    for i, (head, first) in enumerate(parts):
        scores, grad_prob, q_low, g_low, delta = ahead
        if i + 1 < len(parts):
            ahead = products(*parts[i + 1])
        prob = jnp.exp(scores - lse_ref[0, head : head + 1, first : first + rows])
        grad_score = (prob * (grad_prob - delta)).astype(half)
        if waiting is not None:
            add(*waiting)
        waiting = (head, first, q_low, g_low, prob.astype(half), grad_score)
    add(*waiting)
    dproj_ref[GROUP_FEATS : 2 * GROUP_FEATS, :] = dk_ref[...].astype(half)
    dproj_ref[2 * GROUP_FEATS :, :] = dv_ref[...].astype(half)
    for place in range(n_seq):
        send_ref[place, 0] = dproj_ref[:, place * rows_dev : (place + 1) * rows_dev]
    for first in range(0, length, rows):
        turned = dproj_ref[:, first : first + rows].T
        sums_ref[0:1, :] += row_sum(turned.astype(f32))
        w_acc[...] += dot_tn(x_ref[slot, first : first + rows, :], turned)

    @pl.when(slot == pl.num_programs(0) - 1)
    def _():
        spread, stored, width = w_grad_ref.shape
        share = stored // n_doc
        feats = dproj_ref.shape[0]
        quarters = width // feats
        for m in range(spread):
            for q in range(quarters):
                mine = []
                for z in range(n_doc):
                    first = ((z * spread + m) * quarters + q) * share
                    mine.append(w_acc[first : first + share, :])
                w_grad_ref[m, :, q * feats : (q + 1) * feats] = jnp.concatenate(
                    mine, axis=0
                ).astype(half)


def self_backward(n_doc, places, proj, grad_mix, mix, lse, pieces, *after):
    n_seq, slots, _, rows_dev = grad_mix.shape
    feats, length = proj.shape[0], n_seq * rows_dev
    spread = n_seq // HEAD_GROUPS
    stored = D // n_seq
    return pl.pallas_call(
        partial(self_backward_kernel, n_doc),
        grid_spec=pltpu.PrefetchScalarGridSpec(
            num_scalar_prefetch=1,
            grid=(slots,),
            in_specs=[
                pl.BlockSpec((feats, length), lambda s, *_: (0, s)),
                pl.BlockSpec((n_seq, 1, GROUP_FEATS, rows_dev), lambda s, *_: (0, s, 0, 0)),
                pl.BlockSpec((1, GROUP_FEATS, length), lambda s, *_: (s, 0, 0)),
                pl.BlockSpec((1, GROUP_HEADS, length), lambda s, *_: (s, 0, 0)),
            ]
            + [pl.BlockSpec(memory_space=pl.ANY)] * (len(pieces) + len(after)),
            out_specs=[
                pl.BlockSpec((n_seq, 1, feats, rows_dev), lambda s, *_: (0, s, 0, 0)),
                pl.BlockSpec((spread, stored, HEAD_GROUPS * feats), lambda s, *_: (0, 0, 0)),
                pl.BlockSpec((8, feats), lambda s, *_: (0, 0)),
            ],
            scratch_shapes=[
                pltpu.VMEM((feats, length), half),
                pltpu.VMEM((GROUP_FEATS, length), f32),
                pltpu.VMEM((GROUP_FEATS, length), f32),
                pltpu.VMEM((D, feats), f32),
                pltpu.VMEM((slots, length, D), half),
                pltpu.SemaphoreType.DMA((n_seq,)),
            ],
        ),
        out_shape=[
            jax.ShapeDtypeStruct((n_seq, slots, feats, rows_dev), half),
            jax.ShapeDtypeStruct((spread, stored, HEAD_GROUPS * feats), half),
            jax.ShapeDtypeStruct((8, feats), f32),
        ],
        compiler_params=pltpu.CompilerParams(vmem_limit_bytes=vmem_bytes),
        cost_estimate=cost_of(20),
        name="self_backward",
    )(places, proj, grad_mix, mix, lse, *pieces, *after)


def enter_kernel(att_ref, x_ref, vec_ref, w_ref, norm_ref, unit_ref, scale_ref, send_ref, att_all):
    gather_att(att_ref, att_all)
    slots, rows_dev = send_ref.shape[1], send_ref.shape[3]
    rows = min(middle_rows, x_ref.shape[0])
    for first in range(0, x_ref.shape[0], rows):
        where = slice(first, first + rows)
        branch = dot_tn(att_all[:, where], w_ref[:, :D]) + vec_ref[0:1, :]
        unit, scale = normalize(x_ref[where, :].astype(f32) + branch)
        norm = unit * vec_ref[1:2, :] + vec_ref[2:3, :]
        norm_ref[where, :] = norm
        unit_ref[where, :] = unit
        scale_ref[where, :] = jnp.broadcast_to(scale, (rows, scale_ref.shape[1]))
        query = dot_nn(norm.astype(half), w_ref[:, D:]) + vec_ref[3:4, :]
        query = query.astype(half).T
        for group in range(HEAD_GROUPS):
            for place in range(rows // rows_dev):
                send_ref[group, first // rows_dev + place] = query[
                    group * GROUP_FEATS : (group + 1) * GROUP_FEATS,
                    place * rows_dev : (place + 1) * rows_dev,
                ]


def gather_att(att_ref, att_all):
    n_seq, member_slots, _, rows_dev = att_ref.shape
    spread = n_seq // HEAD_GROUPS
    for source in range(n_seq):
        group, m = source // spread, source % spread
        for inner in range(member_slots):
            slot = m * member_slots + inner
            att_all[
                group * GROUP_FEATS : (group + 1) * GROUP_FEATS,
                slot * rows_dev : (slot + 1) * rows_dev,
            ] = att_ref[source, inner]


def enter(att, x_low, vectors, w_pair, slots):
    rows_total, rows_dev = x_low.shape[0], att.shape[3]
    vmem = pl.BlockSpec(memory_space=pltpu.VMEM)
    return pl.pallas_call(
        enter_kernel,
        in_specs=[vmem] * 4,
        out_specs=[vmem] * 4,
        out_shape=[
            jax.ShapeDtypeStruct((rows_total, D), f32),
            jax.ShapeDtypeStruct((rows_total, D), f32),
            jax.ShapeDtypeStruct((rows_total, 128), f32),
            jax.ShapeDtypeStruct((HEAD_GROUPS, slots, GROUP_FEATS, rows_dev), half),
        ],
        scratch_shapes=[pltpu.VMEM((D, rows_total), half)],
        compiler_params=pltpu.CompilerParams(vmem_limit_bytes=vmem_bytes),
        cost_estimate=cost_of(6),
        name="enter",
    )(att, x_low, vectors, w_pair)


def leave_kernel(
    n_doc,
    query_ref,
    att_ref,
    resid_ref,
    norm_ref,
    unit_ref,
    scale_ref,
    vec_ref,
    w_ref,
    mem_ref,
    rows_a_ref,
    rows_b_ref,
    rows_c_ref,
    out_ref,
    send_ref,
    packed_ref,
    att_all,
    query_all,
    query_rows,
    low_rows,
    sums_ref,
):
    slots, rows_dev = query_ref.shape[1], query_ref.shape[3]
    member_slots = att_ref.shape[1]
    spread = slots // member_slots
    rows_total = resid_ref.shape[0]
    rows = min(middle_rows, rows_total)
    gather_att(att_ref, att_all)
    for group in range(HEAD_GROUPS):
        for slot in range(slots):
            query_all[
                group * GROUP_FEATS : (group + 1) * GROUP_FEATS,
                slot * rows_dev : (slot + 1) * rows_dev,
            ] = query_ref[group, slot]
    sums_ref[...] = jnp.zeros_like(sums_ref)
    for first in range(0, rows_total, rows):
        where = slice(first, first + rows)
        query = query_all[:, where].T
        query_rows[where, :] = query
        sums_ref[3:4, :] += row_sum(query.astype(f32))
        incoming = resid_ref[where, :] + dot_nt(query, w_ref[:, D:])
        unit = unit_ref[where, :]
        sums_ref[0:1, :] += row_sum(incoming * unit)
        sums_ref[1:2, :] += row_sum(incoming)
        grad = norm_backward(incoming, vec_ref[1:2, :], unit, scale_ref[where, 0:1])
        out_ref[where, :] = grad
        grad_low = grad.astype(half)
        low_rows[where, :] = grad_low
        sums_ref[2:3, :] += row_sum(grad_low.astype(f32))
    grad_att = dot_nt(w_ref[:, :D], low_rows[...]).astype(half)
    for target in range(HEAD_GROUPS * spread):
        group, m = target // spread, target % spread
        for inner in range(member_slots):
            slot = m * member_slots + inner
            send_ref[target, inner] = grad_att[
                group * GROUP_FEATS : (group + 1) * GROUP_FEATS,
                slot * rows_dev : (slot + 1) * rows_dev,
            ]
    store_rows(packed_ref, n_doc, dot_nn(att_all[...], low_rows[...]), slice(0, D))
    grad = dot_tn(norm_ref[...].astype(half), query_rows[...])
    store_rows(packed_ref, n_doc, grad, slice(D, 2 * D))
    packed_ref[:, :, 2 * D : 4 * D] = mem_ref[...]
    small = [sums_ref[...], rows_a_ref[...], rows_b_ref[...], rows_c_ref[0:1, :]]
    used = sum(rows.shape[0] for rows in small)
    small.append(jnp.zeros((small_cols - used, D), f32))
    store_rows(
        packed_ref, n_doc, jnp.concatenate(small, axis=0).T, slice(4 * D, 4 * D + small_cols)
    )


def leave(n_doc, grad_query, att, resid, norm_one, unit, scale, vectors, w_pair, *others):
    rows_total, n_seq = resid.shape[0], att.shape[0]
    vmem = pl.BlockSpec(memory_space=pltpu.VMEM)
    return pl.pallas_call(
        partial(leave_kernel, n_doc),
        in_specs=[vmem] * (8 + len(others)),
        out_specs=[vmem] * 3,
        out_shape=[
            jax.ShapeDtypeStruct((rows_total, D), f32),
            jax.ShapeDtypeStruct(att.shape, half),
            jax.ShapeDtypeStruct((n_seq, D // n_seq, 4 * D + small_cols), half),
        ],
        scratch_shapes=[
            pltpu.VMEM((D, rows_total), half),
            pltpu.VMEM((D, rows_total), half),
            pltpu.VMEM((rows_total, D), half),
            pltpu.VMEM((rows_total, D), half),
            pltpu.VMEM((8, D), f32),
        ],
        compiler_params=pltpu.CompilerParams(vmem_limit_bytes=vmem_bytes),
        cost_estimate=cost_of(8),
        name="leave",
    )(grad_query, att, resid, norm_one, unit, scale, vectors, w_pair, *others)


def memory_kernel(n_doc, place_ref, mem_ref, *rest):
    pieces, (packed_ref, all_ref, sums_ref) = rest[: place_ref.shape[0]], rest[-3:]
    for turn, piece in enumerate(pieces):
        for kind in range(2):
            first = pl.multiple_of(kind * D + place_ref[turn] * GROUP_FEATS, GROUP_FEATS)
            all_ref[pl.ds(first, GROUP_FEATS), :] = piece[kind]
    turned = all_ref[...].T
    for kind in range(2):
        cols = slice(kind * D, (kind + 1) * D)
        store_rows(packed_ref, n_doc, dot_tn(mem_ref[...], turned[:, cols]), cols)
    sums_ref[...] = jnp.broadcast_to(row_sum(turned[:, D:].astype(f32)), sums_ref.shape)


small_cols = 128


def memory_backward(n_doc, n_seq, places, mem_low, pieces):
    tokens = mem_low.shape[0]
    vmem = pl.BlockSpec(memory_space=pltpu.VMEM)
    return pl.pallas_call(
        partial(memory_kernel, n_doc),
        grid_spec=pltpu.PrefetchScalarGridSpec(
            num_scalar_prefetch=1,
            grid=(1,),
            in_specs=[vmem] * (1 + len(pieces)),
            out_specs=[vmem] * 3,
        ),
        out_shape=[
            jax.ShapeDtypeStruct((n_seq, D // n_seq, 2 * D), half),
            jax.ShapeDtypeStruct((2 * D, tokens), half),
            jax.ShapeDtypeStruct((8, D), f32),
        ],
        compiler_params=pltpu.CompilerParams(vmem_limit_bytes=vmem_bytes),
        cost_estimate=cost_of(7),
        name="memory_backward",
    )(places, mem_low, *pieces)


def finish_kernel(
    n_seq,
    stack_n,
    lanes,
    in_ref,
    qkv_ref,
    out_ref,
    q_ref,
    kv_ref,
    down_ref,
    ffn_ref,
    cross_ref,
    gains_ref,
    biases_ref,
    hidden_ref,
):
    rows = in_ref.shape[0]
    share = rows // n_seq
    spread = n_seq // HEAD_GROUPS
    out_ref[...] = in_ref[:, :D].astype(f32)
    q_ref[...] = in_ref[:, D : 2 * D].astype(f32)
    kv_ref[...] = in_ref[:, 2 * D : 4 * D].astype(f32)
    small = in_ref[:, 4 * D : 4 * D + small_cols].astype(f32).T
    first_col = 4 * D + small_cols
    feats = 3 * GROUP_FEATS
    ff = ffn_ref.shape[1]
    down_col = first_col + HEAD_GROUPS * feats + small_cols
    ffn_col = down_col + stack_n * D
    ffn_ref[...] = in_ref[:, ffn_col : ffn_col + ff].astype(f32)
    cross_ref[...] = in_ref[:, ffn_col + ff :].astype(f32)
    for q in range(stack_n):
        mine = in_ref[:, down_col + q * D : down_col + (q + 1) * D].astype(f32)
        for s in range(n_seq):
            first = (s * stack_n + q) * share
            down_ref[first : first + share, :] = mine[s * share : (s + 1) * share]
    bias = jnp.zeros((share, small_cols), f32)
    wide = in_ref[:, first_col:down_col].astype(f32)
    for s in range(n_seq):
        group, m = s // spread, s % spread
        mine = wide[s * share : (s + 1) * share]
        for q in range(HEAD_GROUPS):
            first = (m * HEAD_GROUPS + q) * share
            for part in range(3):
                start = q * feats + part * GROUP_FEATS
                qkv_ref[
                    first : first + share,
                    part * D + group * GROUP_FEATS : part * D + (group + 1) * GROUP_FEATS,
                ] = mine[:, start : start + GROUP_FEATS]
        bias = bias + mine[:, HEAD_GROUPS * feats :]
    for row, source in enumerate((0, 8, 10)):
        gains_ref[row : row + 1, :] = small[source : source + 1]
    for row, source in ((2, 2), (3, 3), (4, 16 + stack_n), (5, 12), (6, 13), (7, 1), (8, 9), (9, 11)):
        biases_ref[row : row + 1, :] = small[source : source + 1]
    hidden_ref[...] = small[16 : 16 + stack_n]
    per_row = lanes // small_cols
    for row in range(2):
        found = [bias[row * per_row + i : row * per_row + i + 1] for i in range(per_row)]
        biases_ref[row : row + 1, :] = jnp.concatenate(found, axis=1)[:, :rows]


def finish(n_seq, stack_n, lanes, packed):
    rows = packed.shape[0]
    vmem = pl.BlockSpec(memory_space=pltpu.VMEM)
    return pl.pallas_call(
        partial(finish_kernel, n_seq, stack_n, lanes),
        in_specs=[vmem],
        out_specs=[vmem] * 10,
        out_shape=[
            jax.ShapeDtypeStruct((rows, 3 * D), f32),
            jax.ShapeDtypeStruct((rows, D), f32),
            jax.ShapeDtypeStruct((rows, D), f32),
            jax.ShapeDtypeStruct((rows, 2 * D), f32),
            jax.ShapeDtypeStruct((rows * stack_n, D), f32),
            jax.ShapeDtypeStruct((rows, stack_n * D), f32),
            jax.ShapeDtypeStruct((rows, D), f32),
            jax.ShapeDtypeStruct((3, rows), f32),
            jax.ShapeDtypeStruct((10, rows), f32),
            jax.ShapeDtypeStruct((stack_n, rows), f32),
        ],
        compiler_params=pltpu.CompilerParams(vmem_limit_bytes=vmem_bytes),
        cost_estimate=cost_of(6),
        name="finish",
    )(packed)


def load_pieces(place_ref, piece_refs, kv_ref, sems):
    tokens = piece_refs[0].shape[2]
    copies = [
        pltpu.make_async_copy(
            piece,
            kv_ref.at[:, :, pl.ds(pl.multiple_of(place_ref[i] * tokens, tokens), tokens)],
            sems.at[i],
        )
        for i, piece in enumerate(piece_refs)
    ]
    for copy in copies:
        copy.start()
    for copy in copies:
        copy.wait()


def tiles_of(low, high, tile):
    first = low // tile
    return first, jnp.where(high > low, (high + tile - 1) // tile, first)


def cross_forward_kernel(low_ref, high_ref, place_ref, q_ref, *rest):
    pieces, (mix_ref, att_ref, lse_ref, acc_ref, kv_ref, sems) = rest[:-6], rest[-6:]
    slot = pl.program_id(0)

    @pl.when(slot == 0)
    def _():
        load_pieces(place_ref, pieces, kv_ref, sems)

    low, high = low_ref[slot], high_ref[slot]
    rows_dev = q_ref.shape[3]
    q_low = jnp.concatenate([q_ref[i, 0] for i in range(HEAD_GROUPS)], axis=1)
    q_low = q_low * jnp.asarray(score_scale, half)
    rows = q_low.shape[1]
    acc_ref[...] = jnp.zeros_like(acc_ref)

    def step(tile, carry):
        tops, totals = carry
        start = pl.multiple_of(tile * forward_tile, forward_tile)
        keys = pl.ds(start, forward_tile)
        key_pos = start + lax.broadcasted_iota(jnp.int32, (forward_tile, rows), 0)
        counted = (key_pos >= low) & (key_pos < high)

        def score(head):
            feats = head_feats(head)
            return jnp.where(counted, dot_tn(kv_ref[0, feats, keys], q_low[feats]), masked_score)

        def add(head, weight_low, rescale):
            feats = head_feats(head)
            mixed = dot_nn(kv_ref[1, feats, keys], weight_low)
            acc_ref[feats, :] = acc_ref[feats, :] * rescale + mixed

        new_tops, new_totals = [], []
        ahead, waiting = score(0), None
        for head in range(GROUP_HEADS):
            scores = ahead
            if head + 1 < GROUP_HEADS:
                ahead = score(head + 1)
            top = jnp.maximum(tops[head], jnp.max(scores, axis=0, keepdims=True))
            weight = jnp.exp(scores - top)
            rescale = jnp.exp(tops[head] - top)
            new_totals.append(totals[head] * rescale + jnp.sum(weight, axis=0, keepdims=True))
            new_tops.append(top)
            if waiting is not None:
                add(*waiting)
            waiting = (head, weight.astype(half), rescale)
        add(*waiting)
        return (tuple(new_tops), tuple(new_totals))

    init = (
        tuple(jnp.full((1, rows), start_max, f32) for _ in range(GROUP_HEADS)),
        tuple(jnp.zeros((1, rows), f32) for _ in range(GROUP_HEADS)),
    )
    tops, totals = lax.fori_loop(*tiles_of(low, high, forward_tile), step, init)
    for head in range(GROUP_HEADS):
        feats = head_feats(head)
        live = totals[head] > 0
        total = jnp.where(live, totals[head], 1.0)
        mix = acc_ref[feats, :] / total
        mix_ref[0, feats, :] = mix
        mix_low = mix.astype(half)
        for i in range(HEAD_GROUPS):
            att_ref[i, 0, feats, :] = mix_low[:, i * rows_dev : (i + 1) * rows_dev]
        lse_ref[0, head : head + 1, :] = jnp.where(live, tops[head] + jnp.log(total), 0.0)


def cross_forward(low, high, places, queries, pieces):
    groups, slots, feats, rows_dev = queries.shape
    rows = groups * rows_dev
    tokens = pieces[0].shape[2] * len(pieces)
    row_block = pl.BlockSpec((groups, 1, feats, rows_dev), lambda s, *_: (0, s, 0, 0))
    return pl.pallas_call(
        cross_forward_kernel,
        grid_spec=pltpu.PrefetchScalarGridSpec(
            num_scalar_prefetch=3,
            grid=(slots,),
            in_specs=[row_block] + [pl.BlockSpec(memory_space=pl.ANY)] * len(pieces),
            out_specs=[
                pl.BlockSpec((1, feats, rows), lambda s, *_: (s, 0, 0)),
                row_block,
                pl.BlockSpec((1, GROUP_HEADS, rows), lambda s, *_: (s, 0, 0)),
            ],
            scratch_shapes=[
                pltpu.VMEM((feats, rows), f32),
                pltpu.VMEM((2, feats, tokens), half),
                pltpu.SemaphoreType.DMA((len(pieces),)),
            ],
        ),
        out_shape=[
            jax.ShapeDtypeStruct((slots, feats, rows), f32),
            jax.ShapeDtypeStruct(queries.shape, half),
            jax.ShapeDtypeStruct((slots, GROUP_HEADS, rows), f32),
        ],
        compiler_params=pltpu.CompilerParams(vmem_limit_bytes=vmem_bytes),
        cost_estimate=cost_of(33),
        name="cross_forward",
    )(low, high, places, queries, *pieces)


def cross_backward_kernel(
    low_ref, high_ref, place_ref, q_ref, g_ref, mix_ref, lse_ref, *rest
):
    count = place_ref.shape[0]
    spread = count // HEAD_GROUPS
    pieces = rest[:count]
    dq_ref, *dkv_outs = rest[-5 - spread : -4]
    dkv_ref, acc_ref, kv_ref, sems = rest[-4:]
    member = place_ref[0] % spread
    slot = pl.program_id(0)

    @pl.when(slot == 0)
    def _():
        dkv_ref[...] = jnp.zeros_like(dkv_ref)
        load_pieces(place_ref, pieces, kv_ref, sems)

    low, high = low_ref[slot], high_ref[slot]
    rows_dev = q_ref.shape[3]
    tiles_dev = dkv_ref.shape[4] // key_tile
    q_low = jnp.concatenate([q_ref[i, 0] for i in range(HEAD_GROUPS)], axis=1)
    q_low = q_low * jnp.asarray(score_scale, half)
    g_low = jnp.concatenate([g_ref[i, 0] for i in range(HEAD_GROUPS)], axis=1)
    rows = q_low.shape[1]
    acc_ref[...] = jnp.zeros_like(acc_ref)
    product = g_low.astype(f32) * mix_ref[0]
    delta = [jnp.sum(product[head_feats(h)], axis=0, keepdims=True) for h in range(GROUP_HEADS)]
    lse = [lse_ref[0, h : h + 1, :] for h in range(GROUP_HEADS)]

    def step(tile, carry):
        start = pl.multiple_of(tile * key_tile, key_tile)
        owner = tile // tiles_dev
        turn, group = (owner - member + spread) % spread, owner // spread
        inside = pl.multiple_of(tile % tiles_dev * key_tile, key_tile)
        key_pos = start + lax.broadcasted_iota(jnp.int32, (key_tile, rows), 0)
        counted = (key_pos >= low) & (key_pos < high)
        keys = pl.ds(start, key_tile)

        def products(head):
            feats = head_feats(head)
            scores = dot_tn(kv_ref[0, feats, keys], q_low[feats])
            return scores, dot_tn(kv_ref[1, feats, keys], g_low[feats])

        def add(head, prob_low, grad_score):
            feats = head_feats(head)
            own_keys = (feats, pl.ds(inside, key_tile))
            grad_values = dot_nt(prob_low, g_low[feats]).T
            grad_keys = dot_nt(grad_score, q_low[feats]).T
            dkv_ref[(turn, group, 1, *own_keys)] += grad_values.astype(half)
            dkv_ref[(turn, group, 0, *own_keys)] += grad_keys.astype(half)
            acc_ref[feats, :] += dot_nn(kv_ref[0, feats, keys], grad_score)

        ahead, waiting = products(0), None
        for head in range(GROUP_HEADS):
            scores, grad_prob = ahead
            if head + 1 < GROUP_HEADS:
                ahead = products(head + 1)
            prob = jnp.exp(jnp.where(counted, scores, masked_score) - lse[head])
            grad_score = (prob * (grad_prob - delta[head])).astype(half)
            if waiting is not None:
                add(*waiting)
            waiting = (head, prob.astype(half), grad_score)
        add(*waiting)
        return carry

    lax.fori_loop(*tiles_of(low, high, key_tile), step, 0)
    dq_low = (acc_ref[...] * score_scale).astype(half)
    for i in range(HEAD_GROUPS):
        dq_ref[i, 0] = dq_low[:, i * rows_dev : (i + 1) * rows_dev]

    @pl.when(slot == pl.num_programs(0) - 1)
    def _():
        copies = [
            pltpu.make_async_copy(dkv_ref.at[turn], out, sems.at[turn])
            for turn, out in enumerate(dkv_outs)
        ]
        for copy in copies:
            copy.start()
        for copy in copies:
            copy.wait()


def cross_backward(low, high, places, queries, grad_mix, mix, lse, pieces, *after):
    groups, slots, feats, rows_dev = queries.shape
    rows = groups * rows_dev
    tokens = pieces[0].shape[2]
    row_block = pl.BlockSpec((groups, 1, feats, rows_dev), lambda s, *_: (0, s, 0, 0))
    grad_shape = (len(pieces) // groups, groups, 2, feats, tokens)
    return pl.pallas_call(
        cross_backward_kernel,
        grid_spec=pltpu.PrefetchScalarGridSpec(
            num_scalar_prefetch=3,
            grid=(slots,),
            in_specs=[
                row_block,
                row_block,
                pl.BlockSpec((1, feats, rows), lambda s, *_: (s, 0, 0)),
                pl.BlockSpec((1, GROUP_HEADS, rows), lambda s, *_: (s, 0, 0)),
            ]
            + [pl.BlockSpec(memory_space=pl.ANY)] * (len(pieces) + len(after)),
            out_specs=[row_block] + [pl.BlockSpec(memory_space=pl.ANY)] * grad_shape[0],
            scratch_shapes=[
                pltpu.VMEM(grad_shape, half),
                pltpu.VMEM((feats, rows), f32),
                pltpu.VMEM((2, feats, tokens * len(pieces)), half),
                pltpu.SemaphoreType.DMA((len(pieces),)),
            ],
        ),
        out_shape=[
            jax.ShapeDtypeStruct(queries.shape, half),
        ]
        + [jax.ShapeDtypeStruct(grad_shape[1:], half)] * grad_shape[0],
        compiler_params=pltpu.CompilerParams(vmem_limit_bytes=vmem_bytes),
        cost_estimate=cost_of(49),
        name="cross_backward",
    )(low, high, places, queries, grad_mix, mix, lse, *pieces, *after)


middle_rows = 256


def middle_kernel(
    n_doc,
    n_seq,
    att_ref,
    norm_ref,
    out_grad_ref,
    vec_ref,
    bias_ref,
    *rest,
):
    weights = rest[:-17]
    out_ref, resid_ref, send_ref, packed_ref, sums_ref, bias_grad_ref = rest[-17:-11]
    att_all, w_cross, w_in, w_out, norm_low, active = rest[-11:-5]
    slope, low_three, hidden_grad, low_two, sems = rest[-5:]
    slots, rows_dev = att_ref.shape[1], att_ref.shape[3]
    rows_total = slots * rows_dev
    rows = min(middle_rows, rows_total)
    ff = w_out.shape[0]
    chunk = ff // n_doc
    copies = []

    def copy_block(block, block_col, target, row, col):
        rows = pl.ds(block * block_rows, block_rows)
        copies.append(
            pltpu.make_async_copy(
                w_ref.at[rows, pl.ds(block_col * D, D)],
                target.at[pl.ds(row, block_rows), pl.ds(col, D)],
                sems.at[len(copies)],
            )
        )

    blocks = n_doc * n_seq
    block_rows = ff // blocks
    if len(weights) == 1:
        (w_ref,) = weights
        for band in range(blocks // 4):
            row = band * block_rows
            copy_block(4 * band, 1, w_cross, row, 0)
            for at, (block_col, block) in enumerate([(2, 0), (1, 1), (2, 1), (1, 2)]):
                copy_block(4 * band + block, block_col, w_in, row, at * D)
        for block in range(blocks):
            copy_block(block, 0, w_out, block * block_rows, 0)
    else:
        for i, (weight, target) in enumerate(zip(weights, (w_cross, w_in, w_out))):
            copies.append(pltpu.make_async_copy(weight, target, sems.at[i]))
    for copy in copies:
        copy.start()
    for group in range(HEAD_GROUPS):
        for slot in range(slots):
            att_all[
                group * GROUP_FEATS : (group + 1) * GROUP_FEATS,
                slot * rows_dev : (slot + 1) * rows_dev,
            ] = att_ref[group, slot]
    sums_ref[...] = jnp.zeros_like(sums_ref)
    bias_grad_ref[...] = jnp.zeros_like(bias_grad_ref)
    for copy in copies:
        copy.wait()

    def row_block(block, carry):
        where = pl.ds(pl.multiple_of(block * rows, rows), rows)
        gain_two, shift_two = vec_ref[0:1, :], vec_ref[1:2, :]
        gain_three, shift_three = vec_ref[2:3, :], vec_ref[3:4, :]
        branch = dot_tn(att_all[:, where], w_cross[...]) + vec_ref[4:5, :]
        unit_two, scale_two = normalize(norm_ref[where, :] + branch)
        norm_two = unit_two * gain_two + shift_two
        norm_two_low = norm_two.astype(half)
        norm_low[where, :] = norm_two_low
        branch = vec_ref[5:6, :]
        for z in range(n_doc):
            cols = slice(z * chunk, (z + 1) * chunk)
            hidden = dot_nn(norm_two_low, w_in[:, cols]) + bias_ref[:, cols]
            below = 0.5 + 0.5 * lax.erf(hidden * (0.5**0.5))
            density = jnp.exp(-0.5 * hidden * hidden) * 0.3989422804014327
            slope[:, cols] = below + hidden * density
            active_low = (hidden * below).astype(half)
            active[where, cols] = active_low
            branch = branch + dot_nn(active_low, w_out[cols, :])
        unit_three, scale_three = normalize(norm_two + branch)
        out_ref[where, :] = (unit_three * gain_three + shift_three).astype(half)
        incoming = out_grad_ref[where, :].astype(f32)
        sums_ref[2:3, :] += row_sum(incoming * unit_three)
        sums_ref[3:4, :] += row_sum(incoming)
        grad_three = norm_backward(incoming, gain_three, unit_three, scale_three)
        grad_low = grad_three.astype(half)
        low_three[where, :] = grad_low
        sums_ref[5:6, :] += row_sum(grad_low.astype(f32))
        incoming = grad_three
        for z in range(n_doc):
            cols = slice(z * chunk, (z + 1) * chunk)
            hidden_low = (dot_nt(grad_low, w_out[cols, :]) * slope[:, cols]).astype(half)
            hidden_grad[where, cols] = hidden_low
            bias_grad_ref[:, cols] += row_sum(hidden_low.astype(f32))
            incoming = incoming + dot_nt(hidden_low, w_in[:, cols])
        sums_ref[0:1, :] += row_sum(incoming * unit_two)
        sums_ref[1:2, :] += row_sum(incoming)
        grad_two = norm_backward(incoming, gain_two, unit_two, scale_two)
        resid_ref[where, :] = grad_two
        grad_low = grad_two.astype(half)
        low_two[where, :] = grad_low
        sums_ref[4:5, :] += row_sum(grad_low.astype(f32))
        return carry

    lax.fori_loop(0, rows_total // rows, row_block, 0)

    grad_att = dot_nt(w_cross[...], low_two[...]).astype(half)
    for group in range(HEAD_GROUPS):
        for slot in range(slots):
            send_ref[group, slot] = grad_att[
                group * GROUP_FEATS : (group + 1) * GROUP_FEATS,
                slot * rows_dev : (slot + 1) * rows_dev,
            ]

    share = D // (n_doc * n_seq)
    stack_n = chunk // (share * n_seq)

    store_rows(packed_ref, n_doc, dot_nn(att_all[...], low_two[...]), slice(2 * ff, 2 * ff + D))
    for z in range(n_doc):
        cols = slice(z * chunk, (z + 1) * chunk)
        grad = dot_tn(norm_low[...], hidden_grad[:, cols])
        store_rows(packed_ref, n_doc, grad, slice(ff + z * chunk, ff + (z + 1) * chunk))
    for pair in range(n_doc // 2):
        grads = []
        for z in (2 * pair, 2 * pair + 1):
            cols = slice(z * chunk, (z + 1) * chunk)
            grads.append(dot_tn(active[:, cols], low_three[...]))
        for s in range(n_seq):
            for q in range(stack_n):
                first = (s * stack_n + q) * share
                mine = [grad[first : first + share] for grad in grads]
                packed_ref[
                    s, pair * 2 * share : (pair + 1) * 2 * share, q * D : (q + 1) * D
                ] = jnp.concatenate(mine, axis=0).astype(half)


def middle(n_doc, n_seq, att, norm_one, out_grad, vectors, bias, weights):
    groups, slots, feats, rows_dev = att.shape
    rows_total = slots * rows_dev
    ff = weights[-1].shape[0]
    share = D // (n_doc * n_seq)
    vmem = pl.BlockSpec(memory_space=pltpu.VMEM)
    hbm = pl.BlockSpec(memory_space=pl.ANY)
    return pl.pallas_call(
        partial(middle_kernel, n_doc, n_seq),
        in_specs=[vmem] * 5 + [hbm] * len(weights),
        out_specs=[vmem] * 6,
        out_shape=[
            jax.ShapeDtypeStruct((rows_total, D), half),
            jax.ShapeDtypeStruct((rows_total, D), f32),
            jax.ShapeDtypeStruct(att.shape, half),
            jax.ShapeDtypeStruct((n_seq, n_doc * share, 2 * ff + D), half),
            jax.ShapeDtypeStruct((8, D), f32),
            jax.ShapeDtypeStruct((1, ff), f32),
        ],
        scratch_shapes=[
            pltpu.VMEM((D, rows_total), half),
            pltpu.VMEM((D, D), half),
            pltpu.VMEM((D, ff), half),
            pltpu.VMEM((ff, D), half),
            pltpu.VMEM((rows_total, D), half),
            pltpu.VMEM((rows_total, ff), half),
            pltpu.VMEM((min(middle_rows, rows_total), ff), f32),
            pltpu.VMEM((rows_total, D), half),
            pltpu.VMEM((rows_total, ff), half),
            pltpu.VMEM((rows_total, D), half),
            pltpu.SemaphoreType.DMA((n_doc * n_seq * 9 // 4,)),
        ],
        compiler_params=pltpu.CompilerParams(vmem_limit_bytes=vmem_bytes),
        cost_estimate=cost_of(31),
        name="middle",
    )(att, norm_one, out_grad, vectors, bias, *weights)


def body(
    n_doc,
    n_seq,
    dec_input,
    memory,
    doc_lengths,
    doc_count,
    self_qkv,
    self_out,
    cross_q,
    cross_kv,
    cross_out,
    ffn_in,
    ffn_in_bias,
    ffn_out,
    norm_gains,
    biases,
    out_grad,
):
    seq_index = lax.axis_index("seq")
    doc_index = lax.axis_index("doc")
    slots_n, rows_dev = dec_input.shape[1:3]
    rows_total = slots_n * rows_dev
    mem_rows = memory.shape[1]
    spread = n_seq // HEAD_GROUPS
    head_group = seq_index // spread
    member = seq_index % spread
    member_slots = slots_n // spread
    dec_len = rows_dev * n_seq
    same_member = [[h * spread + m for h in range(HEAD_GROUPS)] for m in range(spread)]

    def swap_heads(blocks):
        return lax.all_to_all(blocks, "seq", 0, 0, axis_index_groups=same_member, tiled=True)

    def rotate_both(block, turn_h, turn_m):
        if turn_h == turn_m == 0:
            return block
        return lax.ppermute(
            block,
            "seq",
            [
                (
                    h * spread + m,
                    (h + turn_h) % HEAD_GROUPS * spread + (m + turn_m) % spread,
                )
                for h in range(HEAD_GROUPS)
                for m in range(spread)
            ],
        )

    def rotate_heads(block, turn):
        return rotate_both(block, turn, 0)

    def rotate_members(block, turn):
        return rotate_both(block, 0, turn)

    def rotate_doc(block, turn):
        return lax.ppermute(block, "doc", [(d, (d + turn) % n_doc) for d in range(n_doc)])

    def in_order(pieces, own, axis):
        count = len(pieces)
        shape = pieces[0].shape
        whole = jnp.zeros(shape[:axis] + (count,) + shape[axis:], pieces[0].dtype)
        for turn, piece in enumerate(pieces):
            whole = lax.dynamic_update_index_in_dim(whole, piece, (own - turn) % count, axis)
        return whole

    def send_turns(blocks, axis, count, own, rotate):
        got = []
        for turn in range(count):
            block = lax.dynamic_index_in_dim(blocks, (own + turn) % count, axis, keepdims=False)
            got.append(rotate(block, turn) if turn else block)
        return got

    part = self_qkv.shape[0]
    width = 3 * GROUP_FEATS
    qkv_piece = jnp.concatenate(
        [
            lax.dynamic_slice_in_dim(
                self_qkv, block * D + head_group * GROUP_FEATS, GROUP_FEATS, 1
            )
            for block in range(3)
        ],
        axis=1,
    )
    small = jnp.concatenate([norm_gains, biases, ffn_in_bias.reshape(-1, part)], axis=0)
    small_rows = small.shape[0]
    first_width = width
    pad_rows = -(-small_rows * part // first_width)
    first_rows = -(-(part + pad_rows) // (8 * spread)) * 8 * spread
    pad_rows = first_rows - part
    small = jnp.pad(small.reshape(-1), (0, pad_rows * first_width - small_rows * part))
    first_piece = jnp.concatenate(
        [qkv_piece, small.reshape(pad_rows, width)], axis=0
    )
    first_piece = lax.dynamic_slice_in_dim(
        first_piece.astype(half), member * (first_rows // spread), first_rows // spread, 0
    )

    def join_members(mine):
        pieces = [mine] + [rotate_members(mine, turn) for turn in range(1, spread)]
        return in_order(pieces, member, 1).reshape(n_doc, -1, mine.shape[2])

    first_piece = jnp.broadcast_to(first_piece[None], (n_doc,) + first_piece.shape)
    first_gather = join_members(lax.all_to_all(first_piece, "doc", 0, 0, tiled=True))
    w_qkv_part = first_gather[:, :part].reshape(D, width)
    small = first_gather[:, part:].reshape(n_doc, -1)[:, : small_rows * part]
    small = small.reshape(n_doc, small_rows, part).astype(f32)
    gains_f = small[:, :3].transpose(1, 0, 2).reshape(3, D)
    biases_f = small[:, 3:13].transpose(1, 0, 2).reshape(10, D)
    b_ffn_in = small[:, 13:].reshape(1, -1)

    share = part // n_seq
    ff = ffn_in.shape[1]
    stack_n = ffn_out.shape[0] // part
    member_rows = part // spread

    def gather_halves(*weights):
        piece = [
            lax.dynamic_slice_in_dim(weight, member * member_rows, member_rows, 0).astype(half)
            for weight in weights
        ]
        return lax.all_gather(jnp.concatenate(piece, axis=1), "doc", axis=0)

    w_cross_kv = join_members(gather_halves(cross_kv)).reshape(D, 2 * D)
    pair_halves = gather_halves(self_out, cross_q)

    block_rows, block_cols = divmod(seq_index, 4)

    def column_block(weight, first):
        return lax.dynamic_slice(
            weight, (block_rows * member_rows, first), (member_rows, D)
        ).astype(half)

    def first_cols(*starts):
        return sum(jnp.where(block_cols == i, start, 0) for i, start in enumerate(starts) if start)

    left = jnp.where(
        block_cols == 0,
        column_block(cross_out, 0),
        jnp.where(
            block_cols == 3,
            column_block(self_qkv, D),
            column_block(ffn_in, first_cols(0, D, 3 * D, 0)),
        ),
    )
    right = jnp.where(
        block_cols < 2,
        column_block(ffn_in, first_cols(0, 2 * D, 0, 0)),
        column_block(self_qkv, first_cols(0, 0, 0, 2 * D)),
    )
    down = lax.dynamic_slice_in_dim(ffn_out, seq_index * member_rows, member_rows, 0).astype(half)
    w_blocks = lax.all_gather(
        jnp.concatenate([down, left, right], axis=1), ("doc", "seq"), axis=0, tiled=True
    )
    by_block = w_blocks.reshape(n_doc, spread, 4, member_rows, 3 * D)

    def columns(*blocks):
        found = [by_block[:, :, c, :, third * D : (third + 1) * D] for c, third in blocks]
        return jnp.concatenate(found, axis=3).reshape(D, -1)

    late_weights = [w_blocks]
    if member_rows % 16:
        late_weights = [
            columns((0, 1)),
            columns((0, 2), (1, 1), (1, 2), (2, 1)),
            w_blocks[:, :D],
        ]

    mem_low = memory[0]
    kv_bias = jnp.concatenate([jnp.zeros((D,), f32), biases_f[4]])
    mem_kv = (dot_tt(w_cross_kv, mem_low) + kv_bias[:, None]).astype(half)
    mem_kv = mem_kv.reshape(2, HEAD_GROUPS, GROUP_FEATS, mem_rows)
    pieces = send_turns(mem_kv, 1, HEAD_GROUPS, head_group, rotate_heads)
    pieces = pieces + [
        rotate_members(piece, turn) for turn in range(1, spread) for piece in pieces
    ]

    x_low = dec_input[0].reshape(rows_total, D)
    places = jnp.stack(
        [
            (head_group - turn_h) % HEAD_GROUPS * spread + (member - turn_m) % spread
            for turn_m in range(spread)
            for turn_h in range(HEAD_GROUPS)
        ]
    ).astype(jnp.int32)
    x_pieces = [rotate_heads(dec_input[0], turn) if turn else dec_input[0] for turn in range(HEAD_GROUPS)]
    for turn in range(1, spread):
        first_slot = (member + turn) % spread * member_slots
        blocks = [
            lax.dynamic_slice_in_dim(piece, first_slot, member_slots, 0)
            for piece in x_pieces[:HEAD_GROUPS]
        ]
        x_pieces.append(rotate_members(jnp.stack(blocks), turn))
    group_places = ((head_group - jnp.arange(HEAD_GROUPS)) % HEAD_GROUPS).astype(jnp.int32)
    zero_part = jnp.zeros((GROUP_FEATS,), f32)
    b_query = lax.dynamic_slice_in_dim(biases_f[0], head_group * GROUP_FEATS, GROUP_FEATS)
    b_value = lax.dynamic_slice_in_dim(biases_f[1], head_group * GROUP_FEATS, GROUP_FEATS)
    b_proj = jnp.concatenate([b_query, zero_part, b_value])[None]
    proj, self_mix, self_att_send, self_lse = self_forward(
        places, w_qkv_part, b_proj, x_pieces, n_seq, pieces[0]
    )

    def from_heads(blocks):
        feats = blocks.shape[2]
        got = blocks.reshape(HEAD_GROUPS, slots_n, feats // GROUP_FEATS, GROUP_FEATS, rows_dev)
        return got.transpose(2, 0, 3, 1, 4).reshape(HEAD_GROUPS * feats, rows_total)

    self_att_send, *pieces[1:HEAD_GROUPS] = lax.optimization_barrier(
        (self_att_send, *pieces[1:HEAD_GROUPS])
    )
    self_att = lax.all_to_all(self_att_send, "seq", 0, 0, tiled=True)
    pair_halves = lax.optimization_barrier((pair_halves, self_att_send))[0]
    w_pair = join_members(pair_halves).reshape(D, 2 * D)
    first_vectors = jnp.stack([biases_f[2], gains_f[0], biases_f[7], biases_f[3]])
    first_vectors = jnp.pad(first_vectors, ((0, 4), (0, 0)))
    norm_one, unit_one, scale_one, query_send = enter(
        self_att, x_low, first_vectors, w_pair, slots_n
    )

    lengths = doc_lengths[0]
    live_len = jnp.where(jnp.arange(slots_n) < doc_count[0], lengths, 0)
    key_high = jnp.minimum(jnp.cumsum(live_len), n_seq * mem_rows).astype(jnp.int32)
    key_low = jnp.concatenate([jnp.zeros((1,), jnp.int32), key_high[:-1]])
    query_part = swap_heads(query_send)
    cross_mix, cross_att_send, cross_lse = cross_forward(
        key_low, key_high, places, query_part, pieces
    )
    vectors = jnp.stack(
        [gains_f[1], biases_f[8], gains_f[2], biases_f[9], biases_f[5], biases_f[6]]
    )
    layer_out, grad_r2, grad_mix_send, late_packed, late_rows, grad_b_in = middle(
        n_doc,
        n_seq,
        swap_heads(cross_att_send),
        norm_one,
        out_grad[0].reshape(rows_total, D),
        jnp.pad(vectors, ((0, 2), (0, 0))),
        b_ffn_in,
        late_weights,
    )
    layer_out = layer_out.reshape(dec_input.shape)
    grad_g1, grad_c8, grad_g2, grad_c9, grad_b5, grad_b6 = late_rows[:6]

    def sum_over_seq(packed):
        packed = packed.reshape(D, packed.shape[2])
        return lax.psum_scatter(packed, "seq", scatter_dimension=0, tiled=True)

    def own_rows(packed):
        blocks = packed.reshape(n_doc, share, -1)
        pieces = send_turns(blocks, 0, n_doc, doc_index, rotate_doc)
        return sum(piece.astype(f32) for piece in pieces).astype(half)

    late_blocks = sum_over_seq(late_packed)
    grad_query_send, *grad_kv = cross_backward(
        key_low,
        key_high,
        places,
        query_part,
        swap_heads(grad_mix_send),
        cross_mix,
        cross_lse,
        pieces,
        late_packed,
    )
    grad_kv = [grad_kv[0]] + [
        rotate_members(grad_kv[turn], turn) for turn in range(1, spread)
    ]
    grad_kv_own = []
    for turn in range(HEAD_GROUPS):
        group = (head_group + turn) % HEAD_GROUPS
        total = sum(
            lax.dynamic_index_in_dim(piece, group, 0, keepdims=False).astype(f32)
            for piece in grad_kv
        ).astype(half)
        grad_kv_own.append(rotate_heads(total, turn) if turn else total)
    late_own = own_rows(lax.optimization_barrier((late_blocks, grad_kv_own[2]))[0])
    grad_query_send, *grad_kv_own = lax.optimization_barrier((grad_query_send, *grad_kv_own))
    mem_packed, grad_mem_kv, value_rows = memory_backward(
        n_doc, n_seq, group_places, mem_low, grad_kv_own
    )
    grad_r1, grad_att_send, packed = leave(
        n_doc,
        swap_heads(grad_query_send),
        self_att,
        grad_r2,
        norm_one,
        unit_one,
        scale_one,
        first_vectors,
        w_pair,
        mem_packed,
        late_rows,
        grad_b_in.reshape(n_doc, -1, part).transpose(1, 0, 2).reshape(-1, D),
        value_rows,
    )
    over_seq = sum_over_seq(packed)
    grad_self_part = lax.all_to_all(grad_att_send, "seq", 0, 0, tiled=True)
    grad_proj_send, grad_part, part_sums = self_backward(
        n_doc,
        places,
        proj,
        grad_self_part,
        self_mix,
        self_lse,
        x_pieces,
        packed,
        late_own,
    )
    grad_proj_send = lax.optimization_barrier((grad_proj_send, over_seq))[0]
    grad_proj_got = lax.all_to_all(grad_proj_send, "seq", 0, 0, tiled=True)

    bias_rows = jnp.zeros((2, D), f32)
    bias_rows = lax.dynamic_update_slice(
        bias_rows,
        jnp.stack([part_sums[0, :GROUP_FEATS], part_sums[0, 2 * GROUP_FEATS :]]),
        (0, head_group * GROUP_FEATS),
    )
    lanes = -(-part // small_cols) * small_cols
    bias_rows = jnp.pad(bias_rows.reshape(2, n_doc, part), ((0, 0), (0, 0), (0, lanes - part)))
    bias_rows = bias_rows.transpose(1, 0, 2).reshape(n_doc, -1, small_cols)
    bias_used = bias_rows.shape[1]
    bias_rows = jnp.pad(bias_rows, ((0, 0), (0, share - bias_used), (0, 0)))
    bias_rows = bias_rows.reshape(1, n_doc * share, small_cols).astype(half)
    bias_rows = jnp.pad(bias_rows, ((0, spread - 1), (0, 0), (0, 0)))
    grad_part = jnp.concatenate([grad_part, bias_rows], axis=2)
    grad_part = send_turns(grad_part, 0, spread, member, rotate_members)
    grad_part = sum(piece.astype(f32) for piece in grad_part).astype(half)

    grads = jnp.concatenate([over_seq, grad_part], axis=1)
    owned = jnp.concatenate([own_rows(grads), late_own], axis=1)
    param_grads = finish(n_seq, stack_n, lanes, lax.all_gather(owned, "seq", axis=0, tiled=True))
    (
        grad_w_qkv,
        grad_w_self_out,
        grad_w_cross_q,
        grad_w_cross_kv,
        grad_w_down,
        grad_w_in,
        grad_w_cross_out,
        grad_gains,
        grad_biases,
        grad_b_hidden,
    ) = param_grads
    grad_proj = from_heads(grad_proj_got)
    memory_grad = dot_tt(grad_mem_kv, w_cross_kv)[None]
    w_qkv = columns((2, 2), (3, 1), (3, 2))
    input_grad = (grad_r1 + dot_tt(grad_proj, w_qkv)).reshape(dec_input.shape)
    return (
        layer_out,
        input_grad,
        memory_grad,
        grad_w_qkv,
        grad_w_self_out,
        grad_w_cross_q,
        grad_w_cross_kv,
        grad_w_cross_out,
        grad_w_in,
        grad_b_hidden.reshape(-1),
        grad_w_down,
        grad_gains,
        grad_biases,
    )


def solution(mesh):
    placed = (
        P("doc", None, "seq", None),
        P("doc", "seq", None),
        P("doc", None),
        P("doc"),
        P("doc", None),
        P("doc", None),
        P("doc", None),
        P("doc", None),
        P("doc", None),
        P("doc", None),
        P("doc"),
        P("doc", None),
        P(None, "doc"),
        P(None, "doc"),
        P("doc", None, "seq", None),
    )
    return jax.shard_map(
        partial(body, mesh.shape["doc"], mesh.shape["seq"]),
        mesh=mesh,
        in_specs=placed,
        out_specs=(
            P("doc", None, "seq", None),
            P("doc", None, "seq", None),
            P("doc", "seq", None),
            P("doc", None),
            P("doc", None),
            P("doc", None),
            P("doc", None),
            P("doc", None),
            P("doc", None),
            P("doc"),
            P("doc", None),
            P(None, "doc"),
            P(None, "doc"),
        ),
        check_vma=False,
    )
```

```python
from functools import partial

import jax
import jax.numpy as jnp
from jax import lax
from jax.experimental import pallas as pl
from jax.experimental.pallas import tpu as pltpu
from jax.sharding import PartitionSpec as P

D = 768
HEADS = 12
HEAD_DIM = 64
HEAD_GROUPS = 4
GROUP_HEADS = HEADS // HEAD_GROUPS
GROUP_FEATS = GROUP_HEADS * HEAD_DIM

norm_eps = 1e-05
masked_score = -2e30
start_max = -1e30
score_scale = HEAD_DIM ** (-0.5)
forward_tile = 512
key_tile = 256
row_tile = 256
vmem_bytes = 56 * 2**20

f32 = jnp.float32
half = jnp.bfloat16


def cost_of(micros):
    return pl.CostEstimate(flops=micros * 10**9, bytes_accessed=micros * 10**6, transcendentals=0)


def layer_norm(resid_in, gain_row, shift_row):
    center = resid_in - jnp.mean(resid_in, axis=-1, keepdims=True)
    variance = jnp.mean(center * center, axis=-1, keepdims=True)
    return center * lax.rsqrt(variance + norm_eps) * gain_row + shift_row


def contract(left_op, right_op, left_dim, right_dim):
    return lax.dot_general(
        left_op,
        right_op,
        (((left_dim,), (right_dim,)), ((), ())),
        preferred_element_type=f32,
    )


def dot_nn(left_op, right_op):
    return contract(left_op, right_op, 1, 0)


def dot_nt(left_op, right_op):
    return contract(left_op, right_op, 1, 1)


def dot_tn(left_op, right_op):
    return contract(left_op, right_op, 0, 0)


def dot_tt(left_op, right_op):
    return contract(left_op, right_op, 0, 1)


def col_sums(grad_low):
    return jnp.sum(grad_low.astype(f32), axis=0)


def normalize(resid):
    center = resid - jnp.mean(resid, axis=-1, keepdims=True)
    scale = lax.rsqrt(jnp.mean(center * center, axis=-1, keepdims=True) + norm_eps)
    return center * scale, scale


def norm_backward(incoming, gain_row, unit, scale):
    grad = incoming * gain_row
    mean_one = jnp.mean(grad, axis=-1, keepdims=True)
    mean_two = jnp.mean(grad * unit, axis=-1, keepdims=True)
    return (grad - mean_one - unit * mean_two) * scale


def row_sum(grad):
    return jnp.sum(grad, axis=0, keepdims=True)


def store_rows(packed_ref, n_doc, grad, cols):
    n_seq, rows = packed_ref.shape[:2]
    share = rows // n_doc
    for s in range(n_seq):
        mine = [grad[(z * n_seq + s) * share : (z * n_seq + s + 1) * share] for z in range(n_doc)]
        packed_ref[s, :, cols] = jnp.concatenate(mine, axis=0).astype(half)


def head_feats(head, block=0):
    start = block * GROUP_FEATS + head * HEAD_DIM
    return slice(start, start + HEAD_DIM)


def load_rows(place_ref, piece_refs, x_ref, sems):
    spread = place_ref.shape[0] // HEAD_GROUPS
    slots = x_ref.shape[0]
    rows_dev = x_ref.shape[1] // place_ref.shape[0]
    member = place_ref[0] % spread
    copies = []
    for i in range(place_ref.shape[0]):
        turn_m, turn_h = i // HEAD_GROUPS, i % HEAD_GROUPS
        if turn_m:
            piece = piece_refs[HEAD_GROUPS + turn_m - 1].at[turn_h]
        else:
            piece = piece_refs[turn_h].at[pl.ds(member * slots, slots)]
        first = pl.multiple_of(place_ref[i] * rows_dev, rows_dev)
        copies.append(
            pltpu.make_async_copy(piece, x_ref.at[:, pl.ds(first, rows_dev)], sems.at[i])
        )
    for copy in copies:
        copy.start()
    for copy in copies:
        copy.wait()


def self_forward_kernel(place_ref, w_ref, bias_ref, *rest):
    pieces, (proj_ref, mix_ref, att_ref, lse_ref, x_ref, sems) = rest[:-6], rest[-6:]
    slot = pl.program_id(0)

    @pl.when(slot == 0)
    def _():
        load_rows(place_ref, pieces, x_ref, sems)

    length = proj_ref.shape[1]
    rows_dev = att_ref.shape[3]
    rows = min(row_tile, length)
    for first in range(0, length, rows):
        part = dot_nn(x_ref[slot, first : first + rows, :], w_ref[...]) + bias_ref[0:1, :]
        proj_ref[:, first : first + rows] = part.astype(half).T
    def score(head, first):
        upto = first + rows
        q_low = proj_ref[head_feats(head), first:upto] * jnp.asarray(score_scale, half)
        scores = dot_tn(proj_ref[head_feats(head, 1), :upto], q_low)
        key_pos = lax.broadcasted_iota(jnp.int32, scores.shape, 0)
        row_pos = first + lax.broadcasted_iota(jnp.int32, scores.shape, 1)
        return jnp.where(key_pos <= row_pos, scores, masked_score)

    def store(head, first, weight_low, top, total):
        feats, cols = head_feats(head), slice(first, first + rows)
        mix = dot_nn(proj_ref[head_feats(head, 2), : first + rows], weight_low) / total
        mix_ref[0, feats, cols] = mix
        mix_low = mix.astype(half)
        for place in range(rows // rows_dev):
            att_ref[first // rows_dev + place, 0, feats, :] = mix_low[
                :, place * rows_dev : (place + 1) * rows_dev
            ]
        lse_ref[0, head : head + 1, cols] = top + jnp.log(total)

    parts = [(head, first) for first in range(0, length, rows) for head in range(GROUP_HEADS)]
    ahead, waiting = score(*parts[0]), None
    for i, part in enumerate(parts):
        scores = ahead
        if i + 1 < len(parts):
            ahead = score(*parts[i + 1])
        top = jnp.max(scores, axis=0, keepdims=True)
        weight = jnp.exp(scores - top)
        total = jnp.sum(weight, axis=0, keepdims=True)
        if waiting is not None:
            store(*waiting)
        waiting = (*part, weight.astype(half), top, total)
    store(*waiting)


def self_forward(places, w_part, bias, pieces, n_seq, *after):
    slots = pieces[0].shape[0] * HEAD_GROUPS // n_seq
    length = pieces[0].shape[1] * n_seq
    feats, rows_dev = w_part.shape[1], length // n_seq
    return pl.pallas_call(
        self_forward_kernel,
        grid_spec=pltpu.PrefetchScalarGridSpec(
            num_scalar_prefetch=1,
            grid=(slots,),
            in_specs=[
                pl.BlockSpec(w_part.shape, lambda s, *_: (0, 0)),
                pl.BlockSpec(bias.shape, lambda s, *_: (0, 0)),
            ]
            + [pl.BlockSpec(memory_space=pl.ANY)] * (len(pieces) + len(after)),
            out_specs=[
                pl.BlockSpec((feats, length), lambda s, *_: (0, s)),
                pl.BlockSpec((1, GROUP_FEATS, length), lambda s, *_: (s, 0, 0)),
                pl.BlockSpec((n_seq, 1, GROUP_FEATS, rows_dev), lambda s, *_: (0, s, 0, 0)),
                pl.BlockSpec((1, GROUP_HEADS, length), lambda s, *_: (s, 0, 0)),
            ],
            scratch_shapes=[
                pltpu.VMEM((slots, length, D), half),
                pltpu.SemaphoreType.DMA((n_seq,)),
            ],
        ),
        out_shape=[
            jax.ShapeDtypeStruct((feats, slots * length), half),
            jax.ShapeDtypeStruct((slots, GROUP_FEATS, length), f32),
            jax.ShapeDtypeStruct((n_seq, slots, GROUP_FEATS, rows_dev), half),
            jax.ShapeDtypeStruct((slots, GROUP_HEADS, length), f32),
        ],
        compiler_params=pltpu.CompilerParams(vmem_limit_bytes=vmem_bytes),
        cost_estimate=cost_of(18),
        name="self_forward",
    )(places, w_part, bias, *pieces, *after)


def self_backward_kernel(n_doc, place_ref, proj_ref, grad_ref, mix_ref, lse_ref, *rest):
    ins, (send_ref, w_grad_ref, sums_ref, dproj_ref, dk_ref, dv_ref, w_acc, x_ref, sems) = (
        rest[:-9],
        rest[-9:],
    )
    pieces = ins[: HEAD_GROUPS + place_ref.shape[0] // HEAD_GROUPS - 1]
    slot = pl.program_id(0)

    @pl.when(slot == 0)
    def _():
        load_rows(place_ref, pieces, x_ref, sems)
        w_acc[...] = jnp.zeros_like(w_acc)
        sums_ref[...] = jnp.zeros_like(sums_ref)

    length = proj_ref.shape[1]
    n_seq, rows_dev = grad_ref.shape[0], grad_ref.shape[3]
    rows = min(row_tile, length)
    dk_ref[...] = jnp.zeros_like(dk_ref)
    dv_ref[...] = jnp.zeros_like(dv_ref)
    def products(head, first):
        upto = first + rows
        feats, cols = head_feats(head), slice(first, upto)
        places = range(first // rows_dev, upto // rows_dev)
        q_low = proj_ref[feats, cols] * jnp.asarray(score_scale, half)
        g_low = jnp.concatenate([grad_ref[place, 0, feats, :] for place in places], axis=1)
        delta = jnp.sum(g_low.astype(f32) * mix_ref[0, feats, cols], axis=0, keepdims=True)
        scores = dot_tn(proj_ref[head_feats(head, 1), :upto], q_low)
        key_pos = lax.broadcasted_iota(jnp.int32, scores.shape, 0)
        row_pos = first + lax.broadcasted_iota(jnp.int32, scores.shape, 1)
        scores = jnp.where(key_pos <= row_pos, scores, masked_score)
        return scores, dot_tn(proj_ref[head_feats(head, 2), :upto], g_low), q_low, g_low, delta

    def add(head, first, q_low, g_low, prob_low, grad_score):
        feats, upto = head_feats(head), first + rows
        dv_ref[feats, :upto] += dot_nt(g_low, prob_low)
        dk_ref[feats, :upto] += dot_nt(q_low, grad_score)
        grad_query = dot_nn(proj_ref[head_feats(head, 1), :upto], grad_score) * score_scale
        dproj_ref[feats, first:upto] = grad_query.astype(half)

    parts = [(head, first) for first in range(0, length, rows) for head in range(GROUP_HEADS)]
    ahead, waiting = products(*parts[0]), None
    for i, (head, first) in enumerate(parts):
        scores, grad_prob, q_low, g_low, delta = ahead
        if i + 1 < len(parts):
            ahead = products(*parts[i + 1])
        prob = jnp.exp(scores - lse_ref[0, head : head + 1, first : first + rows])
        grad_score = (prob * (grad_prob - delta)).astype(half)
        if waiting is not None:
            add(*waiting)
        waiting = (head, first, q_low, g_low, prob.astype(half), grad_score)
    add(*waiting)
    dproj_ref[GROUP_FEATS : 2 * GROUP_FEATS, :] = dk_ref[...].astype(half)
    dproj_ref[2 * GROUP_FEATS :, :] = dv_ref[...].astype(half)
    for place in range(n_seq):
        send_ref[place, 0] = dproj_ref[:, place * rows_dev : (place + 1) * rows_dev]
    for first in range(0, length, rows):
        turned = dproj_ref[:, first : first + rows].T
        sums_ref[0:1, :] += row_sum(turned.astype(f32))
        w_acc[...] += dot_tn(x_ref[slot, first : first + rows, :], turned)

    @pl.when(slot == pl.num_programs(0) - 1)
    def _():
        spread, stored, width = w_grad_ref.shape
        share = stored // n_doc
        feats = dproj_ref.shape[0]
        quarters = width // feats
        for m in range(spread):
            for q in range(quarters):
                mine = []
                for z in range(n_doc):
                    first = ((z * spread + m) * quarters + q) * share
                    mine.append(w_acc[first : first + share, :])
                w_grad_ref[m, :, q * feats : (q + 1) * feats] = jnp.concatenate(
                    mine, axis=0
                ).astype(half)


def self_backward(n_doc, places, proj, grad_mix, mix, lse, pieces, *after):
    n_seq, slots, _, rows_dev = grad_mix.shape
    feats, length = proj.shape[0], n_seq * rows_dev
    spread = n_seq // HEAD_GROUPS
    stored = D // n_seq
    return pl.pallas_call(
        partial(self_backward_kernel, n_doc),
        grid_spec=pltpu.PrefetchScalarGridSpec(
            num_scalar_prefetch=1,
            grid=(slots,),
            in_specs=[
                pl.BlockSpec((feats, length), lambda s, *_: (0, s)),
                pl.BlockSpec((n_seq, 1, GROUP_FEATS, rows_dev), lambda s, *_: (0, s, 0, 0)),
                pl.BlockSpec((1, GROUP_FEATS, length), lambda s, *_: (s, 0, 0)),
                pl.BlockSpec((1, GROUP_HEADS, length), lambda s, *_: (s, 0, 0)),
            ]
            + [pl.BlockSpec(memory_space=pl.ANY)] * (len(pieces) + len(after)),
            out_specs=[
                pl.BlockSpec((n_seq, 1, feats, rows_dev), lambda s, *_: (0, s, 0, 0)),
                pl.BlockSpec((spread, stored, HEAD_GROUPS * feats), lambda s, *_: (0, 0, 0)),
                pl.BlockSpec((8, feats), lambda s, *_: (0, 0)),
            ],
            scratch_shapes=[
                pltpu.VMEM((feats, length), half),
                pltpu.VMEM((GROUP_FEATS, length), f32),
                pltpu.VMEM((GROUP_FEATS, length), f32),
                pltpu.VMEM((D, feats), f32),
                pltpu.VMEM((slots, length, D), half),
                pltpu.SemaphoreType.DMA((n_seq,)),
            ],
        ),
        out_shape=[
            jax.ShapeDtypeStruct((n_seq, slots, feats, rows_dev), half),
            jax.ShapeDtypeStruct((spread, stored, HEAD_GROUPS * feats), half),
            jax.ShapeDtypeStruct((8, feats), f32),
        ],
        compiler_params=pltpu.CompilerParams(vmem_limit_bytes=vmem_bytes),
        cost_estimate=cost_of(20),
        name="self_backward",
    )(places, proj, grad_mix, mix, lse, *pieces, *after)


def enter_kernel(att_ref, x_ref, vec_ref, w_ref, norm_ref, unit_ref, scale_ref, send_ref, att_all):
    gather_att(att_ref, att_all)
    slots, rows_dev = send_ref.shape[1], send_ref.shape[3]
    rows = min(middle_rows, x_ref.shape[0])
    for first in range(0, x_ref.shape[0], rows):
        where = slice(first, first + rows)
        branch = dot_tn(att_all[:, where], w_ref[:, :D]) + vec_ref[0:1, :]
        unit, scale = normalize(x_ref[where, :].astype(f32) + branch)
        norm = unit * vec_ref[1:2, :] + vec_ref[2:3, :]
        norm_ref[where, :] = norm
        unit_ref[where, :] = unit
        scale_ref[where, :] = jnp.broadcast_to(scale, (rows, scale_ref.shape[1]))
        query = dot_nn(norm.astype(half), w_ref[:, D:]) + vec_ref[3:4, :]
        query = query.astype(half).T
        for group in range(HEAD_GROUPS):
            for place in range(rows // rows_dev):
                send_ref[group, first // rows_dev + place] = query[
                    group * GROUP_FEATS : (group + 1) * GROUP_FEATS,
                    place * rows_dev : (place + 1) * rows_dev,
                ]


def gather_att(att_ref, att_all):
    n_seq, member_slots, _, rows_dev = att_ref.shape
    spread = n_seq // HEAD_GROUPS
    for source in range(n_seq):
        group, m = source // spread, source % spread
        for inner in range(member_slots):
            slot = m * member_slots + inner
            att_all[
                group * GROUP_FEATS : (group + 1) * GROUP_FEATS,
                slot * rows_dev : (slot + 1) * rows_dev,
            ] = att_ref[source, inner]


def enter(att, x_low, vectors, w_pair, slots):
    rows_total, rows_dev = x_low.shape[0], att.shape[3]
    vmem = pl.BlockSpec(memory_space=pltpu.VMEM)
    return pl.pallas_call(
        enter_kernel,
        in_specs=[vmem] * 4,
        out_specs=[vmem] * 4,
        out_shape=[
            jax.ShapeDtypeStruct((rows_total, D), f32),
            jax.ShapeDtypeStruct((rows_total, D), f32),
            jax.ShapeDtypeStruct((rows_total, 128), f32),
            jax.ShapeDtypeStruct((HEAD_GROUPS, slots, GROUP_FEATS, rows_dev), half),
        ],
        scratch_shapes=[pltpu.VMEM((D, rows_total), half)],
        compiler_params=pltpu.CompilerParams(vmem_limit_bytes=vmem_bytes),
        cost_estimate=cost_of(6),
        name="enter",
    )(att, x_low, vectors, w_pair)


def leave_kernel(
    n_doc,
    query_ref,
    att_ref,
    resid_ref,
    norm_ref,
    unit_ref,
    scale_ref,
    vec_ref,
    w_ref,
    mem_ref,
    rows_a_ref,
    rows_b_ref,
    rows_c_ref,
    out_ref,
    send_ref,
    packed_ref,
    att_all,
    query_all,
    query_rows,
    low_rows,
    sums_ref,
):
    slots, rows_dev = query_ref.shape[1], query_ref.shape[3]
    member_slots = att_ref.shape[1]
    spread = slots // member_slots
    rows_total = resid_ref.shape[0]
    rows = min(middle_rows, rows_total)
    gather_att(att_ref, att_all)
    for group in range(HEAD_GROUPS):
        for slot in range(slots):
            query_all[
                group * GROUP_FEATS : (group + 1) * GROUP_FEATS,
                slot * rows_dev : (slot + 1) * rows_dev,
            ] = query_ref[group, slot]
    sums_ref[...] = jnp.zeros_like(sums_ref)
    for first in range(0, rows_total, rows):
        where = slice(first, first + rows)
        query = query_all[:, where].T
        query_rows[where, :] = query
        sums_ref[3:4, :] += row_sum(query.astype(f32))
        incoming = resid_ref[where, :] + dot_nt(query, w_ref[:, D:])
        unit = unit_ref[where, :]
        sums_ref[0:1, :] += row_sum(incoming * unit)
        sums_ref[1:2, :] += row_sum(incoming)
        grad = norm_backward(incoming, vec_ref[1:2, :], unit, scale_ref[where, 0:1])
        out_ref[where, :] = grad
        grad_low = grad.astype(half)
        low_rows[where, :] = grad_low
        sums_ref[2:3, :] += row_sum(grad_low.astype(f32))
    grad_att = dot_nt(w_ref[:, :D], low_rows[...]).astype(half)
    for target in range(HEAD_GROUPS * spread):
        group, m = target // spread, target % spread
        for inner in range(member_slots):
            slot = m * member_slots + inner
            send_ref[target, inner] = grad_att[
                group * GROUP_FEATS : (group + 1) * GROUP_FEATS,
                slot * rows_dev : (slot + 1) * rows_dev,
            ]
    store_rows(packed_ref, n_doc, dot_nn(att_all[...], low_rows[...]), slice(0, D))
    grad = dot_tn(norm_ref[...].astype(half), query_rows[...])
    store_rows(packed_ref, n_doc, grad, slice(D, 2 * D))
    packed_ref[:, :, 2 * D : 4 * D] = mem_ref[...]
    small = [sums_ref[...], rows_a_ref[...], rows_b_ref[...], rows_c_ref[0:1, :]]
    used = sum(rows.shape[0] for rows in small)
    small.append(jnp.zeros((small_cols - used, D), f32))
    store_rows(
        packed_ref, n_doc, jnp.concatenate(small, axis=0).T, slice(4 * D, 4 * D + small_cols)
    )


def leave(n_doc, grad_query, att, resid, norm_one, unit, scale, vectors, w_pair, *others):
    rows_total, n_seq = resid.shape[0], att.shape[0]
    vmem = pl.BlockSpec(memory_space=pltpu.VMEM)
    return pl.pallas_call(
        partial(leave_kernel, n_doc),
        in_specs=[vmem] * (8 + len(others)),
        out_specs=[vmem] * 3,
        out_shape=[
            jax.ShapeDtypeStruct((rows_total, D), f32),
            jax.ShapeDtypeStruct(att.shape, half),
            jax.ShapeDtypeStruct((n_seq, D // n_seq, 4 * D + small_cols), half),
        ],
        scratch_shapes=[
            pltpu.VMEM((D, rows_total), half),
            pltpu.VMEM((D, rows_total), half),
            pltpu.VMEM((rows_total, D), half),
            pltpu.VMEM((rows_total, D), half),
            pltpu.VMEM((8, D), f32),
        ],
        compiler_params=pltpu.CompilerParams(vmem_limit_bytes=vmem_bytes),
        cost_estimate=cost_of(8),
        name="leave",
    )(grad_query, att, resid, norm_one, unit, scale, vectors, w_pair, *others)


def memory_kernel(n_doc, place_ref, mem_ref, *rest):
    pieces, (packed_ref, all_ref, sums_ref) = rest[: place_ref.shape[0]], rest[-3:]
    for turn, piece in enumerate(pieces):
        for kind in range(2):
            first = pl.multiple_of(kind * D + place_ref[turn] * GROUP_FEATS, GROUP_FEATS)
            all_ref[pl.ds(first, GROUP_FEATS), :] = piece[kind]
    turned = all_ref[...].T
    for kind in range(2):
        cols = slice(kind * D, (kind + 1) * D)
        store_rows(packed_ref, n_doc, dot_tn(mem_ref[...], turned[:, cols]), cols)
    sums_ref[...] = jnp.broadcast_to(row_sum(turned[:, D:].astype(f32)), sums_ref.shape)


small_cols = 128


def memory_backward(n_doc, n_seq, places, mem_low, pieces):
    tokens = mem_low.shape[0]
    vmem = pl.BlockSpec(memory_space=pltpu.VMEM)
    return pl.pallas_call(
        partial(memory_kernel, n_doc),
        grid_spec=pltpu.PrefetchScalarGridSpec(
            num_scalar_prefetch=1,
            grid=(1,),
            in_specs=[vmem] * (1 + len(pieces)),
            out_specs=[vmem] * 3,
        ),
        out_shape=[
            jax.ShapeDtypeStruct((n_seq, D // n_seq, 2 * D), half),
            jax.ShapeDtypeStruct((2 * D, tokens), half),
            jax.ShapeDtypeStruct((8, D), f32),
        ],
        compiler_params=pltpu.CompilerParams(vmem_limit_bytes=vmem_bytes),
        cost_estimate=cost_of(7),
        name="memory_backward",
    )(places, mem_low, *pieces)


def finish_kernel(
    n_seq,
    stack_n,
    lanes,
    in_ref,
    qkv_ref,
    out_ref,
    q_ref,
    kv_ref,
    down_ref,
    ffn_ref,
    cross_ref,
    gains_ref,
    biases_ref,
    hidden_ref,
):
    rows = in_ref.shape[0]
    share = rows // n_seq
    spread = n_seq // HEAD_GROUPS
    out_ref[...] = in_ref[:, :D].astype(f32)
    q_ref[...] = in_ref[:, D : 2 * D].astype(f32)
    kv_ref[...] = in_ref[:, 2 * D : 4 * D].astype(f32)
    small = in_ref[:, 4 * D : 4 * D + small_cols].astype(f32).T
    first_col = 4 * D + small_cols
    feats = 3 * GROUP_FEATS
    ff = ffn_ref.shape[1]
    down_col = first_col + HEAD_GROUPS * feats + small_cols
    ffn_col = down_col + stack_n * D
    ffn_ref[...] = in_ref[:, ffn_col : ffn_col + ff].astype(f32)
    cross_ref[...] = in_ref[:, ffn_col + ff :].astype(f32)
    for q in range(stack_n):
        mine = in_ref[:, down_col + q * D : down_col + (q + 1) * D].astype(f32)
        for s in range(n_seq):
            first = (s * stack_n + q) * share
            down_ref[first : first + share, :] = mine[s * share : (s + 1) * share]
    bias = jnp.zeros((share, small_cols), f32)
    wide = in_ref[:, first_col:down_col].astype(f32)
    for s in range(n_seq):
        group, m = s // spread, s % spread
        mine = wide[s * share : (s + 1) * share]
        for q in range(HEAD_GROUPS):
            first = (m * HEAD_GROUPS + q) * share
            for part in range(3):
                start = q * feats + part * GROUP_FEATS
                qkv_ref[
                    first : first + share,
                    part * D + group * GROUP_FEATS : part * D + (group + 1) * GROUP_FEATS,
                ] = mine[:, start : start + GROUP_FEATS]
        bias = bias + mine[:, HEAD_GROUPS * feats :]
    for row, source in enumerate((0, 8, 10)):
        gains_ref[row : row + 1, :] = small[source : source + 1]
    for row, source in ((2, 2), (3, 3), (4, 16 + stack_n), (5, 12), (6, 13), (7, 1), (8, 9), (9, 11)):
        biases_ref[row : row + 1, :] = small[source : source + 1]
    hidden_ref[...] = small[16 : 16 + stack_n]
    per_row = lanes // small_cols
    for row in range(2):
        found = [bias[row * per_row + i : row * per_row + i + 1] for i in range(per_row)]
        biases_ref[row : row + 1, :] = jnp.concatenate(found, axis=1)[:, :rows]


def finish(n_seq, stack_n, lanes, packed):
    rows = packed.shape[0]
    vmem = pl.BlockSpec(memory_space=pltpu.VMEM)
    return pl.pallas_call(
        partial(finish_kernel, n_seq, stack_n, lanes),
        in_specs=[vmem],
        out_specs=[vmem] * 10,
        out_shape=[
            jax.ShapeDtypeStruct((rows, 3 * D), f32),
            jax.ShapeDtypeStruct((rows, D), f32),
            jax.ShapeDtypeStruct((rows, D), f32),
            jax.ShapeDtypeStruct((rows, 2 * D), f32),
            jax.ShapeDtypeStruct((rows * stack_n, D), f32),
            jax.ShapeDtypeStruct((rows, stack_n * D), f32),
            jax.ShapeDtypeStruct((rows, D), f32),
            jax.ShapeDtypeStruct((3, rows), f32),
            jax.ShapeDtypeStruct((10, rows), f32),
            jax.ShapeDtypeStruct((stack_n, rows), f32),
        ],
        compiler_params=pltpu.CompilerParams(vmem_limit_bytes=vmem_bytes),
        cost_estimate=cost_of(6),
        name="finish",
    )(packed)


def load_pieces(place_ref, piece_refs, kv_ref, sems):
    tokens = piece_refs[0].shape[2]
    copies = [
        pltpu.make_async_copy(
            piece,
            kv_ref.at[:, :, pl.ds(pl.multiple_of(place_ref[i] * tokens, tokens), tokens)],
            sems.at[i],
        )
        for i, piece in enumerate(piece_refs)
    ]
    for copy in copies:
        copy.start()
    for copy in copies:
        copy.wait()


def tiles_of(low, high, tile):
    first = low // tile
    return first, jnp.where(high > low, (high + tile - 1) // tile, first)


def cross_forward_kernel(low_ref, high_ref, place_ref, q_ref, *rest):
    pieces, (mix_ref, att_ref, lse_ref, acc_ref, kv_ref, sems) = rest[:-6], rest[-6:]
    slot = pl.program_id(0)

    @pl.when(slot == 0)
    def _():
        load_pieces(place_ref, pieces, kv_ref, sems)

    low, high = low_ref[slot], high_ref[slot]
    rows_dev = q_ref.shape[3]
    q_low = jnp.concatenate([q_ref[i, 0] for i in range(HEAD_GROUPS)], axis=1)
    q_low = q_low * jnp.asarray(score_scale, half)
    rows = q_low.shape[1]
    acc_ref[...] = jnp.zeros_like(acc_ref)

    def step(tile, carry):
        tops, totals = carry
        start = pl.multiple_of(tile * forward_tile, forward_tile)
        keys = pl.ds(start, forward_tile)
        key_pos = start + lax.broadcasted_iota(jnp.int32, (forward_tile, rows), 0)
        counted = (key_pos >= low) & (key_pos < high)

        def score(head):
            feats = head_feats(head)
            return jnp.where(counted, dot_tn(kv_ref[0, feats, keys], q_low[feats]), masked_score)

        def add(head, weight_low, rescale):
            feats = head_feats(head)
            mixed = dot_nn(kv_ref[1, feats, keys], weight_low)
            acc_ref[feats, :] = acc_ref[feats, :] * rescale + mixed

        new_tops, new_totals = [], []
        ahead, waiting = score(0), None
        for head in range(GROUP_HEADS):
            scores = ahead
            if head + 1 < GROUP_HEADS:
                ahead = score(head + 1)
            top = jnp.maximum(tops[head], jnp.max(scores, axis=0, keepdims=True))
            weight = jnp.exp(scores - top)
            rescale = jnp.exp(tops[head] - top)
            new_totals.append(totals[head] * rescale + jnp.sum(weight, axis=0, keepdims=True))
            new_tops.append(top)
            if waiting is not None:
                add(*waiting)
            waiting = (head, weight.astype(half), rescale)
        add(*waiting)
        return (tuple(new_tops), tuple(new_totals))

    init = (
        tuple(jnp.full((1, rows), start_max, f32) for _ in range(GROUP_HEADS)),
        tuple(jnp.zeros((1, rows), f32) for _ in range(GROUP_HEADS)),
    )
    tops, totals = lax.fori_loop(*tiles_of(low, high, forward_tile), step, init)
    for head in range(GROUP_HEADS):
        feats = head_feats(head)
        live = totals[head] > 0
        total = jnp.where(live, totals[head], 1.0)
        mix = acc_ref[feats, :] / total
        mix_ref[0, feats, :] = mix
        mix_low = mix.astype(half)
        for i in range(HEAD_GROUPS):
            att_ref[i, 0, feats, :] = mix_low[:, i * rows_dev : (i + 1) * rows_dev]
        lse_ref[0, head : head + 1, :] = jnp.where(live, tops[head] + jnp.log(total), 0.0)


def cross_forward(low, high, places, queries, pieces):
    groups, slots, feats, rows_dev = queries.shape
    rows = groups * rows_dev
    tokens = pieces[0].shape[2] * len(pieces)
    row_block = pl.BlockSpec((groups, 1, feats, rows_dev), lambda s, *_: (0, s, 0, 0))
    return pl.pallas_call(
        cross_forward_kernel,
        grid_spec=pltpu.PrefetchScalarGridSpec(
            num_scalar_prefetch=3,
            grid=(slots,),
            in_specs=[row_block] + [pl.BlockSpec(memory_space=pl.ANY)] * len(pieces),
            out_specs=[
                pl.BlockSpec((1, feats, rows), lambda s, *_: (s, 0, 0)),
                row_block,
                pl.BlockSpec((1, GROUP_HEADS, rows), lambda s, *_: (s, 0, 0)),
            ],
            scratch_shapes=[
                pltpu.VMEM((feats, rows), f32),
                pltpu.VMEM((2, feats, tokens), half),
                pltpu.SemaphoreType.DMA((len(pieces),)),
            ],
        ),
        out_shape=[
            jax.ShapeDtypeStruct((slots, feats, rows), f32),
            jax.ShapeDtypeStruct(queries.shape, half),
            jax.ShapeDtypeStruct((slots, GROUP_HEADS, rows), f32),
        ],
        compiler_params=pltpu.CompilerParams(vmem_limit_bytes=vmem_bytes),
        cost_estimate=cost_of(33),
        name="cross_forward",
    )(low, high, places, queries, *pieces)


def cross_backward_kernel(
    low_ref, high_ref, place_ref, q_ref, g_ref, mix_ref, lse_ref, *rest
):
    count = place_ref.shape[0]
    spread = count // HEAD_GROUPS
    pieces = rest[:count]
    dq_ref, *dkv_outs = rest[-5 - spread : -4]
    dkv_ref, acc_ref, kv_ref, sems = rest[-4:]
    member = place_ref[0] % spread
    slot = pl.program_id(0)

    @pl.when(slot == 0)
    def _():
        dkv_ref[...] = jnp.zeros_like(dkv_ref)
        load_pieces(place_ref, pieces, kv_ref, sems)

    low, high = low_ref[slot], high_ref[slot]
    rows_dev = q_ref.shape[3]
    tiles_dev = dkv_ref.shape[4] // key_tile
    q_low = jnp.concatenate([q_ref[i, 0] for i in range(HEAD_GROUPS)], axis=1)
    q_low = q_low * jnp.asarray(score_scale, half)
    g_low = jnp.concatenate([g_ref[i, 0] for i in range(HEAD_GROUPS)], axis=1)
    rows = q_low.shape[1]
    acc_ref[...] = jnp.zeros_like(acc_ref)
    product = g_low.astype(f32) * mix_ref[0]
    delta = [jnp.sum(product[head_feats(h)], axis=0, keepdims=True) for h in range(GROUP_HEADS)]
    lse = [lse_ref[0, h : h + 1, :] for h in range(GROUP_HEADS)]

    def step(tile, carry):
        start = pl.multiple_of(tile * key_tile, key_tile)
        owner = tile // tiles_dev
        turn, group = (owner - member + spread) % spread, owner // spread
        inside = pl.multiple_of(tile % tiles_dev * key_tile, key_tile)
        key_pos = start + lax.broadcasted_iota(jnp.int32, (key_tile, rows), 0)
        counted = (key_pos >= low) & (key_pos < high)
        keys = pl.ds(start, key_tile)

        def products(head):
            feats = head_feats(head)
            scores = dot_tn(kv_ref[0, feats, keys], q_low[feats])
            return scores, dot_tn(kv_ref[1, feats, keys], g_low[feats])

        def add(head, prob_low, grad_score):
            feats = head_feats(head)
            own_keys = (feats, pl.ds(inside, key_tile))
            grad_values = dot_nt(prob_low, g_low[feats]).T
            grad_keys = dot_nt(grad_score, q_low[feats]).T
            dkv_ref[(turn, group, 1, *own_keys)] += grad_values.astype(half)
            dkv_ref[(turn, group, 0, *own_keys)] += grad_keys.astype(half)
            acc_ref[feats, :] += dot_nn(kv_ref[0, feats, keys], grad_score)

        ahead, waiting = products(0), None
        for head in range(GROUP_HEADS):
            scores, grad_prob = ahead
            if head + 1 < GROUP_HEADS:
                ahead = products(head + 1)
            prob = jnp.exp(jnp.where(counted, scores, masked_score) - lse[head])
            grad_score = (prob * (grad_prob - delta[head])).astype(half)
            if waiting is not None:
                add(*waiting)
            waiting = (head, prob.astype(half), grad_score)
        add(*waiting)
        return carry

    lax.fori_loop(*tiles_of(low, high, key_tile), step, 0)
    dq_low = (acc_ref[...] * score_scale).astype(half)
    for i in range(HEAD_GROUPS):
        dq_ref[i, 0] = dq_low[:, i * rows_dev : (i + 1) * rows_dev]

    @pl.when(slot == pl.num_programs(0) - 1)
    def _():
        copies = [
            pltpu.make_async_copy(dkv_ref.at[turn], out, sems.at[turn])
            for turn, out in enumerate(dkv_outs)
        ]
        for copy in copies:
            copy.start()
        for copy in copies:
            copy.wait()


def cross_backward(low, high, places, queries, grad_mix, mix, lse, pieces, *after):
    groups, slots, feats, rows_dev = queries.shape
    rows = groups * rows_dev
    tokens = pieces[0].shape[2]
    row_block = pl.BlockSpec((groups, 1, feats, rows_dev), lambda s, *_: (0, s, 0, 0))
    grad_shape = (len(pieces) // groups, groups, 2, feats, tokens)
    return pl.pallas_call(
        cross_backward_kernel,
        grid_spec=pltpu.PrefetchScalarGridSpec(
            num_scalar_prefetch=3,
            grid=(slots,),
            in_specs=[
                row_block,
                row_block,
                pl.BlockSpec((1, feats, rows), lambda s, *_: (s, 0, 0)),
                pl.BlockSpec((1, GROUP_HEADS, rows), lambda s, *_: (s, 0, 0)),
            ]
            + [pl.BlockSpec(memory_space=pl.ANY)] * (len(pieces) + len(after)),
            out_specs=[row_block] + [pl.BlockSpec(memory_space=pl.ANY)] * grad_shape[0],
            scratch_shapes=[
                pltpu.VMEM(grad_shape, half),
                pltpu.VMEM((feats, rows), f32),
                pltpu.VMEM((2, feats, tokens * len(pieces)), half),
                pltpu.SemaphoreType.DMA((len(pieces),)),
            ],
        ),
        out_shape=[
            jax.ShapeDtypeStruct(queries.shape, half),
        ]
        + [jax.ShapeDtypeStruct(grad_shape[1:], half)] * grad_shape[0],
        compiler_params=pltpu.CompilerParams(vmem_limit_bytes=vmem_bytes),
        cost_estimate=cost_of(49),
        name="cross_backward",
    )(low, high, places, queries, grad_mix, mix, lse, *pieces, *after)


middle_rows = 256


def middle_kernel(
    n_doc,
    n_seq,
    att_ref,
    norm_ref,
    out_grad_ref,
    vec_ref,
    bias_ref,
    *rest,
):
    weights = rest[:-17]
    out_ref, resid_ref, send_ref, packed_ref, sums_ref, bias_grad_ref = rest[-17:-11]
    att_all, w_cross, w_in, w_out, norm_low, active = rest[-11:-5]
    slope, low_three, hidden_grad, low_two, sems = rest[-5:]
    slots, rows_dev = att_ref.shape[1], att_ref.shape[3]
    rows_total = slots * rows_dev
    rows = min(middle_rows, rows_total)
    ff = w_out.shape[0]
    chunk = ff // n_doc
    copies = []

    def copy_block(block, block_col, target, row, col):
        rows = pl.ds(block * block_rows, block_rows)
        copies.append(
            pltpu.make_async_copy(
                w_ref.at[rows, pl.ds(block_col * D, D)],
                target.at[pl.ds(row, block_rows), pl.ds(col, D)],
                sems.at[len(copies)],
            )
        )

    blocks = n_doc * n_seq
    block_rows = ff // blocks
    if len(weights) == 1:
        (w_ref,) = weights
        for band in range(blocks // 4):
            row = band * block_rows
            copy_block(4 * band, 1, w_cross, row, 0)
            for at, (block_col, block) in enumerate([(2, 0), (1, 1), (2, 1), (1, 2)]):
                copy_block(4 * band + block, block_col, w_in, row, at * D)
        for block in range(blocks):
            copy_block(block, 0, w_out, block * block_rows, 0)
    else:
        for i, (weight, target) in enumerate(zip(weights, (w_cross, w_in, w_out))):
            copies.append(pltpu.make_async_copy(weight, target, sems.at[i]))
    for copy in copies:
        copy.start()
    for group in range(HEAD_GROUPS):
        for slot in range(slots):
            att_all[
                group * GROUP_FEATS : (group + 1) * GROUP_FEATS,
                slot * rows_dev : (slot + 1) * rows_dev,
            ] = att_ref[group, slot]
    sums_ref[...] = jnp.zeros_like(sums_ref)
    bias_grad_ref[...] = jnp.zeros_like(bias_grad_ref)
    for copy in copies:
        copy.wait()

    def row_block(block, carry):
        where = pl.ds(pl.multiple_of(block * rows, rows), rows)
        gain_two, shift_two = vec_ref[0:1, :], vec_ref[1:2, :]
        gain_three, shift_three = vec_ref[2:3, :], vec_ref[3:4, :]
        branch = dot_tn(att_all[:, where], w_cross[...]) + vec_ref[4:5, :]
        unit_two, scale_two = normalize(norm_ref[where, :] + branch)
        norm_two = unit_two * gain_two + shift_two
        norm_two_low = norm_two.astype(half)
        norm_low[where, :] = norm_two_low
        branch = vec_ref[5:6, :]
        for z in range(n_doc):
            cols = slice(z * chunk, (z + 1) * chunk)
            hidden = dot_nn(norm_two_low, w_in[:, cols]) + bias_ref[:, cols]
            below = 0.5 + 0.5 * lax.erf(hidden * (0.5**0.5))
            density = jnp.exp(-0.5 * hidden * hidden) * 0.3989422804014327
            slope[:, cols] = below + hidden * density
            active_low = (hidden * below).astype(half)
            active[where, cols] = active_low
            branch = branch + dot_nn(active_low, w_out[cols, :])
        unit_three, scale_three = normalize(norm_two + branch)
        out_ref[where, :] = (unit_three * gain_three + shift_three).astype(half)
        incoming = out_grad_ref[where, :].astype(f32)
        sums_ref[2:3, :] += row_sum(incoming * unit_three)
        sums_ref[3:4, :] += row_sum(incoming)
        grad_three = norm_backward(incoming, gain_three, unit_three, scale_three)
        grad_low = grad_three.astype(half)
        low_three[where, :] = grad_low
        sums_ref[5:6, :] += row_sum(grad_low.astype(f32))
        incoming = grad_three
        for z in range(n_doc):
            cols = slice(z * chunk, (z + 1) * chunk)
            hidden_low = (dot_nt(grad_low, w_out[cols, :]) * slope[:, cols]).astype(half)
            hidden_grad[where, cols] = hidden_low
            bias_grad_ref[:, cols] += row_sum(hidden_low.astype(f32))
            incoming = incoming + dot_nt(hidden_low, w_in[:, cols])
        sums_ref[0:1, :] += row_sum(incoming * unit_two)
        sums_ref[1:2, :] += row_sum(incoming)
        grad_two = norm_backward(incoming, gain_two, unit_two, scale_two)
        resid_ref[where, :] = grad_two
        grad_low = grad_two.astype(half)
        low_two[where, :] = grad_low
        sums_ref[4:5, :] += row_sum(grad_low.astype(f32))
        return carry

    lax.fori_loop(0, rows_total // rows, row_block, 0)

    grad_att = dot_nt(w_cross[...], low_two[...]).astype(half)
    for group in range(HEAD_GROUPS):
        for slot in range(slots):
            send_ref[group, slot] = grad_att[
                group * GROUP_FEATS : (group + 1) * GROUP_FEATS,
                slot * rows_dev : (slot + 1) * rows_dev,
            ]

    share = D // (n_doc * n_seq)
    stack_n = chunk // (share * n_seq)

    store_rows(packed_ref, n_doc, dot_nn(att_all[...], low_two[...]), slice(2 * ff, 2 * ff + D))
    for z in range(n_doc):
        cols = slice(z * chunk, (z + 1) * chunk)
        grad = dot_tn(norm_low[...], hidden_grad[:, cols])
        store_rows(packed_ref, n_doc, grad, slice(ff + z * chunk, ff + (z + 1) * chunk))
    for pair in range(n_doc // 2):
        grads = []
        for z in (2 * pair, 2 * pair + 1):
            cols = slice(z * chunk, (z + 1) * chunk)
            grads.append(dot_tn(active[:, cols], low_three[...]))
        for s in range(n_seq):
            for q in range(stack_n):
                first = (s * stack_n + q) * share
                mine = [grad[first : first + share] for grad in grads]
                packed_ref[
                    s, pair * 2 * share : (pair + 1) * 2 * share, q * D : (q + 1) * D
                ] = jnp.concatenate(mine, axis=0).astype(half)


def middle(n_doc, n_seq, att, norm_one, out_grad, vectors, bias, weights):
    groups, slots, feats, rows_dev = att.shape
    rows_total = slots * rows_dev
    ff = weights[-1].shape[0]
    share = D // (n_doc * n_seq)
    vmem = pl.BlockSpec(memory_space=pltpu.VMEM)
    hbm = pl.BlockSpec(memory_space=pl.ANY)
    return pl.pallas_call(
        partial(middle_kernel, n_doc, n_seq),
        in_specs=[vmem] * 5 + [hbm] * len(weights),
        out_specs=[vmem] * 6,
        out_shape=[
            jax.ShapeDtypeStruct((rows_total, D), half),
            jax.ShapeDtypeStruct((rows_total, D), f32),
            jax.ShapeDtypeStruct(att.shape, half),
            jax.ShapeDtypeStruct((n_seq, n_doc * share, 2 * ff + D), half),
            jax.ShapeDtypeStruct((8, D), f32),
            jax.ShapeDtypeStruct((1, ff), f32),
        ],
        scratch_shapes=[
            pltpu.VMEM((D, rows_total), half),
            pltpu.VMEM((D, D), half),
            pltpu.VMEM((D, ff), half),
            pltpu.VMEM((ff, D), half),
            pltpu.VMEM((rows_total, D), half),
            pltpu.VMEM((rows_total, ff), half),
            pltpu.VMEM((min(middle_rows, rows_total), ff), f32),
            pltpu.VMEM((rows_total, D), half),
            pltpu.VMEM((rows_total, ff), half),
            pltpu.VMEM((rows_total, D), half),
            pltpu.SemaphoreType.DMA((n_doc * n_seq * 9 // 4,)),
        ],
        compiler_params=pltpu.CompilerParams(vmem_limit_bytes=vmem_bytes),
        cost_estimate=cost_of(31),
        name="middle",
    )(att, norm_one, out_grad, vectors, bias, *weights)


def body(
    n_doc,
    n_seq,
    dec_input,
    memory,
    doc_lengths,
    doc_count,
    self_qkv,
    self_out,
    cross_q,
    cross_kv,
    cross_out,
    ffn_in,
    ffn_in_bias,
    ffn_out,
    norm_gains,
    biases,
    out_grad,
):
    seq_index = lax.axis_index("seq")
    doc_index = lax.axis_index("doc")
    slots_n, rows_dev = dec_input.shape[1:3]
    rows_total = slots_n * rows_dev
    mem_rows = memory.shape[1]
    spread = n_seq // HEAD_GROUPS
    head_group = seq_index // spread
    member = seq_index % spread
    member_slots = slots_n // spread
    dec_len = rows_dev * n_seq
    same_member = [[h * spread + m for h in range(HEAD_GROUPS)] for m in range(spread)]

    def swap_heads(blocks):
        return lax.all_to_all(blocks, "seq", 0, 0, axis_index_groups=same_member, tiled=True)

    def rotate_both(block, turn_h, turn_m):
        if turn_h == turn_m == 0:
            return block
        return lax.ppermute(
            block,
            "seq",
            [
                (
                    h * spread + m,
                    (h + turn_h) % HEAD_GROUPS * spread + (m + turn_m) % spread,
                )
                for h in range(HEAD_GROUPS)
                for m in range(spread)
            ],
        )

    def rotate_heads(block, turn):
        return rotate_both(block, turn, 0)

    def rotate_members(block, turn):
        return rotate_both(block, 0, turn)

    def rotate_doc(block, turn):
        return lax.ppermute(block, "doc", [(d, (d + turn) % n_doc) for d in range(n_doc)])

    def in_order(pieces, own, axis):
        count = len(pieces)
        shape = pieces[0].shape
        whole = jnp.zeros(shape[:axis] + (count,) + shape[axis:], pieces[0].dtype)
        for turn, piece in enumerate(pieces):
            whole = lax.dynamic_update_index_in_dim(whole, piece, (own - turn) % count, axis)
        return whole

    def send_turns(blocks, axis, count, own, rotate):
        got = []
        for turn in range(count):
            block = lax.dynamic_index_in_dim(blocks, (own + turn) % count, axis, keepdims=False)
            got.append(rotate(block, turn) if turn else block)
        return got

    part = self_qkv.shape[0]
    width = 3 * GROUP_FEATS
    qkv_piece = jnp.concatenate(
        [
            lax.dynamic_slice_in_dim(
                self_qkv, block * D + head_group * GROUP_FEATS, GROUP_FEATS, 1
            )
            for block in range(3)
        ],
        axis=1,
    )
    small = jnp.concatenate([norm_gains, biases, ffn_in_bias.reshape(-1, part)], axis=0)
    small_rows = small.shape[0]
    first_width = width
    pad_rows = -(-small_rows * part // first_width)
    first_rows = -(-(part + pad_rows) // (8 * spread)) * 8 * spread
    pad_rows = first_rows - part
    small = jnp.pad(small.reshape(-1), (0, pad_rows * first_width - small_rows * part))
    first_piece = jnp.concatenate(
        [qkv_piece, small.reshape(pad_rows, width)], axis=0
    )
    first_piece = lax.dynamic_slice_in_dim(
        first_piece.astype(half), member * (first_rows // spread), first_rows // spread, 0
    )

    def join_members(mine):
        pieces = [mine] + [rotate_members(mine, turn) for turn in range(1, spread)]
        return in_order(pieces, member, 1).reshape(n_doc, -1, mine.shape[2])

    first_piece = jnp.broadcast_to(first_piece[None], (n_doc,) + first_piece.shape)
    first_gather = join_members(lax.all_to_all(first_piece, "doc", 0, 0, tiled=True))
    w_qkv_part = first_gather[:, :part].reshape(D, width)
    small = first_gather[:, part:].reshape(n_doc, -1)[:, : small_rows * part]
    small = small.reshape(n_doc, small_rows, part).astype(f32)
    gains_f = small[:, :3].transpose(1, 0, 2).reshape(3, D)
    biases_f = small[:, 3:13].transpose(1, 0, 2).reshape(10, D)
    b_ffn_in = small[:, 13:].reshape(1, -1)

    share = part // n_seq
    ff = ffn_in.shape[1]
    stack_n = ffn_out.shape[0] // part
    member_rows = part // spread

    def own_halves(*weights):
        piece = [
            lax.dynamic_slice_in_dim(weight, member * member_rows, member_rows, 0).astype(half)
            for weight in weights
        ]
        return jnp.concatenate(piece, axis=1)

    kv_halves = lax.all_gather(own_halves(cross_kv), "doc", axis=0)
    w_cross_kv = join_members(kv_halves).reshape(D, 2 * D)
    pair_halves = own_halves(self_out, cross_q)
    pair_halves = jnp.broadcast_to(pair_halves[None], (n_doc,) + pair_halves.shape)
    pair_halves, first_gather = lax.optimization_barrier((pair_halves, first_gather))
    pair_halves = lax.all_to_all(pair_halves, "doc", 0, 0, tiled=True)

    block_rows, block_cols = divmod(seq_index, 4)

    def column_block(weight, first):
        return lax.dynamic_slice(
            weight, (block_rows * member_rows, first), (member_rows, D)
        ).astype(half)

    def first_cols(*starts):
        return sum(jnp.where(block_cols == i, start, 0) for i, start in enumerate(starts) if start)

    left = jnp.where(
        block_cols == 0,
        column_block(cross_out, 0),
        jnp.where(
            block_cols == 3,
            column_block(self_qkv, D),
            column_block(ffn_in, first_cols(0, D, 3 * D, 0)),
        ),
    )
    right = jnp.where(
        block_cols < 2,
        column_block(ffn_in, first_cols(0, 2 * D, 0, 0)),
        column_block(self_qkv, first_cols(0, 0, 0, 2 * D)),
    )
    down = lax.dynamic_slice_in_dim(ffn_out, seq_index * member_rows, member_rows, 0).astype(half)
    w_blocks = lax.all_gather(
        jnp.concatenate([down, left, right], axis=1), ("doc", "seq"), axis=0, tiled=True
    )
    by_block = w_blocks.reshape(n_doc, spread, 4, member_rows, 3 * D)

    def columns(*blocks):
        found = [by_block[:, :, c, :, third * D : (third + 1) * D] for c, third in blocks]
        return jnp.concatenate(found, axis=3).reshape(D, -1)

    late_weights = [w_blocks]
    if member_rows % 16:
        late_weights = [
            columns((0, 1)),
            columns((0, 2), (1, 1), (1, 2), (2, 1)),
            w_blocks[:, :D],
        ]

    mem_low = memory[0]
    kv_bias = jnp.concatenate([jnp.zeros((D,), f32), biases_f[4]])
    mem_kv = (dot_tt(w_cross_kv, mem_low) + kv_bias[:, None]).astype(half)
    mem_kv = mem_kv.reshape(2, HEAD_GROUPS, GROUP_FEATS, mem_rows)
    pieces = send_turns(mem_kv, 1, HEAD_GROUPS, head_group, rotate_heads)
    pieces = pieces + [
        rotate_members(piece, turn) for turn in range(1, spread) for piece in pieces
    ]

    x_low = dec_input[0].reshape(rows_total, D)
    places = jnp.stack(
        [
            (head_group - turn_h) % HEAD_GROUPS * spread + (member - turn_m) % spread
            for turn_m in range(spread)
            for turn_h in range(HEAD_GROUPS)
        ]
    ).astype(jnp.int32)
    x_pieces = [rotate_heads(dec_input[0], turn) if turn else dec_input[0] for turn in range(HEAD_GROUPS)]
    for turn in range(1, spread):
        first_slot = (member + turn) % spread * member_slots
        blocks = [
            lax.dynamic_slice_in_dim(piece, first_slot, member_slots, 0)
            for piece in x_pieces[:HEAD_GROUPS]
        ]
        x_pieces.append(rotate_members(jnp.stack(blocks), turn))
    group_places = ((head_group - jnp.arange(HEAD_GROUPS)) % HEAD_GROUPS).astype(jnp.int32)
    zero_part = jnp.zeros((GROUP_FEATS,), f32)
    b_query = lax.dynamic_slice_in_dim(biases_f[0], head_group * GROUP_FEATS, GROUP_FEATS)
    b_value = lax.dynamic_slice_in_dim(biases_f[1], head_group * GROUP_FEATS, GROUP_FEATS)
    b_proj = jnp.concatenate([b_query, zero_part, b_value])[None]
    proj, self_mix, self_att_send, self_lse = self_forward(
        places, w_qkv_part, b_proj, x_pieces, n_seq, pieces[0]
    )

    def from_heads(blocks):
        feats = blocks.shape[2]
        got = blocks.reshape(HEAD_GROUPS, slots_n, feats // GROUP_FEATS, GROUP_FEATS, rows_dev)
        return got.transpose(2, 0, 3, 1, 4).reshape(HEAD_GROUPS * feats, rows_total)

    self_att_send, *pieces[1:HEAD_GROUPS] = lax.optimization_barrier(
        (self_att_send, *pieces[1:HEAD_GROUPS])
    )
    self_att = lax.all_to_all(self_att_send, "seq", 0, 0, tiled=True)
    pair_halves = lax.optimization_barrier((pair_halves, self_att_send))[0]
    w_pair = join_members(pair_halves).reshape(D, 2 * D)
    first_vectors = jnp.stack([biases_f[2], gains_f[0], biases_f[7], biases_f[3]])
    first_vectors = jnp.pad(first_vectors, ((0, 4), (0, 0)))
    norm_one, unit_one, scale_one, query_send = enter(
        self_att, x_low, first_vectors, w_pair, slots_n
    )

    lengths = doc_lengths[0]
    live_len = jnp.where(jnp.arange(slots_n) < doc_count[0], lengths, 0)
    key_high = jnp.minimum(jnp.cumsum(live_len), n_seq * mem_rows).astype(jnp.int32)
    key_low = jnp.concatenate([jnp.zeros((1,), jnp.int32), key_high[:-1]])
    query_part = swap_heads(query_send)
    cross_mix, cross_att_send, cross_lse = cross_forward(
        key_low, key_high, places, query_part, pieces
    )
    vectors = jnp.stack(
        [gains_f[1], biases_f[8], gains_f[2], biases_f[9], biases_f[5], biases_f[6]]
    )
    layer_out, grad_r2, grad_mix_send, late_packed, late_rows, grad_b_in = middle(
        n_doc,
        n_seq,
        swap_heads(cross_att_send),
        norm_one,
        out_grad[0].reshape(rows_total, D),
        jnp.pad(vectors, ((0, 2), (0, 0))),
        b_ffn_in,
        late_weights,
    )
    layer_out = layer_out.reshape(dec_input.shape)
    grad_g1, grad_c8, grad_g2, grad_c9, grad_b5, grad_b6 = late_rows[:6]

    def sum_over_seq(packed):
        packed = packed.reshape(D, packed.shape[2])
        return lax.psum_scatter(packed, "seq", scatter_dimension=0, tiled=True)

    def own_rows(packed):
        blocks = packed.reshape(n_doc, share, -1)
        pieces = send_turns(blocks, 0, n_doc, doc_index, rotate_doc)
        return sum(piece.astype(f32) for piece in pieces).astype(half)

    late_blocks = sum_over_seq(late_packed)
    grad_query_send, *grad_kv = cross_backward(
        key_low,
        key_high,
        places,
        query_part,
        swap_heads(grad_mix_send),
        cross_mix,
        cross_lse,
        pieces,
        late_packed,
    )
    grad_kv = [grad_kv[0]] + [
        rotate_members(grad_kv[turn], turn) for turn in range(1, spread)
    ]
    grad_kv_own = []
    for turn in range(HEAD_GROUPS):
        group = (head_group + turn) % HEAD_GROUPS
        total = sum(
            lax.dynamic_index_in_dim(piece, group, 0, keepdims=False).astype(f32)
            for piece in grad_kv
        ).astype(half)
        grad_kv_own.append(rotate_heads(total, turn) if turn else total)
    late_own = own_rows(lax.optimization_barrier((late_blocks, grad_kv_own[2]))[0])
    grad_query_send, *grad_kv_own = lax.optimization_barrier((grad_query_send, *grad_kv_own))
    mem_packed, grad_mem_kv, value_rows = memory_backward(
        n_doc, n_seq, group_places, mem_low, grad_kv_own
    )
    grad_r1, grad_att_send, packed = leave(
        n_doc,
        swap_heads(grad_query_send),
        self_att,
        grad_r2,
        norm_one,
        unit_one,
        scale_one,
        first_vectors,
        w_pair,
        mem_packed,
        late_rows,
        grad_b_in.reshape(n_doc, -1, part).transpose(1, 0, 2).reshape(-1, D),
        value_rows,
    )
    over_seq = sum_over_seq(packed)
    grad_self_part = lax.all_to_all(grad_att_send, "seq", 0, 0, tiled=True)
    grad_proj_send, grad_part, part_sums = self_backward(
        n_doc,
        places,
        proj,
        grad_self_part,
        self_mix,
        self_lse,
        x_pieces,
        packed,
        late_own,
    )
    grad_proj_send = lax.optimization_barrier((grad_proj_send, over_seq))[0]
    grad_proj_got = lax.all_to_all(grad_proj_send, "seq", 0, 0, tiled=True)

    bias_rows = jnp.zeros((2, D), f32)
    bias_rows = lax.dynamic_update_slice(
        bias_rows,
        jnp.stack([part_sums[0, :GROUP_FEATS], part_sums[0, 2 * GROUP_FEATS :]]),
        (0, head_group * GROUP_FEATS),
    )
    lanes = -(-part // small_cols) * small_cols
    bias_rows = jnp.pad(bias_rows.reshape(2, n_doc, part), ((0, 0), (0, 0), (0, lanes - part)))
    bias_rows = bias_rows.transpose(1, 0, 2).reshape(n_doc, -1, small_cols)
    bias_used = bias_rows.shape[1]
    bias_rows = jnp.pad(bias_rows, ((0, 0), (0, share - bias_used), (0, 0)))
    bias_rows = bias_rows.reshape(1, n_doc * share, small_cols).astype(half)
    bias_rows = jnp.pad(bias_rows, ((0, spread - 1), (0, 0), (0, 0)))
    grad_part = jnp.concatenate([grad_part, bias_rows], axis=2)
    grad_part = send_turns(grad_part, 0, spread, member, rotate_members)
    grad_part = sum(piece.astype(f32) for piece in grad_part).astype(half)

    grads = jnp.concatenate([over_seq, grad_part], axis=1)
    owned = jnp.concatenate([own_rows(grads), late_own], axis=1)
    param_grads = finish(n_seq, stack_n, lanes, lax.all_gather(owned, "seq", axis=0, tiled=True))
    (
        grad_w_qkv,
        grad_w_self_out,
        grad_w_cross_q,
        grad_w_cross_kv,
        grad_w_down,
        grad_w_in,
        grad_w_cross_out,
        grad_gains,
        grad_biases,
        grad_b_hidden,
    ) = param_grads
    grad_proj = from_heads(grad_proj_got)
    memory_grad = dot_tt(grad_mem_kv, w_cross_kv)[None]
    w_qkv = columns((2, 2), (3, 1), (3, 2))
    input_grad = (grad_r1 + dot_tt(grad_proj, w_qkv)).reshape(dec_input.shape)
    return (
        layer_out,
        input_grad,
        memory_grad,
        grad_w_qkv,
        grad_w_self_out,
        grad_w_cross_q,
        grad_w_cross_kv,
        grad_w_cross_out,
        grad_w_in,
        grad_b_hidden.reshape(-1),
        grad_w_down,
        grad_gains,
        grad_biases,
    )


def solution(mesh):
    placed = (
        P("doc", None, "seq", None),
        P("doc", "seq", None),
        P("doc", None),
        P("doc"),
        P("doc", None),
        P("doc", None),
        P("doc", None),
        P("doc", None),
        P("doc", None),
        P("doc", None),
        P("doc"),
        P("doc", None),
        P(None, "doc"),
        P(None, "doc"),
        P("doc", None, "seq", None),
    )
    return jax.shard_map(
        partial(body, mesh.shape["doc"], mesh.shape["seq"]),
        mesh=mesh,
        in_specs=placed,
        out_specs=(
            P("doc", None, "seq", None),
            P("doc", None, "seq", None),
            P("doc", "seq", None),
            P("doc", None),
            P("doc", None),
            P("doc", None),
            P("doc", None),
            P("doc", None),
            P("doc", None),
            P("doc"),
            P("doc", None),
            P(None, "doc"),
            P(None, "doc"),
        ),
        check_vma=False,
    )
```
